32 devices in a mesh: dp: 16 (over z, x, core), tensor: 2 (over y).
Axes of the slice: x: 2, y: 2, z: 4, core: 2. Of those that a mesh axis runs over, the one named last changes fastest.
Arguments:
- tokens: bfloat16 [16384, 1536], P('dp'), may hold values from -6 to 6
- cotangent: bfloat16 [16384, 1536], P('dp'), may hold values from -6 to 6
- segments: int32 [32, 256], P('dp'), may hold values from 0 to 3, never falling along the last dimension, each value on 1 to 128 neighbouring positions
- gain_attn: float32 [1536], replicated, may hold values from 0.5 to 1.5
- w_query: bfloat16 [1536, 1536], P(None, 'tensor'), may hold values from -0.15625 to 0.15625
- w_key: bfloat16 [1536, 1536], P(None, 'tensor'), may hold values from -0.15625 to 0.15625
- w_value: bfloat16 [1536, 1536], P(None, 'tensor'), may hold values from -0.15625 to 0.15625
- w_outgate: bfloat16 [1536, 1536], P(None, 'tensor'), may hold values from -0.15625 to 0.15625
- w_forget: bfloat16 [1536, 24], P(None, 'tensor'), may hold values from -0.15625 to 0.15625
- b_forget: float32 [24], P('tensor'), may hold values from 2 to 7
- w_out: bfloat16 [1536, 1536], P('tensor'), may hold values from -0.4375 to 0.4375
- gain_mlp: float32 [1536], replicated, may hold values from 0.5 to 1.5
- w_gate: bfloat16 [1536, 4096], P(None, 'tensor'), may hold values from -0.15625 to 0.15625
- w_up: bfloat16 [1536, 4096], P(None, 'tensor'), may hold values from -0.15625 to 0.15625
- w_down: bfloat16 [4096, 1536], P('tensor'), may hold values from -0.09375 to 0.09375
Outputs:
- result: bfloat16 [16384, 1536], P('dp')
- d_tokens: bfloat16 [16384, 1536], P('dp')
- g_gain_attn: float32 [1536], P('dp')
- g_query: float32 [1536, 1536], P('dp', 'tensor')
- g_key: float32 [1536, 1536], P('dp', 'tensor')
- g_value: float32 [1536, 1536], P('dp', 'tensor')
- g_outgate: float32 [1536, 1536], P('dp', 'tensor')
- g_forget: float32 [1536, 24], P('dp', 'tensor')
- g_forget_bias: float32 [24], P('tensor')
- g_out: float32 [1536, 1536], P('tensor', 'dp')
- g_gain_mlp: float32 [1536], P('dp')
- g_gate: float32 [1536, 4096], P('dp', 'tensor')
- g_up: float32 [1536, 4096], P('dp', 'tensor')
- g_down: float32 [4096, 1536], P('tensor', 'dp')
The draws below stay inside these ranges and needn't reach their ends.
Inputs may be any that keep to these rules, and one draw needn't show every extreme that they name: `segments`: in each row the continuation numbers never fall; each of the 4 continuations has 1 to 128 rows, and one has exactly 128.
All inputs are finite; a program needn't handle non-finite values.
Results may differ from the reference program's by a relative error of at most 0.025.
Values may be sent and summed in bfloat16 or wider, within the bound.
No kernel may reach another device: no remote copies, remote signals or barrier semaphores. Data moves between devices by JAX's collectives and lax.ppermute only.
A program may use at most 384 MiB of HBM per device.

```python
import math
import jax
import jax.numpy as jnp
import numpy as np
from jax import lax

D = 1536
HEADS = 24
HDIM = 64
FF = 4096
PROMPT = 256
CONT_TOK = 256
CONTS = 4
CONT_MOST = 128
GROUPS = 32
TOKENS = 16384
N_TENSOR = 2


def with_spikes(values, own_key, source, target, shards_of, factor):
    owner, partner = [(jnp.arange(values.shape[axis_at]) // (values.shape[axis_at] // shards_of)).reshape([-1 if axis == axis_at else 1 for axis in range(values.ndim)]) for axis_at in (source, target)]
    chosen = jax.random.permutation(own_key, shards_of)[partner]
    strong = (owner == chosen) | (owner == (partner + shards_of // 2) % shards_of)
    return jnp.where(strong, factor * values, values)


def level_of(rng, extent, pieces, smallest, high):
    def one(position, parts):
        draws = jax.random.uniform(jax.random.fold_in(jax.random.fold_in(rng, 6), position), (parts,), jnp.float32, smallest / len(pieces), high / len(pieces))
        return jnp.repeat(jnp.exp(draws), extent[position] // parts).reshape((-1,) + (1,) * (len(extent) - position - 1))

    level = one(*pieces[0])
    for cut in pieces[1:]:
        level = level * one(*cut)
    return level


def profile(amount, total, bound, lean):
    loads = [(1 << 20) // math.isqrt(standing ** lean) + 1 for standing in range(2, amount + 1)]
    surplus, holding = total - bound - (amount - 1), [1] * (amount - 1)
    while surplus > 0:
        free = [i for i in range(amount - 1) if holding[i] < bound]
        mass, left = sum([loads[i] for i in free]), surplus
        for i in free:
            addition = min(bound - holding[i], max(1, left * loads[i] // mass), surplus)
            holding[i] = holding[i] + addition
            surplus = surplus - addition
    return np.array([bound] + holding)


def ragged_sizes(key, number_of, total, most, skew):
    if number_of == 2:
        one = jax.random.randint(key, (), max(1, total - most), min(most, total - 1) + 1)
        return jnp.stack([one, total - one])
    tallies = jnp.asarray(profile(number_of, total, most, skew), jnp.int32)
    couples = (number_of - 1) // 2
    source_of, sink = tallies[1:1 + 2 * couples:2], tallies[2:2 + 2 * couples:2]
    room = jnp.minimum(source_of - 1, most - sink)
    passed = jax.random.randint(jax.random.fold_in(key, 1), (couples,), 0, 1 << 20) % (room + 1)
    tallies = tallies.at[1:1 + 2 * couples:2].set(source_of - passed).at[2:2 + 2 * couples:2].set(sink + passed)
    return tallies[jax.random.permutation(jax.random.fold_in(key, 2), number_of)]


def noise(stream_key, dims, width, reach, cuts=(), kind=jnp.bfloat16):
    level = level_of(stream_key, dims, cuts, -0.22, 0.18) if cuts else 1.0
    array = jax.random.normal(stream_key, dims, jnp.float32) * width * level
    return jnp.minimum(jnp.maximum(array, -reach), reach).astype(kind)


def bell_draw_with(rng, shape, width, most, split, heavy, dtype=jnp.bfloat16):
    values = width * jax.random.normal(rng, shape, jnp.float32)
    if split:
        values = values * level_of(rng, shape, split, -0.22, 0.18)
    return jnp.clip(with_spikes(values, jax.random.fold_in(rng, 3), *heavy), -most, most).astype(dtype)


def setup_inputs(seed: int = 0) -> dict:
    keys = jax.random.split(jax.random.key(seed), 16)
    tokens = bell_draw_with(keys[0], (TOKENS, D), 1.0, 6.0, ((0, 16),), (0, 1, 16, 2.0))
    cotangent = bell_draw_with(keys[1], (TOKENS, D), 1.0, 6.0, ((0, 16),), (0, 1, 16, 2.0))
    segments = jax.vmap(lambda own: jnp.searchsorted(jnp.cumsum(ragged_sizes(own, CONTS, CONT_TOK, CONT_MOST, 1)), jnp.arange(CONT_TOK), side="right"))(jax.random.split(keys[2], GROUPS)).reshape((GROUPS, CONT_TOK)).astype(jnp.int32)
    gain_attn = jnp.clip(1.0 + 0.1 * jax.random.normal(keys[3], (D,), jnp.float32), 0.5, 1.5)
    w_query = noise(keys[4], (D, HEADS * HDIM), D ** -0.5, 0.15625, ((1, 2),))
    w_key = noise(keys[5], (D, HEADS * HDIM), D ** -0.5, 0.15625, ((1, 2),))
    w_value = noise(keys[6], (D, HEADS * HDIM), D ** -0.5, 0.15625, ((1, 2),))
    w_outgate = noise(keys[7], (D, HEADS * HDIM), D ** -0.5, 0.15625, ((1, 2),))
    w_forget = noise(keys[8], (D, HEADS), D ** -0.5, 0.15625, ((1, 2),))
    b_forget = jnp.clip(2.0 + 5.0 * jax.random.uniform(keys[9], (HEADS,), jnp.float32) ** level_of(keys[9], (HEADS,), ((0, 2),), -0.2, 0.2), 2.0, 7.0)
    w_out = noise(keys[10], (HEADS * HDIM, D), (HEADS * HDIM // 8) ** -0.5, 0.4375, ((0, 2),))
    gain_mlp = jnp.clip(1.0 + 0.1 * jax.random.normal(keys[11], (D,), jnp.float32), 0.5, 1.5)
    w_gate = noise(keys[12], (D, FF), D ** -0.5, 0.15625, ((1, 2),))
    w_up = noise(keys[13], (D, FF), D ** -0.5, 0.15625, ((1, 2),))
    w_down = noise(keys[14], (FF, D), FF ** -0.5, 0.09375, ((0, 2),))
    return {"tokens": tokens, "cotangent": cotangent, "segments": segments, "gain_attn": gain_attn, "w_query": w_query, "w_key": w_key, "w_value": w_value, "w_outgate": w_outgate, "w_forget": w_forget, "b_forget": b_forget, "w_out": w_out, "gain_mlp": gain_mlp, "w_gate": w_gate, "w_up": w_up, "w_down": w_down}


EPS = 1e-06
highest = lax.Precision.HIGHEST

@jax.custom_vjp
def low(v):
    return lax.optimization_barrier(v.astype(jnp.bfloat16)).astype(jnp.float32)

@jax.custom_vjp
def low_back(v):
    return v

def low_keep(v):
    return (low(v), None)

def low_pass(kept, grad):
    return (grad,)

def back_keep(v):
    return (v, None)

def back_low(kept, grad):
    return (low(grad),)
low.defvjp(low_keep, low_pass)
low_back.defvjp(back_keep, back_low)

def dense(first_arg, second_arg):
    return jnp.dot(first_arg, second_arg, precision=highest)

def rms_norm(values, gain):
    return values * lax.rsqrt(lax.optimization_barrier(jnp.mean(values * values, axis=-1, keepdims=True)) + EPS) * gain

def path_mask(segment_row):
    ident = jnp.concatenate([jnp.full((PROMPT,), -1, jnp.int32), segment_row.astype(jnp.int32)])
    total_rows = ident.shape[0]
    row_ids = lax.broadcasted_iota(jnp.int32, (total_rows, total_rows), 0)
    col_ids = lax.broadcasted_iota(jnp.int32, (total_rows, total_rows), 1)
    same_path = jnp.logical_or(ident[None, :] == -1, ident[None, :] == ident[:, None])
    return jnp.logical_and(col_ids <= row_ids, same_path)

def group_attention(group_data):
    queries, keys_full, values_full, log_forget, segment_row = group_data
    allowed = path_mask(segment_row)
    decay_sum = jnp.dot(allowed.astype(jnp.float32), log_forget, precision=highest)
    raw = jnp.einsum('qhd,khd->hqk', queries, keys_full, precision=highest) * HDIM ** (-0.5)
    raw = raw + decay_sum.T[:, :, None] - decay_sum.T[:, None, :]
    scores = jnp.where(allowed[None], low_back(raw), -1e+30)
    probs_low = low(jax.nn.softmax(scores, axis=-1))
    return low_back(jnp.einsum('hqk,khd->qhd', probs_low, values_full, precision=highest))

def layer(x_full, gain_attn, w_query, w_key, w_value, w_outgate, w_forget, b_forget, w_out, gain_mlp, w_gate, w_up, w_down, segments):
    act_attn = low(rms_norm(x_full, gain_attn))
    head_cols = HEADS * HDIM // N_TENSOR
    head_share = HEADS // N_TENSOR
    ff_share = FF // N_TENSOR
    query_list, key_list, value_list, gate_list, forget_list = ([], [], [], [], [])
    for share_index in range(N_TENSOR):
        local_act = low_back(act_attn)
        col_slice = slice(share_index * head_cols, (share_index + 1) * head_cols)
        head_slice = slice(share_index * head_share, (share_index + 1) * head_share)
        query_list.append(low(low_back(dense(local_act, w_query[:, col_slice]))))
        key_list.append(low(low_back(dense(local_act, w_key[:, col_slice]))))
        value_list.append(low(low_back(dense(local_act, w_value[:, col_slice]))))
        gate_list.append(low_back(dense(local_act, w_outgate[:, col_slice])))
        forget_list.append(low_back(dense(local_act, w_forget[:, head_slice]) + b_forget[head_slice]))
    queries = jnp.concatenate(query_list, axis=1)
    keys_full = jnp.concatenate(key_list, axis=1)
    values_full = jnp.concatenate(value_list, axis=1)
    gate_pre = jnp.concatenate(gate_list, axis=1)
    log_forget = jax.nn.log_sigmoid(jnp.concatenate(forget_list, axis=1))
    row_count = x_full.shape[0]
    group_rows = PROMPT + CONT_TOK
    group_count = row_count // group_rows
    four_shape = (group_count, group_rows, HEADS, HDIM)
    attended = lax.map(jax.checkpoint(group_attention), (queries.reshape(four_shape), keys_full.reshape(four_shape), values_full.reshape(four_shape), log_forget.reshape(group_count, group_rows, HEADS), segments))
    attended = attended.reshape(row_count, HEADS * HDIM)
    gated = low(attended * jax.nn.sigmoid(gate_pre))
    attn_sum = jnp.zeros_like(x_full)
    for share_index in range(N_TENSOR):
        col_slice = slice(share_index * head_cols, (share_index + 1) * head_cols)
        attn_sum = attn_sum + low(dense(gated[:, col_slice], w_out[col_slice, :]))
    hidden = x_full + low_back(attn_sum)
    act_mlp = low(rms_norm(hidden, gain_mlp))
    mlp_sum = jnp.zeros_like(x_full)
    for share_index in range(N_TENSOR):
        local_act = low_back(act_mlp)
        ff_slice = slice(share_index * ff_share, (share_index + 1) * ff_share)
        gate_mlp = low_back(dense(local_act, w_gate[:, ff_slice]))
        up_mlp = low_back(dense(local_act, w_up[:, ff_slice]))
        inner_act = low(jax.nn.silu(gate_mlp) * up_mlp)
        mlp_sum = mlp_sum + low(dense(inner_act, w_down[ff_slice, :]))
    return hidden + low_back(mlp_sum)

def reference(tokens, cotangent, segments, gain_attn, w_query, w_key, w_value, w_outgate, w_forget, b_forget, w_out, gain_mlp, w_gate, w_up, w_down):
    floats = (tokens.astype(jnp.float32), gain_attn.astype(jnp.float32), w_query.astype(jnp.float32), w_key.astype(jnp.float32), w_value.astype(jnp.float32), w_outgate.astype(jnp.float32), w_forget.astype(jnp.float32), b_forget.astype(jnp.float32), w_out.astype(jnp.float32), gain_mlp.astype(jnp.float32), w_gate.astype(jnp.float32), w_up.astype(jnp.float32), w_down.astype(jnp.float32))

    def forward(x_full, gain_attn, w_query, w_key, w_value, w_outgate, w_forget, b_forget, w_out, gain_mlp, w_gate, w_up, w_down):
        return layer(x_full, gain_attn, w_query, w_key, w_value, w_outgate, w_forget, b_forget, w_out, gain_mlp, w_gate, w_up, w_down, segments)
    result, pullback = jax.vjp(forward, *floats)
    gradients = pullback(cotangent.astype(jnp.float32))
    return (result.astype(jnp.bfloat16), gradients[0].astype(jnp.bfloat16), gradients[1], gradients[2], gradients[3], gradients[4], gradients[5], gradients[6], gradients[7], gradients[8], gradients[9], gradients[10], gradients[11], gradients[12])
```

```python
import functools

import jax
import jax.numpy as jnp
from jax import lax
from jax.experimental import pallas as pl
from jax.experimental.pallas import tpu as pltpu
from jax.sharding import PartitionSpec as P

PROMPT = 256
CONT_TOK = 256
GROUP = PROMPT + CONT_TOK
LANES = 128
HEAD = 64
BLOCK_HEADS = 4
BLOCK_COLS = HEAD * BLOCK_HEADS
EPS = 1e-06
NEG = -1e30
BF = jnp.bfloat16
F32 = jnp.float32


def dot_dims(first_arg, second_arg, first_dim, second_dim):
    return lax.dot_general(
        first_arg,
        second_arg,
        (((first_dim,), (second_dim,)), ((), ())),
        preferred_element_type=F32,
    )


def dot_nn(first_arg, second_arg):
    return dot_dims(first_arg, second_arg, 1, 0)


def dot_nt(first_arg, second_arg):
    return dot_dims(first_arg, second_arg, 1, 1)


def dot_tn(first_arg, second_arg):
    return dot_dims(first_arg, second_arg, 0, 0)


def sigmoid(values):
    return 1.0 / (1.0 + jnp.exp(-values))


def split_three(values):
    high = values.astype(BF).astype(F32)
    rest = values - high
    middle = rest.astype(BF).astype(F32)
    return high, middle, rest - middle


def visible_pairs(ident_row_ref, ident_col_ref):
    row_ids = lax.broadcasted_iota(jnp.int32, (GROUP, GROUP), 0)
    col_ids = lax.broadcasted_iota(jnp.int32, (GROUP, GROUP), 1)
    ident_row = ident_row_ref[...]
    same = jnp.logical_or(ident_row == -1, ident_row == ident_col_ref[...])
    return jnp.logical_and(col_ids <= row_ids, same)


def lane_ids():
    return lax.broadcasted_iota(jnp.int32, (GROUP, LANES), 1)


def place_extras(lanes, own, main, base, extras, constant_at):
    value = jnp.where(
        jnp.logical_and(lanes >= base + constant_at, lanes < base + constant_at + 3), 1.0, 0.0
    )
    offset = 0 if constant_at else 3
    for position, column in enumerate(extras):
        value = jnp.where(lanes == base + offset + position, column, value)
    return jnp.where(own, main, value).astype(BF)


def column_of(lanes, values, index):
    return jnp.sum(jnp.where(lanes == index, values, 0.0), axis=1, keepdims=True)


def attn_fwd_kernel(
    x_ref,
    ident_row_ref,
    ident_col_ref,
    gain_ref,
    wq_ref,
    wk_ref,
    wv_ref,
    wg_ref,
    wf_ref,
    bias_ref,
    wo_ref,
    part_ref,
    act_ref,
    q_ref,
    k_ref,
    v_ref,
    sig_ref,
    att_ref,
    gated_ref,
    lse_ref,
    decay_ref,
    forget_ref,
    acc_ref,
    mask_ref,
):
    step = pl.program_id(0)
    lanes = lane_ids()

    @pl.when(step == 0)
    def _():
        x = x_ref[...].astype(F32)
        scale = lax.rsqrt(jnp.mean(x * x, axis=1, keepdims=True) + EPS)
        act = (x * scale * gain_ref[...]).astype(BF)
        act_ref[...] = act
        forget_pre = dot_nn(act, wf_ref[...]) + bias_ref[...]
        forget_ref[...] = forget_pre
        log_forget = jnp.minimum(forget_pre, 0.0) - jnp.log1p(jnp.exp(-jnp.abs(forget_pre)))
        allowed = visible_pairs(ident_row_ref, ident_col_ref)
        mask_ref[...] = jnp.where(allowed, 0.0, NEG)
        ancestry = jnp.where(allowed, 1.0, 0.0).astype(BF)
        high, middle, low = split_three(log_forget)
        decay_ref[...] = (
            dot_nn(ancestry, high.astype(BF))
            + dot_nn(ancestry, middle.astype(BF))
            + dot_nn(ancestry, low.astype(BF))
        )
        acc_ref[...] = jnp.zeros_like(acc_ref)
        lse_ref[...] = jnp.zeros_like(lse_ref)

    act = act_ref[...]
    queries = dot_nn(act, wq_ref[...]).astype(BF)
    keys_low = dot_nn(act, wk_ref[...]).astype(BF)
    values_low = dot_nn(act, wv_ref[...]).astype(BF)
    gate = sigmoid(dot_nn(act, wg_ref[...]))
    q_ref[...] = queries
    k_ref[...] = keys_low
    v_ref[...] = values_low
    sig_ref[...] = gate
    attended_pairs = []
    for pair in range(BLOCK_HEADS // 2):
        cols = slice(pair * LANES, (pair + 1) * LANES)
        q_pair = queries[:, cols].astype(F32) * (HEAD**-0.5)
        k_pair = keys_low[:, cols].astype(F32)
        v_pair = values_low[:, cols]
        outs = []
        for half in range(2):
            own = (lanes < HEAD) if half == 0 else (lanes >= HEAD)
            base = HEAD if half == 0 else 0
            head = step * BLOCK_HEADS + pair * 2 + half
            decay = column_of(lanes, decay_ref[...], head)
            parts = split_three(decay)
            q_ext = place_extras(lanes, own, q_pair, base, parts, 3)
            k_ext = place_extras(lanes, own, k_pair, base, [-value for value in parts], 0)
            scores_p = dot_nt(q_ext[:PROMPT], k_ext[:PROMPT]) + mask_ref[:PROMPT, :PROMPT]
            scores_a = dot_nt(q_ext[PROMPT:], k_ext[:PROMPT])
            scores_b = dot_nt(q_ext[PROMPT:], k_ext[PROMPT:]) + mask_ref[PROMPT:, PROMPT:]
            max_p = jnp.max(scores_p, axis=1, keepdims=True)
            exp_p = jnp.exp(scores_p - max_p)
            sum_p = jnp.sum(exp_p, axis=1, keepdims=True)
            out_p = dot_nn(exp_p.astype(BF), v_pair[:PROMPT]) * (1.0 / sum_p)
            max_c = jnp.maximum(
                jnp.max(scores_a, axis=1, keepdims=True), jnp.max(scores_b, axis=1, keepdims=True)
            )
            exp_a = jnp.exp(scores_a - max_c)
            exp_b = jnp.exp(scores_b - max_c)
            sum_c = jnp.sum(exp_a, axis=1, keepdims=True) + jnp.sum(exp_b, axis=1, keepdims=True)
            out_c = dot_nn(exp_a.astype(BF), v_pair[:PROMPT]) + dot_nn(
                exp_b.astype(BF), v_pair[PROMPT:]
            )
            out_c = out_c * (1.0 / sum_c)
            outs.append(jnp.concatenate([out_p, out_c], axis=0))
            lse = jnp.concatenate([max_p + jnp.log(sum_p), max_c + jnp.log(sum_c)], axis=0)
            lse_ref[...] = jnp.where(lanes == head, lse, lse_ref[...])
        attended_pairs.append(jnp.where(lanes < HEAD, outs[0], outs[1]))
    attended = jnp.concatenate(attended_pairs, axis=1)
    att_ref[...] = attended
    gated = (attended * gate).astype(BF)
    gated_ref[...] = gated
    acc_ref[...] += dot_nn(gated, wo_ref[...])

    @pl.when(step == pl.num_programs(0) - 1)
    def _():
        part_ref[...] = acc_ref[...].astype(BF)


def mlp_kernel(
    x_ref,
    own_ref,
    other_ref,
    d_ref,
    gain_ref,
    wg_ref,
    wu_ref,
    wd_ref,
    hidden_ref,
    act_ref,
    inner_ref,
    dgate_ref,
    dup_ref,
    mlp_ref,
    dact_ref,
    acc_mlp_ref,
    acc_dact_ref,
):
    step = pl.program_id(0)

    @pl.when(step == 0)
    def _():
        hidden = x_ref[...].astype(F32) + (own_ref[...].astype(F32) + other_ref[...].astype(F32))
        hidden_ref[...] = hidden
        scale = lax.rsqrt(jnp.mean(hidden * hidden, axis=1, keepdims=True) + EPS)
        act_ref[...] = (hidden * scale * gain_ref[...]).astype(BF)
        acc_mlp_ref[...] = jnp.zeros_like(acc_mlp_ref)
        acc_dact_ref[...] = jnp.zeros_like(acc_dact_ref)

    act = act_ref[...]
    gate = dot_nn(act, wg_ref[...])
    up = dot_nn(act, wu_ref[...])
    d_inner = dot_nt(d_ref[...], wd_ref[...])
    gate_sigmoid = sigmoid(gate)
    silu_value = gate * gate_sigmoid
    inner = (silu_value * up).astype(BF)
    d_gate = (d_inner * up * gate_sigmoid * (1.0 + gate * (1.0 - gate_sigmoid))).astype(BF)
    d_up = (d_inner * silu_value).astype(BF)
    inner_ref[...] = inner
    dgate_ref[...] = d_gate
    dup_ref[...] = d_up
    acc_dact_ref[...] += dot_nt(d_gate, wg_ref[...]) + dot_nt(d_up, wu_ref[...])
    acc_mlp_ref[...] += dot_nn(inner, wd_ref[...])

    @pl.when(step == pl.num_programs(0) - 1)
    def _():
        dact_ref[...] = acc_dact_ref[...].astype(BF)
        mlp_ref[...] = acc_mlp_ref[...].astype(BF)


def attn_bwd_kernel(
    x_ref,
    d_ref,
    hidden_ref,
    own_ref,
    other_ref,
    gain_ref,
    ident_row_ref,
    ident_col_ref,
    q_ref,
    k_ref,
    v_ref,
    sig_ref,
    att_ref,
    lse_ref,
    decay_ref,
    forget_ref,
    wo_ref,
    wq_ref,
    wk_ref,
    wv_ref,
    wg_ref,
    wf_ref,
    dhidden_ref,
    dattn_ref,
    gains_ref,
    dq_ref,
    dk_ref,
    dv_ref,
    dgp_ref,
    dfp_ref,
    gbias_ref,
    dact_ref,
    acc_ref,
    mask_ref,
    ddecay_ref,
):
    step = pl.program_id(0)
    lanes = lane_ids()

    @pl.when(step == 0)
    def _():
        hidden = hidden_ref[...]
        d_act = own_ref[...].astype(F32) + other_ref[...].astype(F32)
        scale = lax.rsqrt(jnp.mean(hidden * hidden, axis=1, keepdims=True) + EPS)
        weighted = d_act * gain_ref[...]
        inner_mean = jnp.mean(weighted * hidden, axis=1, keepdims=True)
        d_hidden = d_ref[...].astype(F32) + (
            scale * weighted - hidden * (scale * scale * scale) * inner_mean
        )
        dhidden_ref[...] = d_hidden
        dattn_ref[...] = d_hidden.astype(BF)
        gains_ref[0:1, :] = jnp.sum(d_act * hidden * scale, axis=0, keepdims=True)
        allowed = visible_pairs(ident_row_ref, ident_col_ref)
        mask_ref[...] = jnp.where(allowed, 0.0, NEG)
        acc_ref[...] = jnp.zeros_like(acc_ref)
        ddecay_ref[...] = jnp.zeros_like(ddecay_ref)

    d_gated = dot_nt(dattn_ref[...], wo_ref[...])
    gate = sig_ref[...]
    attended = att_ref[...]
    d_gate_pre = (d_gated * attended * gate * (1.0 - gate)).astype(BF)
    dgp_ref[...] = d_gate_pre
    d_attended = (d_gated * gate).astype(BF)
    grads_q, grads_k, grads_v = [], [], []
    for pair in range(BLOCK_HEADS // 2):
        cols = slice(pair * LANES, (pair + 1) * LANES)
        q_low = q_ref[:, cols]
        k_low = k_ref[:, cols]
        v_low = v_ref[:, cols]
        q_pair = q_low.astype(F32)
        k_pair = k_low.astype(F32)
        v_pair = v_low.astype(F32)
        do_low = d_attended[:, cols]
        do_pair = do_low.astype(F32)
        row_products = do_pair * attended[:, cols]
        dqs, dks, dvs = [], [], []
        for half in range(2):
            own = (lanes < HEAD) if half == 0 else (lanes >= HEAD)
            base = HEAD if half == 0 else 0
            head = step * BLOCK_HEADS + pair * 2 + half
            decay = column_of(lanes, decay_ref[...], head)
            lse = column_of(lanes, lse_ref[...], head)
            row_inner = jnp.sum(jnp.where(own, row_products, 0.0), axis=1, keepdims=True)
            q_ext = place_extras(
                lanes, own, q_pair * (HEAD**-0.5), base, split_three(decay - lse), 3
            )
            k_ext = place_extras(
                lanes, own, k_pair, base, [-value for value in split_three(decay)], 0
            )
            do_ext = place_extras(lanes, own, do_pair, base, split_three(-row_inner), 3)
            v_ext = place_extras(lanes, own, v_pair, base, [], 0)
            k_one = jnp.where(own, k_pair, 1.0).astype(BF)
            q_one = jnp.where(own, q_pair, 1.0).astype(BF)
            probs_p = jnp.exp(
                dot_nt(q_ext[:PROMPT], k_ext[:PROMPT]) + mask_ref[:PROMPT, :PROMPT]
            )
            probs_a = jnp.exp(dot_nt(q_ext[PROMPT:], k_ext[:PROMPT]))
            probs_b = jnp.exp(
                dot_nt(q_ext[PROMPT:], k_ext[PROMPT:]) + mask_ref[PROMPT:, PROMPT:]
            )
            ds_p = (probs_p * dot_nt(do_ext[:PROMPT], v_ext[:PROMPT])).astype(BF)
            ds_a = (probs_a * dot_nt(do_ext[PROMPT:], v_ext[:PROMPT])).astype(BF)
            ds_b = (probs_b * dot_nt(do_ext[PROMPT:], v_ext[PROMPT:])).astype(BF)
            dv_top = dot_tn(probs_p.astype(BF), do_low[:PROMPT]) + dot_tn(
                probs_a.astype(BF), do_low[PROMPT:]
            )
            dv_low = dot_tn(probs_b.astype(BF), do_low[PROMPT:])
            dk_top = dot_tn(ds_p, q_one[:PROMPT]) + dot_tn(ds_a, q_one[PROMPT:])
            dk_low = dot_tn(ds_b, q_one[PROMPT:])
            dq_top = dot_nn(ds_p, k_one[:PROMPT])
            dq_low = dot_nn(ds_a, k_one[:PROMPT]) + dot_nn(ds_b, k_one[PROMPT:])
            dvs.append(jnp.concatenate([dv_top, dv_low], axis=0))
            dks.append(jnp.concatenate([dk_top, dk_low], axis=0))
            dqs.append(jnp.concatenate([dq_top, dq_low], axis=0))
            sums = (dqs[-1] - dks[-1])[:, base : base + 1]
            ddecay_ref[...] = jnp.where(lanes == head, sums, ddecay_ref[...])
        grads_q.append(jnp.where(lanes < HEAD, dqs[0], dqs[1]) * (HEAD**-0.5))
        grads_k.append(jnp.where(lanes < HEAD, dks[0], dks[1]) * (HEAD**-0.5))
        grads_v.append(jnp.where(lanes < HEAD, dvs[0], dvs[1]))
    d_queries = jnp.concatenate(grads_q, axis=1).astype(BF)
    d_keys = jnp.concatenate(grads_k, axis=1).astype(BF)
    d_values = jnp.concatenate(grads_v, axis=1).astype(BF)
    dq_ref[...] = d_queries
    dk_ref[...] = d_keys
    dv_ref[...] = d_values
    acc_ref[...] += (
        dot_nt(d_queries, wq_ref[...])
        + dot_nt(d_keys, wk_ref[...])
        + dot_nt(d_values, wv_ref[...])
        + dot_nt(d_gate_pre, wg_ref[...])
    )

    @pl.when(step == pl.num_programs(0) - 1)
    def _():
        ancestry = jnp.where(visible_pairs(ident_row_ref, ident_col_ref), 1.0, 0.0).astype(BF)
        high, middle, low = split_three(ddecay_ref[...])
        d_log_forget = (
            dot_tn(ancestry, high.astype(BF))
            + dot_tn(ancestry, middle.astype(BF))
            + dot_tn(ancestry, low.astype(BF))
        )
        d_forget = (d_log_forget * sigmoid(-forget_ref[...])).astype(BF)
        dfp_ref[...] = d_forget
        gbias_ref[0:1, :] = jnp.sum(d_forget.astype(F32), axis=0, keepdims=True)
        d_act = (acc_ref[...] + dot_nt(d_forget, wf_ref[...])).astype(BF)
        dact_ref[...] = d_act
        x = x_ref[...].astype(F32)
        scale = lax.rsqrt(jnp.mean(x * x, axis=1, keepdims=True) + EPS)
        gains_ref[1:2, :] = jnp.sum(d_act.astype(F32) * x * scale, axis=0, keepdims=True)


def whole(shape):
    return pl.BlockSpec(shape, lambda step: (0,) * len(shape))


def rows_of(group, width):
    return pl.BlockSpec((GROUP, width), lambda step: (group, 0))


def cols_block(rows, width):
    return pl.BlockSpec((rows, width), lambda step: (0, step))


def rows_block(width, cols):
    return pl.BlockSpec((width, cols), lambda step: (step, 0))


def shape_of(rows, cols, dtype):
    return jax.ShapeDtypeStruct((rows, cols), dtype)


def cost_of(length_us):
    return pl.CostEstimate(
        flops=int(length_us * 500_000_000), bytes_accessed=100_000, transcendentals=0
    )


def params_for():
    return pltpu.CompilerParams(
        vmem_limit_bytes=60 * 1024 * 1024, dimension_semantics=("arbitrary",)
    )


def attn_forward(group, tokens, ident, gain, weights, forget_weight, forget_bias, w_out):
    width = tokens.shape[1]
    head_cols = w_out.shape[0]
    return pl.pallas_call(
        attn_fwd_kernel,
        grid=(head_cols // BLOCK_COLS,),
        in_specs=[
            rows_of(group, width),
            whole((1, GROUP)),
            whole((GROUP, 1)),
            whole((1, width)),
            cols_block(width, BLOCK_COLS),
            cols_block(width, BLOCK_COLS),
            cols_block(width, BLOCK_COLS),
            cols_block(width, BLOCK_COLS),
            whole((width, LANES)),
            whole((1, LANES)),
            rows_block(BLOCK_COLS, width),
        ],
        out_specs=[
            whole((GROUP, width)),
            whole((GROUP, width)),
            cols_block(GROUP, BLOCK_COLS),
            cols_block(GROUP, BLOCK_COLS),
            cols_block(GROUP, BLOCK_COLS),
            cols_block(GROUP, BLOCK_COLS),
            cols_block(GROUP, BLOCK_COLS),
            cols_block(GROUP, BLOCK_COLS),
            whole((GROUP, LANES)),
            whole((GROUP, LANES)),
            whole((GROUP, LANES)),
        ],
        out_shape=[
            shape_of(GROUP, width, BF),
            shape_of(GROUP, width, BF),
            shape_of(GROUP, head_cols, BF),
            shape_of(GROUP, head_cols, BF),
            shape_of(GROUP, head_cols, BF),
            shape_of(GROUP, head_cols, F32),
            shape_of(GROUP, head_cols, F32),
            shape_of(GROUP, head_cols, BF),
            shape_of(GROUP, LANES, F32),
            shape_of(GROUP, LANES, F32),
            shape_of(GROUP, LANES, F32),
        ],
        scratch_shapes=[pltpu.VMEM((GROUP, width), F32), pltpu.VMEM((GROUP, GROUP), F32)],
        compiler_params=params_for(),
        cost_estimate=cost_of(21),
        name="attn_fwd",
    )(tokens, ident[0], ident[1], gain, *weights, forget_weight, forget_bias, w_out)


def mlp_both(group, tokens, own, other, cotangent, gain, w_gate, w_up, w_down):
    width = tokens.shape[1]
    hidden_units = w_down.shape[0]
    block = 512
    return pl.pallas_call(
        mlp_kernel,
        grid=(hidden_units // block,),
        in_specs=[
            rows_of(group, width),
            whole((GROUP, width)),
            whole((GROUP, width)),
            rows_of(group, width),
            whole((1, width)),
            cols_block(width, block),
            cols_block(width, block),
            rows_block(block, width),
        ],
        out_specs=[
            whole((GROUP, width)),
            whole((GROUP, width)),
            cols_block(GROUP, block),
            cols_block(GROUP, block),
            cols_block(GROUP, block),
            whole((GROUP, width)),
            whole((GROUP, width)),
        ],
        out_shape=[
            shape_of(GROUP, width, F32),
            shape_of(GROUP, width, BF),
            shape_of(GROUP, hidden_units, BF),
            shape_of(GROUP, hidden_units, BF),
            shape_of(GROUP, hidden_units, BF),
            shape_of(GROUP, width, BF),
            shape_of(GROUP, width, BF),
        ],
        scratch_shapes=[pltpu.VMEM((GROUP, width), F32), pltpu.VMEM((GROUP, width), F32)],
        compiler_params=params_for(),
        cost_estimate=cost_of(32),
        name="mlp_both",
    )(tokens, own, other, cotangent, gain, w_gate, w_up, w_down)


def attn_backward(
    group, tokens, cotangent, hidden, own, other, gain, ident, saved, w_out, weights, forget_weight
):
    width = tokens.shape[1]
    head_cols = w_out.shape[0]
    queries, keys_low, values_low, gate, attended, lse, decay, forget_pre = saved
    return pl.pallas_call(
        attn_bwd_kernel,
        grid=(head_cols // BLOCK_COLS,),
        in_specs=[
            rows_of(group, width),
            rows_of(group, width),
            whole((GROUP, width)),
            whole((GROUP, width)),
            whole((GROUP, width)),
            whole((1, width)),
            whole((1, GROUP)),
            whole((GROUP, 1)),
            cols_block(GROUP, BLOCK_COLS),
            cols_block(GROUP, BLOCK_COLS),
            cols_block(GROUP, BLOCK_COLS),
            cols_block(GROUP, BLOCK_COLS),
            cols_block(GROUP, BLOCK_COLS),
            whole((GROUP, LANES)),
            whole((GROUP, LANES)),
            whole((GROUP, LANES)),
            rows_block(BLOCK_COLS, width),
            cols_block(width, BLOCK_COLS),
            cols_block(width, BLOCK_COLS),
            cols_block(width, BLOCK_COLS),
            cols_block(width, BLOCK_COLS),
            whole((width, LANES)),
        ],
        out_specs=[
            whole((GROUP, width)),
            whole((GROUP, width)),
            whole((8, width)),
            cols_block(GROUP, BLOCK_COLS),
            cols_block(GROUP, BLOCK_COLS),
            cols_block(GROUP, BLOCK_COLS),
            cols_block(GROUP, BLOCK_COLS),
            whole((GROUP, LANES)),
            whole((8, LANES)),
            whole((GROUP, width)),
        ],
        out_shape=[
            shape_of(GROUP, width, F32),
            shape_of(GROUP, width, BF),
            shape_of(8, width, F32),
            shape_of(GROUP, head_cols, BF),
            shape_of(GROUP, head_cols, BF),
            shape_of(GROUP, head_cols, BF),
            shape_of(GROUP, head_cols, BF),
            shape_of(GROUP, LANES, BF),
            shape_of(8, LANES, F32),
            shape_of(GROUP, width, BF),
        ],
        scratch_shapes=[
            pltpu.VMEM((GROUP, width), F32),
            pltpu.VMEM((GROUP, GROUP), F32),
            pltpu.VMEM((GROUP, LANES), F32),
        ],
        compiler_params=params_for(),
        cost_estimate=cost_of(32),
        name="attn_bwd",
    )(
        tokens,
        cotangent,
        hidden,
        own,
        other,
        gain,
        ident[0],
        ident[1],
        queries,
        keys_low,
        values_low,
        gate,
        attended,
        lse,
        decay,
        forget_pre,
        w_out,
        *weights,
        forget_weight,
    )


def grad_kernel(place_ref, extra_ref, *refs, groups, plan, order, flip):
    inputs = refs[:-3]
    keep_ref, send_ref, total_ref = refs[-3:]
    step = pl.program_id(0)
    blocks, block_rows = total_ref.shape[0], total_ref.shape[1]
    place = place_ref[0]

    def emit(left_refs, right_refs, with_extra):
        total = dot_tn(left_refs[0][...], right_refs[0][...])
        for left_ref, right_ref in zip(left_refs[1:], right_refs[1:]):
            total = total + dot_tn(left_ref[...], right_ref[...])
        if with_extra:
            total = total + extra_ref[...]
        block = total.shape[1]
        for index in range(blocks):
            total_ref[index, :, :block] = total[index * block_rows : (index + 1) * block_rows]
        for index, slot in enumerate(order):
            kept = total_ref[jnp.bitwise_xor(place, slot), :, :block]
            sent = total_ref[jnp.bitwise_xor(place, slot ^ flip), :, :block]
            keep_ref[index, :, :block] = kept.astype(BF)
            send_ref[index, :, :block] = sent.astype(BF)

    for left_at, right_at, first, count, with_extra in plan:
        pl.when(jnp.logical_and(step >= first, step < first + count))(
            functools.partial(
                emit,
                inputs[left_at : left_at + groups],
                inputs[right_at : right_at + groups],
                with_extra,
            )
        )


def half_order(bits):
    slots = [0]
    for bit in reversed(bits[1:]):
        slots = slots + [slot ^ bit for slot in slots]
    return slots


def weight_grad(products, place, devices, bits, block, extra=None):
    width = products[0][0][0].shape[1]
    groups = len(products[0][0])
    rows = width // devices
    half = devices // 2
    arrays, specs, plan, seen = [], [], [], {}
    first = 0

    def add(items, make_spec):
        at = len(arrays)
        arrays.extend(items)
        specs.extend([make_spec()] * groups)
        return at

    for index, (lefts, rights) in enumerate(products):
        if id(lefts[0]) not in seen:
            seen[id(lefts[0])] = add(lefts, lambda: rows_of(0, width))
        narrow = extra is not None and index == len(products) - 1
        cols = rights[0].shape[1]
        count = 1 if narrow else cols // block
        at = add(
            rights,
            lambda: pl.BlockSpec(
                (GROUP, cols if narrow else block),
                lambda step, first=first, count=count: (
                    0,
                    jnp.minimum(jnp.maximum(step - first, 0), count - 1),
                ),
            ),
        )
        plan.append((seen[id(lefts[0])], at, first, count, narrow))
        first += count
    if extra is None:
        extra = jnp.zeros((8, LANES), F32)
    return pl.pallas_call(
        functools.partial(
            grad_kernel, groups=groups, plan=plan, order=half_order(bits), flip=bits[0]
        ),
        grid=(first,),
        in_specs=[pl.BlockSpec(memory_space=pltpu.SMEM), whole(extra.shape)] + specs,
        out_specs=[pl.BlockSpec((half, rows, block), lambda step: (0, 0, step))] * 2,
        out_shape=[jax.ShapeDtypeStruct((half, rows, first * block), BF)] * 2,
        scratch_shapes=[pltpu.VMEM((devices, rows, block), F32)],
        compiler_params=params_for(),
        cost_estimate=cost_of(5.7 * first * block / 1024),
        name="weight_grad",
    )(place, extra, *arrays)


class SharedSum:
    def __init__(self, keep, send, bits, devices):
        self.parts, self.send, self.bits, self.devices = [keep], send, bits, devices
        self.stage = 0

    def exchange(self):
        bit = self.bits[self.stage]
        got = lax.ppermute(
            self.send, "dp", [(index, index ^ bit) for index in range(self.devices)]
        )
        self.parts.append(got)
        self.stage += 1
        remaining = got.shape[0]
        half = remaining // 2
        if self.stage < len(self.bits):
            pieces = [part[half:remaining].astype(F32) for part in self.parts]
            self.send = functools.reduce(jnp.add, pieces).astype(BF)
            self.parts = [part[:half] for part in self.parts]
        return self

    def keep(self):
        return self.parts[0]

    def result(self):
        while self.stage < len(self.bits):
            self.exchange()
        return functools.reduce(jnp.add, [part[0].astype(F32) for part in self.parts])


def after(values, *earlier):
    return lax.optimization_barrier((values, earlier))[0]


def local(
    tokens,
    cotangent,
    segments,
    gain_attn,
    w_query,
    w_key,
    w_value,
    w_outgate,
    w_forget,
    b_forget,
    w_out,
    gain_mlp,
    w_gate,
    w_up,
    w_down,
):
    devices = lax.axis_size("dp")
    place_index = lax.axis_index("dp")
    width = tokens.shape[1]
    groups = tokens.shape[0] // GROUP
    heads = w_forget.shape[1]
    rows = width // devices
    butterfly = devices & (devices - 1) == 0 and rows % 16 == 0
    place = jnp.reshape(place_index, (1,)).astype(jnp.int32)
    bits = [1 << level for level in range(devices.bit_length() - 1)]

    def swap(values):
        return lax.ppermute(values, "tensor", [(0, 1), (1, 0)])

    gain_attn_row = gain_attn[None, :]
    gain_mlp_row = gain_mlp[None, :]
    forget_weight = jnp.pad(w_forget, ((0, 0), (0, LANES - heads)))
    forget_bias = jnp.pad(b_forget, (0, LANES - heads))[None, :]
    weights = (w_query, w_key, w_value, w_outgate)
    idents = []
    for group in range(groups):
        row = jnp.concatenate([jnp.full((PROMPT,), -1, jnp.int32), segments[group]])
        idents.append((row[None, :], row[:, None]))

    def pick(source, index):
        return [source[group][index] for group in range(groups)]

    def sharing(products, block, extra=None):
        return SharedSum(
            *weight_grad(products, place, devices, bits, block, extra), bits, devices
        )

    def scattered(lefts, rights):
        total = functools.reduce(
            jnp.add, [dot_tn(left, right) for left, right in zip(lefts, rights)]
        )
        return lax.psum_scatter(total, "dp", scatter_dimension=0, tiled=True)

    def forward_of(group, rows_in):
        return attn_forward(
            group,
            rows_in,
            idents[group],
            gain_attn_row,
            weights,
            forget_weight,
            forget_bias,
            w_out,
        )

    def middle_of(group, own):
        return mlp_both(
            group,
            tokens,
            own,
            attn_other[group],
            cotangent,
            gain_mlp_row,
            w_gate,
            w_up,
            w_down,
        )

    def backward_of(group, own):
        (_, _, queries, keys_low, values_low, gate, attended, _, lse, decay, forget_pre) = forward[
            group
        ]
        return attn_backward(
            group,
            tokens,
            cotangent,
            middle[group][0],
            own,
            dact_other[group],
            gain_mlp_row,
            idents[group],
            (queries, keys_low, values_low, gate, attended, lse, decay, forget_pre),
            w_out,
            weights,
            forget_weight,
        )

    forward = []
    for group in range(groups):
        earlier = () if group == 0 else (forward[-1][0],)
        forward.append(forward_of(group, after(tokens, *earlier)))
    attn_other = [swap(forward[group][0]) for group in range(groups)]
    middle = []
    for group in range(groups):
        earlier = () if group == 0 else (middle[-1][6],)
        middle.append(middle_of(group, after(forward[group][0], *earlier)))
    dact_other = []
    for group in range(groups):
        earlier = () if group == 0 else (dact_other[-1],)
        dact_other.append(swap(after(middle[group][6], *earlier)))
    mlp_other = []
    for group in range(groups):
        earlier = (dact_other[-1],) if group == 0 else (mlp_other[-1],)
        mlp_other.append(swap(after(middle[group][5], *earlier)))
    results = [
        (
            middle[group][0] + (middle[group][5].astype(F32) + mlp_other[group].astype(F32))
        ).astype(BF)
        for group in range(groups)
    ]
    d_rows = [cotangent[group * GROUP : (group + 1) * GROUP] for group in range(groups)]
    acts_mlp = pick(middle, 1)
    acts_attn = pick(forward, 1)
    sums = {}
    before = {group: () for group in range(groups)}
    if butterfly:
        sum_gate = sharing([(acts_mlp, pick(middle, 3))], 512)
        sum_gate.send = after(sum_gate.send, dact_other[0])
        sum_up = sharing([(acts_mlp, after(pick(middle, 4), sum_gate.keep()))], 512)
        sum_gate.exchange()
        before[0] = (sum_up.send, sum_gate.send)
    else:
        sums["gate"] = scattered(acts_mlp, pick(middle, 3))
        sums["up"] = scattered(acts_mlp, pick(middle, 4))
        sums["down"] = scattered(d_rows, pick(middle, 2))
    backward = []
    for group in range(groups):
        backward.append(backward_of(group, after(middle[group][6], *before[group])))
        if butterfly and group == 0:
            inners = after(pick(middle, 2), backward[0][9])
            sum_down = sharing([(d_rows, inners)], 512)
            sum_gate.exchange()
            sum_up.exchange()
            before[1] = (sum_gate.send, sum_up.send, sum_down.send)
    dtok_other = [swap(backward[group][9]) for group in range(groups)]
    d_tokens = []
    for group in range(groups):
        x = tokens[group * GROUP : (group + 1) * GROUP].astype(F32)
        scale = lax.rsqrt(jnp.mean(x * x, axis=1, keepdims=True) + EPS)
        d_act = backward[group][9].astype(F32) + dtok_other[group].astype(F32)
        weighted = d_act * gain_attn_row
        inner_mean = jnp.mean(weighted * x, axis=1, keepdims=True)
        d_tokens.append(
            (
                backward[group][0] + (scale * weighted - x * (scale * scale * scale) * inner_mean)
            ).astype(BF)
        )

    gains = functools.reduce(jnp.add, pick(backward, 2))
    g_bias = functools.reduce(jnp.add, pick(backward, 8))[0, :heads]
    gain_attn_sum = gains[1] + swap(gains[1])
    extra = jnp.concatenate(
        [
            jnp.zeros((width, heads), F32),
            gains[0][:, None],
            gain_attn_sum[:, None],
            jnp.broadcast_to(g_bias[None, :], (width, heads)),
            jnp.zeros((width, LANES - 2 - 2 * heads), F32),
        ],
        axis=1,
    )
    dattns = pick(backward, 1)
    gateds = pick(forward, 7)
    forget_grads = pick(backward, 7)
    if butterfly:
        head_cols = w_out.shape[0]
        block = 384
        sum_down.exchange()
        sum_up.exchange()
        sum_gate.exchange()
        first_acts, first_dattns = after(
            (acts_attn, dattns), sum_up.send, sum_gate.send, sum_down.send, results[0]
        )
        first = sharing(
            [
                (first_dattns, gateds),
                (first_acts, pick(backward, 3)),
                (first_acts, pick(backward, 4)),
            ],
            block,
        )
        sum_down.exchange()
        second = sharing(
            [
                (acts_attn, pick(backward, 5)),
                (acts_attn, pick(backward, 6)),
                (acts_attn, after(forget_grads, sum_down.send, first.send, dtok_other[0])),
            ],
            block,
            extra,
        )
        first.exchange()
        first.send = after(first.send, second.send)
        sums["gate"], sums["up"], sums["down"] = [
            one.result() for one in (sum_gate, sum_up, sum_down)
        ]
        total = first.result()
        sums["out"], sums["query"], sums["key"] = [
            total[:, index * head_cols : (index + 1) * head_cols] for index in range(3)
        ]
        total = second.result()
        sums["value"], sums["outgate"] = [
            total[:, index * head_cols : (index + 1) * head_cols] for index in range(2)
        ]
        small_sum = total[:, 2 * head_cols : 2 * head_cols + LANES]
    else:
        sums["out"] = scattered(dattns, gateds)
        for index, name in enumerate(("query", "key", "value", "outgate")):
            sums[name] = scattered(acts_attn, pick(backward, 3 + index))
        g_forget = functools.reduce(
            jnp.add, [dot_tn(left, right) for left, right in zip(acts_attn, forget_grads)]
        )
        small_sum = lax.psum_scatter(g_forget + extra, "dp", scatter_dimension=0, tiled=True)
    return (
        jnp.concatenate(results, axis=0),
        jnp.concatenate(d_tokens, axis=0),
        small_sum[:, heads + 1],
        sums["query"],
        sums["key"],
        sums["value"],
        sums["outgate"],
        small_sum[:, :heads],
        small_sum[0, heads + 2 : 2 * heads + 2],
        sums["out"].T,
        small_sum[:, heads],
        sums["gate"],
        sums["up"],
        sums["down"].T,
    )


def solution(mesh):
    in_specs = (
        P("dp", None),
        P("dp", None),
        P("dp", None),
        P(),
        P(None, "tensor"),
        P(None, "tensor"),
        P(None, "tensor"),
        P(None, "tensor"),
        P(None, "tensor"),
        P("tensor"),
        P("tensor", None),
        P(),
        P(None, "tensor"),
        P(None, "tensor"),
        P("tensor", None),
    )
    out_specs = (
        P("dp", None),
        P("dp", None),
        P("dp"),
        P("dp", "tensor"),
        P("dp", "tensor"),
        P("dp", "tensor"),
        P("dp", "tensor"),
        P("dp", "tensor"),
        P("tensor"),
        P("tensor", "dp"),
        P("dp"),
        P("dp", "tensor"),
        P("dp", "tensor"),
        P("tensor", "dp"),
    )
    return jax.shard_map(local, mesh=mesh, in_specs=in_specs, out_specs=out_specs, check_vma=False)
```

```python
import functools

import jax
import jax.numpy as jnp
from jax import lax
from jax.experimental import pallas as pl
from jax.experimental.pallas import tpu as pltpu
from jax.sharding import PartitionSpec as P

PROMPT = 256
CONT_TOK = 256
GROUP = PROMPT + CONT_TOK
LANES = 128
HEAD = 64
BLOCK_HEADS = 4
BLOCK_COLS = HEAD * BLOCK_HEADS
EPS = 1e-06
NEG = -1e30
VM = (60, 38, 36, 26)
BF = jnp.bfloat16
F32 = jnp.float32


def dot_dims(first_arg, second_arg, first_dim, second_dim):
    return lax.dot_general(
        first_arg,
        second_arg,
        (((first_dim,), (second_dim,)), ((), ())),
        preferred_element_type=F32,
    )


def dot_nn(first_arg, second_arg):
    return dot_dims(first_arg, second_arg, 1, 0)


def dot_nt(first_arg, second_arg):
    return dot_dims(first_arg, second_arg, 1, 1)


def dot_tn(first_arg, second_arg):
    return dot_dims(first_arg, second_arg, 0, 0)


def sigmoid(values):
    return 1.0 / (1.0 + jnp.exp(-values))


def split_three(values):
    high = values.astype(BF).astype(F32)
    rest = values - high
    middle = rest.astype(BF).astype(F32)
    return high, middle, rest - middle


def visible_pairs(ident_row_ref, ident_col_ref):
    row_ids = lax.broadcasted_iota(jnp.int32, (GROUP, GROUP), 0)
    col_ids = lax.broadcasted_iota(jnp.int32, (GROUP, GROUP), 1)
    ident_row = ident_row_ref[...]
    same = jnp.logical_or(ident_row == -1, ident_row == ident_col_ref[...])
    return jnp.logical_and(col_ids <= row_ids, same)


def lane_ids():
    return lax.broadcasted_iota(jnp.int32, (GROUP, LANES), 1)


def place_extras(lanes, own, main, base, extras, constant_at):
    value = jnp.where(
        jnp.logical_and(lanes >= base + constant_at, lanes < base + constant_at + 3), 1.0, 0.0
    )
    offset = 0 if constant_at else 3
    for position, column in enumerate(extras):
        value = jnp.where(lanes == base + offset + position, column, value)
    return jnp.where(own, main, value).astype(BF)


def column_of(lanes, values, index):
    return jnp.sum(jnp.where(lanes == index, values, 0.0), axis=1, keepdims=True)


def attn_fwd_kernel(
    x_ref,
    ident_row_ref,
    ident_col_ref,
    gain_ref,
    wq_ref,
    wk_ref,
    wv_ref,
    wg_ref,
    wf_ref,
    bias_ref,
    wo_ref,
    part_ref,
    act_ref,
    q_ref,
    k_ref,
    v_ref,
    gpre_ref,
    att_ref,
    gated_ref,
    lse_ref,
    decay_ref,
    forget_ref,
    acc_ref,
    mask_ref,
):
    step = pl.program_id(0)
    lanes = lane_ids()

    @pl.when(step == 0)
    def _():
        x = x_ref[...].astype(F32)
        scale = lax.rsqrt(jnp.mean(x * x, axis=1, keepdims=True) + EPS)
        act = (x * scale * gain_ref[...]).astype(BF)
        act_ref[...] = act
        forget_pre = dot_nn(act, wf_ref[...]) + bias_ref[...]
        forget_ref[...] = forget_pre
        log_forget = jnp.minimum(forget_pre, 0.0) - jnp.log1p(jnp.exp(-jnp.abs(forget_pre)))
        allowed = visible_pairs(ident_row_ref, ident_col_ref)
        mask_ref[...] = jnp.where(allowed, 0.0, NEG)
        ancestry = jnp.where(allowed, 1.0, 0.0).astype(BF)
        high, middle, low = split_three(log_forget)
        decay_ref[...] = (
            dot_nn(ancestry, high.astype(BF))
            + dot_nn(ancestry, middle.astype(BF))
            + dot_nn(ancestry, low.astype(BF))
        )
        acc_ref[...] = jnp.zeros_like(acc_ref)
        lse_ref[...] = jnp.zeros_like(lse_ref)

    act = act_ref[...]
    queries = dot_nn(act, wq_ref[...]).astype(BF)
    keys_low = dot_nn(act, wk_ref[...]).astype(BF)
    values_low = dot_nn(act, wv_ref[...]).astype(BF)
    gate_pre = dot_nn(act, wg_ref[...])
    gate = sigmoid(gate_pre)
    q_ref[...] = queries
    k_ref[...] = keys_low
    v_ref[...] = values_low
    gpre_ref[...] = gate_pre.astype(BF)
    attended_pairs = []
    for pair in range(BLOCK_HEADS // 2):
        cols = slice(pair * LANES, (pair + 1) * LANES)
        q_pair = queries[:, cols].astype(F32) * (HEAD**-0.5)
        k_pair = keys_low[:, cols].astype(F32)
        v_pair = values_low[:, cols]
        outs = []
        for half in range(2):
            own = (lanes < HEAD) if half == 0 else (lanes >= HEAD)
            base = HEAD if half == 0 else 0
            head = step * BLOCK_HEADS + pair * 2 + half
            decay = column_of(lanes, decay_ref[...], head)
            parts = split_three(decay)
            q_ext = place_extras(lanes, own, q_pair, base, parts, 3)
            k_ext = place_extras(lanes, own, k_pair, base, [-value for value in parts], 0)
            scores_p = dot_nt(q_ext[:PROMPT], k_ext[:PROMPT]) + mask_ref[:PROMPT, :PROMPT]
            scores_a = dot_nt(q_ext[PROMPT:], k_ext[:PROMPT])
            scores_b = dot_nt(q_ext[PROMPT:], k_ext[PROMPT:]) + mask_ref[PROMPT:, PROMPT:]
            max_p = jnp.max(scores_p, axis=1, keepdims=True)
            exp_p = jnp.exp(scores_p - max_p)
            sum_p = jnp.sum(exp_p, axis=1, keepdims=True)
            out_p = dot_nn(exp_p.astype(BF), v_pair[:PROMPT]) * (1.0 / sum_p)
            max_c = jnp.maximum(
                jnp.max(scores_a, axis=1, keepdims=True), jnp.max(scores_b, axis=1, keepdims=True)
            )
            exp_a = jnp.exp(scores_a - max_c)
            exp_b = jnp.exp(scores_b - max_c)
            sum_c = jnp.sum(exp_a, axis=1, keepdims=True) + jnp.sum(exp_b, axis=1, keepdims=True)
            out_c = dot_nn(exp_a.astype(BF), v_pair[:PROMPT]) + dot_nn(
                exp_b.astype(BF), v_pair[PROMPT:]
            )
            out_c = out_c * (1.0 / sum_c)
            outs.append(jnp.concatenate([out_p, out_c], axis=0))
            lse = jnp.concatenate([max_p + jnp.log(sum_p), max_c + jnp.log(sum_c)], axis=0)
            lse_ref[...] = jnp.where(lanes == head, lse, lse_ref[...])
        attended_pairs.append(jnp.where(lanes < HEAD, outs[0], outs[1]))
    attended = jnp.concatenate(attended_pairs, axis=1)
    att_ref[...] = attended.astype(BF)
    gated = (attended * gate).astype(BF)
    gated_ref[...] = gated
    acc_ref[...] += dot_nn(gated, wo_ref[...])

    @pl.when(step == pl.num_programs(0) - 1)
    def _():
        part_ref[...] = acc_ref[...].astype(BF)


def mlp_kernel(
    x_ref,
    own_ref,
    other_ref,
    d_ref,
    gain_ref,
    wg_ref,
    wu_ref,
    wd_ref,
    hidden_ref,
    act_ref,
    inner_ref,
    dgate_ref,
    dup_ref,
    mlp_ref,
    dact_ref,
    acc_mlp_ref,
    acc_dact_ref,
):
    step = pl.program_id(0)

    @pl.when(step == 0)
    def _():
        hidden = x_ref[...].astype(F32) + (own_ref[...].astype(F32) + other_ref[...].astype(F32))
        hidden_ref[...] = hidden.astype(BF)
        scale = lax.rsqrt(jnp.mean(hidden * hidden, axis=1, keepdims=True) + EPS)
        act_ref[...] = (hidden * scale * gain_ref[...]).astype(BF)
        acc_mlp_ref[...] = jnp.zeros_like(acc_mlp_ref)
        acc_dact_ref[...] = jnp.zeros_like(acc_dact_ref)

    act = act_ref[...]
    gate = dot_nn(act, wg_ref[...])
    up = dot_nn(act, wu_ref[...])
    d_inner = dot_nt(d_ref[...], wd_ref[...])
    gate_sigmoid = sigmoid(gate)
    silu_value = gate * gate_sigmoid
    inner = (silu_value * up).astype(BF)
    d_gate = (d_inner * up * gate_sigmoid * (1.0 + gate * (1.0 - gate_sigmoid))).astype(BF)
    d_up = (d_inner * silu_value).astype(BF)
    inner_ref[...] = inner
    dgate_ref[...] = d_gate
    dup_ref[...] = d_up
    acc_dact_ref[...] += dot_nt(d_gate, wg_ref[...]) + dot_nt(d_up, wu_ref[...])
    acc_mlp_ref[...] += dot_nn(inner, wd_ref[...])

    @pl.when(step == pl.num_programs(0) - 1)
    def _():
        dact_ref[...] = acc_dact_ref[...].astype(BF)
        mlp_ref[...] = acc_mlp_ref[...].astype(BF)


def attn_bwd_kernel(
    x_ref,
    d_ref,
    hidden_ref,
    own_ref,
    other_ref,
    gain_ref,
    ident_row_ref,
    ident_col_ref,
    q_ref,
    k_ref,
    v_ref,
    gpre_ref,
    att_ref,
    lse_ref,
    decay_ref,
    forget_ref,
    wo_ref,
    wq_ref,
    wk_ref,
    wv_ref,
    wg_ref,
    wf_ref,
    pair_ref,
    dattn_ref,
    gains_ref,
    dq_ref,
    dk_ref,
    dv_ref,
    dgp_ref,
    dfp_ref,
    gbias_ref,
    dact_ref,
    acc_ref,
    mask_ref,
    ddecay_ref,
):
    step = pl.program_id(0)
    lanes = lane_ids()

    @pl.when(step == 0)
    def _():
        hidden = hidden_ref[...].astype(F32)
        d_act = own_ref[...].astype(F32) + other_ref[...].astype(F32)
        scale = lax.rsqrt(jnp.mean(hidden * hidden, axis=1, keepdims=True) + EPS)
        weighted = d_act * gain_ref[...]
        inner_mean = jnp.mean(weighted * hidden, axis=1, keepdims=True)
        d_hidden = d_ref[...].astype(F32) + (
            scale * weighted - hidden * (scale * scale * scale) * inner_mean
        )
        dattn_ref[...] = d_hidden.astype(BF)
        gains_ref[...] = jnp.zeros_like(gains_ref)
        gains_ref[0:1, :] = jnp.sum(d_act * hidden * scale, axis=0, keepdims=True)
        allowed = visible_pairs(ident_row_ref, ident_col_ref)
        mask_ref[...] = jnp.where(allowed, 0.0, NEG)
        acc_ref[...] = jnp.zeros_like(acc_ref)
        ddecay_ref[...] = jnp.zeros_like(ddecay_ref)

    d_gated = dot_nt(dattn_ref[...], wo_ref[...])
    gate = sigmoid(gpre_ref[...].astype(F32))
    attended = att_ref[...].astype(F32)
    d_gate_pre = (d_gated * attended * gate * (1.0 - gate)).astype(BF)
    dgp_ref[...] = d_gate_pre
    d_attended = (d_gated * gate).astype(BF)
    grads_q, grads_k, grads_v = [], [], []
    for pair in range(BLOCK_HEADS // 2):
        cols = slice(pair * LANES, (pair + 1) * LANES)
        q_low = q_ref[:, cols]
        k_low = k_ref[:, cols]
        v_low = v_ref[:, cols]
        q_pair = q_low.astype(F32)
        k_pair = k_low.astype(F32)
        v_pair = v_low.astype(F32)
        do_low = d_attended[:, cols]
        do_pair = do_low.astype(F32)
        row_products = do_pair * attended[:, cols]
        dqs, dks, dvs = [], [], []
        for half in range(2):
            own = (lanes < HEAD) if half == 0 else (lanes >= HEAD)
            base = HEAD if half == 0 else 0
            head = step * BLOCK_HEADS + pair * 2 + half
            decay = column_of(lanes, decay_ref[...], head)
            lse = column_of(lanes, lse_ref[...], head)
            row_inner = jnp.sum(jnp.where(own, row_products, 0.0), axis=1, keepdims=True)
            q_ext = place_extras(
                lanes, own, q_pair * (HEAD**-0.5), base, split_three(decay - lse), 3
            )
            k_ext = place_extras(
                lanes, own, k_pair, base, [-value for value in split_three(decay)], 0
            )
            do_ext = place_extras(lanes, own, do_pair, base, split_three(-row_inner), 3)
            v_ext = place_extras(lanes, own, v_pair, base, [], 0)
            k_one = jnp.where(own, k_pair, 1.0).astype(BF)
            q_one = jnp.where(own, q_pair, 1.0).astype(BF)
            probs_p = jnp.exp(
                dot_nt(q_ext[:PROMPT], k_ext[:PROMPT]) + mask_ref[:PROMPT, :PROMPT]
            )
            probs_a = jnp.exp(dot_nt(q_ext[PROMPT:], k_ext[:PROMPT]))
            probs_b = jnp.exp(
                dot_nt(q_ext[PROMPT:], k_ext[PROMPT:]) + mask_ref[PROMPT:, PROMPT:]
            )
            ds_p = (probs_p * dot_nt(do_ext[:PROMPT], v_ext[:PROMPT])).astype(BF)
            ds_a = (probs_a * dot_nt(do_ext[PROMPT:], v_ext[:PROMPT])).astype(BF)
            ds_b = (probs_b * dot_nt(do_ext[PROMPT:], v_ext[PROMPT:])).astype(BF)
            dv_top = dot_tn(probs_p.astype(BF), do_low[:PROMPT]) + dot_tn(
                probs_a.astype(BF), do_low[PROMPT:]
            )
            dv_low = dot_tn(probs_b.astype(BF), do_low[PROMPT:])
            dk_top = dot_tn(ds_p, q_one[:PROMPT]) + dot_tn(ds_a, q_one[PROMPT:])
            dk_low = dot_tn(ds_b, q_one[PROMPT:])
            dq_top = dot_nn(ds_p, k_one[:PROMPT])
            dq_low = dot_nn(ds_a, k_one[:PROMPT]) + dot_nn(ds_b, k_one[PROMPT:])
            dvs.append(jnp.concatenate([dv_top, dv_low], axis=0))
            dks.append(jnp.concatenate([dk_top, dk_low], axis=0))
            dqs.append(jnp.concatenate([dq_top, dq_low], axis=0))
            sums = (dqs[-1] - dks[-1])[:, base : base + 1]
            ddecay_ref[...] = jnp.where(lanes == head, sums, ddecay_ref[...])
        grads_q.append(jnp.where(lanes < HEAD, dqs[0], dqs[1]) * (HEAD**-0.5))
        grads_k.append(jnp.where(lanes < HEAD, dks[0], dks[1]) * (HEAD**-0.5))
        grads_v.append(jnp.where(lanes < HEAD, dvs[0], dvs[1]))
    d_queries = jnp.concatenate(grads_q, axis=1).astype(BF)
    d_keys = jnp.concatenate(grads_k, axis=1).astype(BF)
    d_values = jnp.concatenate(grads_v, axis=1).astype(BF)
    dq_ref[...] = d_queries
    dk_ref[...] = d_keys
    dv_ref[...] = d_values
    acc_ref[...] += (
        dot_nt(d_queries, wq_ref[...])
        + dot_nt(d_keys, wk_ref[...])
        + dot_nt(d_values, wv_ref[...])
        + dot_nt(d_gate_pre, wg_ref[...])
    )

    @pl.when(step == pl.num_programs(0) - 1)
    def _():
        ancestry = jnp.where(visible_pairs(ident_row_ref, ident_col_ref), 1.0, 0.0).astype(BF)
        high, middle, low = split_three(ddecay_ref[...])
        d_log_forget = (
            dot_tn(ancestry, high.astype(BF))
            + dot_tn(ancestry, middle.astype(BF))
            + dot_tn(ancestry, low.astype(BF))
        )
        d_forget = (d_log_forget * sigmoid(-forget_ref[...])).astype(BF)
        dfp_ref[...] = d_forget
        gbias_ref[0:1, :] = jnp.sum(d_forget.astype(F32), axis=0, keepdims=True)
        d_act = (acc_ref[...] + dot_nt(d_forget, wf_ref[...])).astype(BF)
        dact_ref[...] = d_act
        x = x_ref[...].astype(F32)
        scale = lax.rsqrt(jnp.mean(x * x, axis=1, keepdims=True) + EPS)
        gains_ref[1:2, :] = jnp.sum(d_act.astype(F32) * x * scale, axis=0, keepdims=True)


def whole(shape):
    return pl.BlockSpec(shape, lambda step: (0,) * len(shape), pipeline_mode=pl.Buffered(1))


def rows_of(group, width):
    return pl.BlockSpec(
        (GROUP, width), lambda step: (group, 0), pipeline_mode=pl.Buffered(1)
    )


def cols_block(rows, width):
    return pl.BlockSpec((rows, width), lambda step: (0, step))


def rows_block(width, cols):
    return pl.BlockSpec((width, cols), lambda step: (step, 0))


def shape_of(rows, cols, dtype):
    return jax.ShapeDtypeStruct((rows, cols), dtype)


def brief_cost():
    return pl.CostEstimate(flops=100_000_000, bytes_accessed=100_000, transcendentals=0)


def params_for(mebibytes):
    return pltpu.CompilerParams(
        vmem_limit_bytes=mebibytes * 1024 * 1024, dimension_semantics=("arbitrary",)
    )


def attn_forward(group, tokens, ident, gain, weights, forget_weight, forget_bias, w_out):
    width = tokens.shape[1]
    head_cols = w_out.shape[0]
    return pl.pallas_call(
        attn_fwd_kernel,
        grid=(head_cols // BLOCK_COLS,),
        in_specs=[
            rows_of(group, width),
            whole((1, GROUP)),
            whole((GROUP, 1)),
            whole((1, width)),
            cols_block(width, BLOCK_COLS),
            cols_block(width, BLOCK_COLS),
            cols_block(width, BLOCK_COLS),
            cols_block(width, BLOCK_COLS),
            whole((width, LANES)),
            whole((1, LANES)),
            rows_block(BLOCK_COLS, width),
        ],
        out_specs=[
            whole((GROUP, width)),
            whole((GROUP, width)),
            cols_block(GROUP, BLOCK_COLS),
            cols_block(GROUP, BLOCK_COLS),
            cols_block(GROUP, BLOCK_COLS),
            cols_block(GROUP, BLOCK_COLS),
            cols_block(GROUP, BLOCK_COLS),
            cols_block(GROUP, BLOCK_COLS),
            whole((GROUP, LANES)),
            whole((GROUP, LANES)),
            whole((GROUP, LANES)),
        ],
        out_shape=[
            shape_of(GROUP, width, BF),
            shape_of(GROUP, width, BF),
            shape_of(GROUP, head_cols, BF),
            shape_of(GROUP, head_cols, BF),
            shape_of(GROUP, head_cols, BF),
            shape_of(GROUP, head_cols, BF),
            shape_of(GROUP, head_cols, BF),
            shape_of(GROUP, head_cols, BF),
            shape_of(GROUP, LANES, F32),
            shape_of(GROUP, LANES, F32),
            shape_of(GROUP, LANES, F32),
        ],
        scratch_shapes=[pltpu.VMEM((GROUP, width), F32), pltpu.VMEM((GROUP, GROUP), F32)],
        compiler_params=params_for(VM[0]),
        cost_estimate=brief_cost(),
        name="attn_fwd",
    )(tokens, ident[0], ident[1], gain, *weights, forget_weight, forget_bias, w_out)


def mlp_both(group, tokens, own, other, cotangent, gain, w_gate, w_up, w_down):
    width = tokens.shape[1]
    hidden_units = w_down.shape[0]
    block = 512
    return pl.pallas_call(
        mlp_kernel,
        grid=(hidden_units // block,),
        in_specs=[
            rows_of(group, width),
            whole((GROUP, width)),
            whole((GROUP, width)),
            rows_of(group, width),
            whole((1, width)),
            cols_block(width, block),
            cols_block(width, block),
            rows_block(block, width),
        ],
        out_specs=[
            whole((GROUP, width)),
            whole((GROUP, width)),
            cols_block(GROUP, block),
            cols_block(GROUP, block),
            cols_block(GROUP, block),
            rows_of(0, width),
            whole((GROUP, width)),
        ],
        out_shape=[
            shape_of(GROUP, width, BF),
            shape_of(GROUP, width, BF),
            shape_of(GROUP, hidden_units, BF),
            shape_of(GROUP, hidden_units, BF),
            shape_of(GROUP, hidden_units, BF),
            shape_of(2 * GROUP, width, BF),
            shape_of(GROUP, width, BF),
        ],
        scratch_shapes=[pltpu.VMEM((GROUP, width), F32), pltpu.VMEM((GROUP, width), F32)],
        compiler_params=params_for(VM[1]),
        cost_estimate=brief_cost(),
        name="mlp_both",
    )(tokens, own, other, cotangent, gain, w_gate, w_up, w_down)


def attn_backward(
    group, tokens, cotangent, hidden, own, other, gain, ident, saved, w_out, weights, forget_weight,
    pair,
):
    width = tokens.shape[1]
    head_cols = w_out.shape[0]
    queries, keys_low, values_low, gate, attended, lse, decay, forget_pre = saved
    return pl.pallas_call(
        attn_bwd_kernel,
        grid=(head_cols // BLOCK_COLS,),
        in_specs=[
            rows_of(group, width),
            rows_of(group, width),
            whole((GROUP, width)),
            whole((GROUP, width)),
            whole((GROUP, width)),
            whole((1, width)),
            whole((1, GROUP)),
            whole((GROUP, 1)),
            cols_block(GROUP, BLOCK_COLS),
            cols_block(GROUP, BLOCK_COLS),
            cols_block(GROUP, BLOCK_COLS),
            cols_block(GROUP, BLOCK_COLS),
            cols_block(GROUP, BLOCK_COLS),
            whole((GROUP, LANES)),
            whole((GROUP, LANES)),
            whole((GROUP, LANES)),
            rows_block(BLOCK_COLS, width),
            cols_block(width, BLOCK_COLS),
            cols_block(width, BLOCK_COLS),
            cols_block(width, BLOCK_COLS),
            cols_block(width, BLOCK_COLS),
            whole((width, LANES)),
            pl.BlockSpec(memory_space=pl.ANY),
        ],
        out_specs=[
            whole((GROUP, width)),
            whole((8, width)),
            cols_block(GROUP, BLOCK_COLS),
            cols_block(GROUP, BLOCK_COLS),
            cols_block(GROUP, BLOCK_COLS),
            cols_block(GROUP, BLOCK_COLS),
            whole((GROUP, LANES)),
            whole((8, LANES)),
            rows_of(1, width),
        ],
        out_shape=[
            shape_of(GROUP, width, BF),
            shape_of(8, width, F32),
            shape_of(GROUP, head_cols, BF),
            shape_of(GROUP, head_cols, BF),
            shape_of(GROUP, head_cols, BF),
            shape_of(GROUP, head_cols, BF),
            shape_of(GROUP, LANES, BF),
            shape_of(8, LANES, F32),
            shape_of(2 * GROUP, width, BF),
        ],
        input_output_aliases={22: 8},
        scratch_shapes=[
            pltpu.VMEM((GROUP, width), F32),
            pltpu.VMEM((GROUP, GROUP), F32),
            pltpu.VMEM((GROUP, LANES), F32),
        ],
        compiler_params=params_for(VM[2]),
        cost_estimate=brief_cost(),
        name="attn_bwd",
    )(
        tokens,
        cotangent,
        hidden,
        own,
        other,
        gain,
        ident[0],
        ident[1],
        queries,
        keys_low,
        values_low,
        gate,
        attended,
        lse,
        decay,
        forget_pre,
        w_out,
        *weights,
        forget_weight,
        pair,
    )


def grad_kernel(place_ref, columns_ref, row_ref, *refs, groups, sets):
    total_ref = refs[-1]
    outputs = refs[-1 - 3 * len(sets) : -1]
    step = pl.program_id(0)
    blocks, block_rows = total_ref.shape[0], total_ref.shape[1]
    place = place_ref[0]

    def emit(left_refs, right_refs, extra_from, order, flip, keep_ref, low_ref, high_ref):
        total = dot_tn(left_refs[0][...], right_refs[0][...])
        for left_ref, right_ref in zip(left_refs[1:], right_refs[1:]):
            total = total + dot_tn(left_ref[...], right_ref[...])
        block = total.shape[1]
        if extra_from:
            lanes = lax.broadcasted_iota(jnp.int32, (8, block), 1)
            lines = lax.broadcasted_iota(jnp.int32, (8, block), 0)
            chosen = jnp.where(
                jnp.logical_and(lanes == lines + extra_from, lines < 2), 1.0, 0.0
            ).astype(BF)
            for part in split_three(columns_ref[...]):
                total = total + dot_tn(part.astype(BF), chosen)
            total = total + row_ref[0:1, :]
        for index in range(blocks):
            total_ref[index, :, :block] = total[index * block_rows : (index + 1) * block_rows]
        half = len(order) // 2
        for index, slot in enumerate(order):
            kept = total_ref[jnp.bitwise_xor(place, slot), :, :block]
            sent = total_ref[jnp.bitwise_xor(place, slot ^ flip), :, :block]
            keep_ref[index, :, :block] = kept.astype(BF)
            target = low_ref if index < half else high_ref
            target[index % half, :, :block] = sent.astype(BF)

    for number, (order, flip, plan) in enumerate(sets):
        for left_at, right_at, first, count, extra_from in plan:
            pl.when(jnp.logical_and(step >= first, step < first + count))(
                functools.partial(
                    emit,
                    refs[left_at : left_at + groups],
                    refs[right_at : right_at + groups],
                    extra_from,
                    order,
                    flip,
                    *outputs[3 * number : 3 * number + 3],
                )
            )


def half_order(bits):
    slots = [0]
    for bit in reversed(bits[1:]):
        slots = slots + [slot ^ bit for slot in slots]
    return slots


def weight_grad(sets, place, devices, block, extra=None):
    lefts = sets[0][0][0][0]
    width = lefts[0].shape[1]
    groups = len(lefts)
    rows = width // devices
    half = devices // 2
    arrays, specs, seen, layout, out_specs, out_shape = [], [], {}, [], [], []
    first = 0

    def span(start, count):
        return lambda step: (0, jnp.minimum(jnp.maximum(step - start, 0), count - 1))

    def add(items, spec):
        arrays.extend(items)
        specs.extend([spec] * groups)
        return len(arrays) - groups

    for number, (products, bits) in enumerate(sets):
        plan, start = [], first
        for index, (lefts, rights) in enumerate(products):
            if id(lefts[0]) not in seen:
                seen[id(lefts[0])] = add(lefts, rows_of(0, width))
            cols = rights[0].shape[1]
            narrow = cols < block
            count = max(cols // block, 1)
            at = add(rights, pl.BlockSpec((GROUP, min(cols, block)), span(first, count)))
            plan.append((seen[id(lefts[0])], at, first, count, extra[2] if narrow else 0))
            first += count
        layout.append((half_order(bits), bits[0], plan))
        place_of = span(start, first - start)
        for count in (half, half // 2, half // 2):
            out_specs.append(
                pl.BlockSpec(
                    (count, rows, block), lambda step, place_of=place_of: (0,) + place_of(step)
                )
            )
            out_shape.append(jax.ShapeDtypeStruct((count, rows, (first - start) * block), BF))
    columns, row = (jnp.zeros((8, LANES), F32),) * 2 if extra is None else extra[:2]
    outputs = pl.pallas_call(
        functools.partial(grad_kernel, groups=groups, sets=layout),
        grid=(first,),
        in_specs=[pl.BlockSpec(memory_space=pltpu.SMEM), whole(columns.shape), whole(row.shape)]
        + specs,
        out_specs=out_specs,
        out_shape=out_shape,
        scratch_shapes=[pltpu.VMEM((devices, rows, block), F32)],
        compiler_params=params_for(VM[3]),
        cost_estimate=brief_cost(),
        name="weight_grad",
    )(place, columns, row, *arrays)
    return [
        SharedSum(*outputs[3 * number : 3 * number + 3], bits, devices)
        for number, (_, bits) in enumerate(sets)
    ]


class SharedSum:
    def __init__(self, keep, low, high, bits, devices):
        self.parts, self.send = [keep], (low, high)
        self.bits, self.devices, self.stage = bits, devices, 0

    def exchange(self, *earlier):
        bit = self.bits[self.stage]
        pairs = [(index, index ^ bit) for index in range(self.devices)]
        got = jax.tree.map(lambda piece: lax.ppermute(piece, "dp", pairs), self.send)
        if earlier:
            got = after(got, *earlier)
        self.stage += 1
        if self.stage == len(self.bits):
            self.parts.append(got)
            return
        low, high = got if isinstance(got, tuple) else jnp.split(got, 2)
        half = low.shape[0]
        leaving = [part[half:] for part in self.parts] + [high]
        self.parts = [part[:half] for part in self.parts] + [low]
        self.send = functools.reduce(jnp.add, [part.astype(F32) for part in leaving]).astype(BF)

    def result(self):
        return functools.reduce(jnp.add, [part[0].astype(F32) for part in self.parts])


def after(values, *earlier):
    return lax.optimization_barrier((values, earlier))[0]


def local(
    tokens,
    cotangent,
    segments,
    gain_attn,
    w_query,
    w_key,
    w_value,
    w_outgate,
    w_forget,
    b_forget,
    w_out,
    gain_mlp,
    w_gate,
    w_up,
    w_down,
):
    devices = lax.axis_size("dp")
    place_index = lax.axis_index("dp")
    width = tokens.shape[1]
    groups = tokens.shape[0] // GROUP
    heads = w_forget.shape[1]
    rows = width // devices
    butterfly = devices & (devices - 1) == 0 and rows % 16 == 0
    place = jnp.reshape(place_index, (1,)).astype(jnp.int32)
    bits = [1 << level for level in range(devices.bit_length() - 1)]

    def swap(values):
        return lax.ppermute(values, "tensor", [(0, 1), (1, 0)])

    gain_attn_row = gain_attn[None, :]
    gain_mlp_row = gain_mlp[None, :]
    forget_weight = jnp.pad(w_forget, ((0, 0), (0, LANES - heads)))
    forget_bias = jnp.pad(b_forget, (0, LANES - heads))[None, :]
    weights = (w_query, w_key, w_value, w_outgate)
    idents = []
    for group in range(groups):
        row = jnp.concatenate([jnp.full((PROMPT,), -1, jnp.int32), segments[group]])
        idents.append((row[None, :], row[:, None]))

    def pick(source, index):
        return [source[group][index] for group in range(groups)]

    def scattered(lefts, rights):
        total = functools.reduce(
            jnp.add, [dot_tn(left, right) for left, right in zip(lefts, rights)]
        )
        return lax.psum_scatter(total, "dp", scatter_dimension=0, tiled=True)

    def forward_of(group, rows_in):
        return attn_forward(
            group,
            rows_in,
            idents[group],
            gain_attn_row,
            weights,
            forget_weight,
            forget_bias,
            w_out,
        )

    def middle_of(group, own):
        return mlp_both(
            group,
            tokens,
            own,
            attn_other[group],
            cotangent,
            gain_mlp_row,
            w_gate,
            w_up,
            w_down,
        )

    def backward_of(group, own):
        (_, _, queries, keys_low, values_low, gate, attended, _, lse, decay, forget_pre) = forward[
            group
        ]
        return attn_backward(
            group,
            tokens,
            cotangent,
            middle[group][0],
            own,
            dact_other[group],
            gain_mlp_row,
            idents[group],
            (queries, keys_low, values_low, gate, attended, lse, decay, forget_pre),
            w_out,
            weights,
            forget_weight,
            middle[group][5],
        )

    done = []

    def ordered(values):
        return after(values, *done) if done else values

    def mark(*values):
        done[:] = values

    def step(*sums_at_work):
        for one in sums_at_work:
            one.exchange(*done)
            mark(one.send if one.stage < len(one.bits) else one.parts)

    def gradient(sets, block, extra=None):
        lefts = sets[0][0][0][0]
        held = ordered(lefts)
        sets = [
            ([(held if left is lefts else left, right) for left, right in products], bits)
            for products, bits in sets
        ]
        sums_made = weight_grad(sets, place, devices, block, extra)
        mark(*[one.send for one in sums_made])
        return sums_made

    forward = []
    for group in range(groups):
        forward.append(forward_of(group, ordered(tokens)))
        mark(forward[-1][0])
    attn_other = [swap(forward[group][0]) for group in range(groups)]
    middle = []
    for group in range(groups):
        middle.append(middle_of(group, ordered(forward[group][0])))
        mark(middle[-1][6])
    dact_other = [swap(middle[group][6]) for group in range(groups)]
    d_rows = [cotangent[group * GROUP : (group + 1) * GROUP] for group in range(groups)]
    acts_mlp = pick(middle, 1)
    acts_attn = pick(forward, 1)
    z_first = [bits[0]] + bits[2:] + bits[1:2]
    sums = {}
    backward, last_other = [], []

    def go_back(group):
        backward.append(backward_of(group, ordered(middle[group][6])))
        mark(backward[-1][8])

    def send_last(group):
        last_other.append(swap(ordered(backward[group][8])))

    if butterfly:
        (sum_gate,) = gradient([([(acts_mlp, pick(middle, 3))], bits)], 512)
        dact_other[0] = ordered(dact_other[0])
        sum_gate.send = after(sum_gate.send, dact_other[0])
        (sum_up,) = gradient([([(acts_mlp, pick(middle, 4))], z_first)], 512)
        step(sum_gate)
        (sum_down,) = gradient([([(d_rows, pick(middle, 2))], bits)], 512)
        step(sum_up)
        go_back(0)
        for group in range(1, groups):
            dact_other[group] = ordered(dact_other[group])
        mark(dact_other[1:])
        step(sum_gate, sum_up, sum_down)
        send_last(0)
        for group in range(1, groups):
            go_back(group)
        step(sum_gate, sum_up, sum_down)
    else:
        sums["gate"] = scattered(acts_mlp, pick(middle, 3))
        sums["up"] = scattered(acts_mlp, pick(middle, 4))
        sums["down"] = scattered(d_rows, pick(middle, 2))
        for group in range(groups):
            go_back(group)
            send_last(group)

    gains = functools.reduce(jnp.add, pick(backward, 1))
    g_bias = functools.reduce(jnp.add, pick(backward, 7))
    g_bias = jnp.pad(g_bias[:, :heads], ((0, 0), (heads + 2, LANES - 2 * heads - 2)))
    dattns = pick(backward, 0)
    gateds = pick(forward, 7)
    forget_grads = pick(backward, 6)
    if butterfly:
        head_cols = w_out.shape[0]
        (sum_first,) = gradient(
            [
                (
                    [
                        (acts_attn, pick(backward, 2)),
                        (acts_attn, pick(backward, 3)),
                        (dattns, gateds),
                    ],
                    bits,
                )
            ],
            384,
        )
        step(sum_gate, sum_up, sum_down)
        (sum_second,) = gradient(
            [
                (
                    [
                        (acts_attn, pick(backward, 4)),
                        (acts_attn, pick(backward, 5)),
                        (acts_attn, forget_grads),
                    ],
                    z_first,
                )
            ],
            256,
            (gains, g_bias, heads),
        )
        last_other[0] = ordered(last_other[0])
        mark(last_other[0])
        step(sum_first, sum_second)
        for group in range(1, groups):
            send_last(group)
        step(sum_second, sum_down, sum_first)
        step(sum_first)
        for group in range(1, groups):
            last_other[group] = ordered(last_other[group])
        mark(last_other)
        step(sum_second)
        step(sum_second, sum_first)
        sums["gate"], sums["up"], sums["down"] = [
            one.result() for one in (sum_gate, sum_up, sum_down)
        ]
        total = sum_first.result()
        sums["query"], sums["key"], sums["out"] = [
            total[:, index * head_cols : (index + 1) * head_cols] for index in range(3)
        ]
        total = sum_second.result()
        sums["value"], sums["outgate"] = [
            total[:, index * head_cols : (index + 1) * head_cols] for index in range(2)
        ]
        small_sum = total[:, 2 * head_cols : 2 * head_cols + LANES]
    else:
        sums["out"] = scattered(dattns, gateds)
        for index, name in enumerate(("query", "key", "value", "outgate")):
            sums[name] = scattered(acts_attn, pick(backward, 2 + index))
        g_forget = functools.reduce(
            jnp.add, [dot_tn(left, right) for left, right in zip(acts_attn, forget_grads)]
        )
        columns = jnp.pad(gains[:2].T, ((0, 0), (heads, LANES - heads - 2)))
        small = g_forget + columns + g_bias[:1]
        small_sum = lax.psum_scatter(small, "dp", scatter_dimension=0, tiled=True)
    results, d_tokens = [], []
    for group in range(groups):
        x = tokens[group * GROUP : (group + 1) * GROUP].astype(F32)
        both = backward[group][8].astype(F32) + last_other[group].astype(F32)
        mlp_sum, d_act = both[:GROUP], both[GROUP:]
        results.append((middle[group][0].astype(F32) + mlp_sum).astype(BF))
        scale = lax.rsqrt(jnp.mean(x * x, axis=1, keepdims=True) + EPS)
        weighted = d_act * gain_attn_row
        inner_mean = jnp.mean(weighted * x, axis=1, keepdims=True)
        d_norm = scale * weighted - x * (scale * scale * scale) * inner_mean
        d_tokens.append((backward[group][0].astype(F32) + d_norm).astype(BF))
    return (
        jnp.concatenate(results, axis=0),
        jnp.concatenate(d_tokens, axis=0),
        small_sum[:, heads + 1] + swap(small_sum[:, heads + 1]),
        sums["query"],
        sums["key"],
        sums["value"],
        sums["outgate"],
        small_sum[:, :heads],
        small_sum[0, heads + 2 : 2 * heads + 2],
        sums["out"].T,
        small_sum[:, heads],
        sums["gate"],
        sums["up"],
        sums["down"].T,
    )


def solution(mesh):
    in_specs = (
        P("dp", None),
        P("dp", None),
        P("dp", None),
        P(),
        P(None, "tensor"),
        P(None, "tensor"),
        P(None, "tensor"),
        P(None, "tensor"),
        P(None, "tensor"),
        P("tensor"),
        P("tensor", None),
        P(),
        P(None, "tensor"),
        P(None, "tensor"),
        P("tensor", None),
    )
    out_specs = (
        P("dp", None),
        P("dp", None),
        P("dp"),
        P("dp", "tensor"),
        P("dp", "tensor"),
        P("dp", "tensor"),
        P("dp", "tensor"),
        P("dp", "tensor"),
        P("tensor"),
        P("tensor", "dp"),
        P("dp"),
        P("dp", "tensor"),
        P("dp", "tensor"),
        P("tensor", "dp"),
    )
    return jax.shard_map(local, mesh=mesh, in_specs=in_specs, out_specs=out_specs, check_vma=False)
```

```python
import functools

import jax
import jax.numpy as jnp
from jax import lax
from jax.experimental import pallas as pl
from jax.experimental.pallas import tpu as pltpu
from jax.sharding import PartitionSpec as P

PROMPT = 256
CONT_TOK = 256
GROUP = PROMPT + CONT_TOK
LANES = 128
HEAD = 64
BLOCK_HEADS = 4
BLOCK_COLS = HEAD * BLOCK_HEADS
EPS = 1e-06
NEG = -1e30
VM = (60, 40, 38, 26)
BF = jnp.bfloat16
F32 = jnp.float32


def dot_dims(first_arg, second_arg, first_dim, second_dim):
    return lax.dot_general(
        first_arg,
        second_arg,
        (((first_dim,), (second_dim,)), ((), ())),
        preferred_element_type=F32,
    )


def dot_nn(first_arg, second_arg):
    return dot_dims(first_arg, second_arg, 1, 0)


def dot_nt(first_arg, second_arg):
    return dot_dims(first_arg, second_arg, 1, 1)


def dot_tn(first_arg, second_arg):
    return dot_dims(first_arg, second_arg, 0, 0)


def sigmoid(values):
    return 1.0 / (1.0 + jnp.exp(-values))


def split_three(values):
    high = values.astype(BF).astype(F32)
    rest = values - high
    middle = rest.astype(BF).astype(F32)
    return high, middle, rest - middle


def visible_pairs(ident_row_ref, ident_col_ref):
    row_ids = lax.broadcasted_iota(jnp.int32, (GROUP, GROUP), 0)
    col_ids = lax.broadcasted_iota(jnp.int32, (GROUP, GROUP), 1)
    ident_row = ident_row_ref[...]
    same = jnp.logical_or(ident_row == -1, ident_row == ident_col_ref[...])
    return jnp.logical_and(col_ids <= row_ids, same)


def lane_ids():
    return lax.broadcasted_iota(jnp.int32, (GROUP, LANES), 1)


def place_extras(lanes, own, main, base, extras, constant_at):
    value = jnp.where(
        jnp.logical_and(lanes >= base + constant_at, lanes < base + constant_at + 3), 1.0, 0.0
    )
    offset = 0 if constant_at else 3
    for position, column in enumerate(extras):
        value = jnp.where(lanes == base + offset + position, column, value)
    return jnp.where(own, main, value).astype(BF)


def column_of(lanes, values, index):
    return jnp.sum(jnp.where(lanes == index, values, 0.0), axis=1, keepdims=True)


def attn_fwd_kernel(
    x_ref,
    ident_row_ref,
    ident_col_ref,
    gain_ref,
    wq_ref,
    wk_ref,
    wv_ref,
    wg_ref,
    wf_ref,
    bias_ref,
    wo_ref,
    part_ref,
    act_ref,
    q_ref,
    k_ref,
    v_ref,
    gpre_ref,
    att_ref,
    gated_ref,
    lse_ref,
    decay_ref,
    forget_ref,
    acc_ref,
    mask_ref,
):
    step = pl.program_id(0)
    lanes = lane_ids()

    @pl.when(step == 0)
    def _():
        x = x_ref[...].astype(F32)
        scale = lax.rsqrt(jnp.mean(x * x, axis=1, keepdims=True) + EPS)
        act = (x * scale * gain_ref[...]).astype(BF)
        act_ref[...] = act
        forget_pre = dot_nn(act, wf_ref[...]) + bias_ref[...]
        forget_ref[...] = forget_pre
        log_forget = jnp.minimum(forget_pre, 0.0) - jnp.log1p(jnp.exp(-jnp.abs(forget_pre)))
        allowed = visible_pairs(ident_row_ref, ident_col_ref)
        mask_ref[...] = jnp.where(allowed, 0.0, NEG)
        ancestry = jnp.where(allowed, 1.0, 0.0).astype(BF)
        high, middle, low = split_three(log_forget)
        decay_ref[...] = (
            dot_nn(ancestry, high.astype(BF))
            + dot_nn(ancestry, middle.astype(BF))
            + dot_nn(ancestry, low.astype(BF))
        )
        acc_ref[...] = jnp.zeros_like(acc_ref)
        lse_ref[...] = jnp.zeros_like(lse_ref)

    act = act_ref[...]
    queries = dot_nn(act, wq_ref[...]).astype(BF)
    keys_low = dot_nn(act, wk_ref[...]).astype(BF)
    values_low = dot_nn(act, wv_ref[...]).astype(BF)
    gate_pre = dot_nn(act, wg_ref[...])
    gate = sigmoid(gate_pre)
    q_ref[...] = queries
    k_ref[...] = keys_low
    v_ref[...] = values_low
    gpre_ref[...] = gate_pre.astype(BF)
    attended_pairs = []
    for pair in range(BLOCK_HEADS // 2):
        cols = slice(pair * LANES, (pair + 1) * LANES)
        q_pair = queries[:, cols].astype(F32) * (HEAD**-0.5)
        k_pair = keys_low[:, cols].astype(F32)
        v_pair = values_low[:, cols]
        outs = []
        for half in range(2):
            own = (lanes < HEAD) if half == 0 else (lanes >= HEAD)
            base = HEAD if half == 0 else 0
            head = step * BLOCK_HEADS + pair * 2 + half
            decay = column_of(lanes, decay_ref[...], head)
            parts = split_three(decay)
            q_ext = place_extras(lanes, own, q_pair, base, parts, 3)
            k_ext = place_extras(lanes, own, k_pair, base, [-value for value in parts], 0)
            scores_p = dot_nt(q_ext[:PROMPT], k_ext[:PROMPT]) + mask_ref[:PROMPT, :PROMPT]
            scores_a = dot_nt(q_ext[PROMPT:], k_ext[:PROMPT])
            scores_b = dot_nt(q_ext[PROMPT:], k_ext[PROMPT:]) + mask_ref[PROMPT:, PROMPT:]
            max_p = jnp.max(scores_p, axis=1, keepdims=True)
            exp_p = jnp.exp(scores_p - max_p)
            sum_p = jnp.sum(exp_p, axis=1, keepdims=True)
            out_p = dot_nn(exp_p.astype(BF), v_pair[:PROMPT]) * (1.0 / sum_p)
            max_c = jnp.maximum(
                jnp.max(scores_a, axis=1, keepdims=True), jnp.max(scores_b, axis=1, keepdims=True)
            )
            exp_a = jnp.exp(scores_a - max_c)
            exp_b = jnp.exp(scores_b - max_c)
            sum_c = jnp.sum(exp_a, axis=1, keepdims=True) + jnp.sum(exp_b, axis=1, keepdims=True)
            out_c = dot_nn(exp_a.astype(BF), v_pair[:PROMPT]) + dot_nn(
                exp_b.astype(BF), v_pair[PROMPT:]
            )
            out_c = out_c * (1.0 / sum_c)
            outs.append(jnp.concatenate([out_p, out_c], axis=0))
            lse = jnp.concatenate([max_p + jnp.log(sum_p), max_c + jnp.log(sum_c)], axis=0)
            lse_ref[...] = jnp.where(lanes == head, lse, lse_ref[...])
        attended_pairs.append(jnp.where(lanes < HEAD, outs[0], outs[1]))
    attended = jnp.concatenate(attended_pairs, axis=1)
    att_ref[...] = attended.astype(BF)
    gated = (attended * gate).astype(BF)
    gated_ref[...] = gated
    acc_ref[...] += dot_nn(gated, wo_ref[...])

    @pl.when(step == pl.num_programs(0) - 1)
    def _():
        part_ref[...] = acc_ref[...].astype(BF)


def mlp_kernel(
    x_ref,
    own_ref,
    other_ref,
    d_ref,
    gain_ref,
    wg_ref,
    wu_ref,
    wd_ref,
    hidden_ref,
    act_ref,
    inner_ref,
    dgate_ref,
    dup_ref,
    mlp_ref,
    dact_ref,
    acc_mlp_ref,
    acc_dact_ref,
):
    step = pl.program_id(0)

    @pl.when(step == 0)
    def _():
        hidden = x_ref[...].astype(F32) + (own_ref[...].astype(F32) + other_ref[...].astype(F32))
        hidden_ref[...] = hidden
        scale = lax.rsqrt(jnp.mean(hidden * hidden, axis=1, keepdims=True) + EPS)
        act_ref[...] = (hidden * scale * gain_ref[...]).astype(BF)
        acc_mlp_ref[...] = jnp.zeros_like(acc_mlp_ref)
        acc_dact_ref[...] = jnp.zeros_like(acc_dact_ref)

    act = act_ref[...]
    gate = dot_nn(act, wg_ref[...])
    up = dot_nn(act, wu_ref[...])
    d_inner = dot_nt(d_ref[...], wd_ref[...])
    gate_sigmoid = sigmoid(gate)
    silu_value = gate * gate_sigmoid
    inner = (silu_value * up).astype(BF)
    d_gate = (d_inner * up * gate_sigmoid * (1.0 + gate * (1.0 - gate_sigmoid))).astype(BF)
    d_up = (d_inner * silu_value).astype(BF)
    inner_ref[...] = inner
    dgate_ref[...] = d_gate
    dup_ref[...] = d_up
    acc_dact_ref[...] += dot_nt(d_gate, wg_ref[...]) + dot_nt(d_up, wu_ref[...])
    acc_mlp_ref[...] += dot_nn(inner, wd_ref[...])

    @pl.when(step == pl.num_programs(0) - 1)
    def _():
        dact_ref[...] = acc_dact_ref[...].astype(BF)
        mlp_ref[...] = acc_mlp_ref[...].astype(BF)


def attn_bwd_kernel(
    x_ref,
    d_ref,
    hidden_ref,
    own_ref,
    other_ref,
    gain_ref,
    ident_row_ref,
    ident_col_ref,
    q_ref,
    k_ref,
    v_ref,
    gpre_ref,
    att_ref,
    lse_ref,
    decay_ref,
    forget_ref,
    wo_ref,
    wq_ref,
    wk_ref,
    wv_ref,
    wg_ref,
    wf_ref,
    pair_ref,
    dattn_ref,
    gains_ref,
    dq_ref,
    dk_ref,
    dv_ref,
    dgp_ref,
    dfp_ref,
    gbias_ref,
    dact_ref,
    acc_ref,
    mask_ref,
    ddecay_ref,
):
    step = pl.program_id(0)
    lanes = lane_ids()

    @pl.when(step == 0)
    def _():
        hidden = hidden_ref[...].astype(F32)
        d_act = own_ref[...].astype(F32) + other_ref[...].astype(F32)
        scale = lax.rsqrt(jnp.mean(hidden * hidden, axis=1, keepdims=True) + EPS)
        weighted = d_act * gain_ref[...]
        inner_mean = jnp.mean(weighted * hidden, axis=1, keepdims=True)
        d_hidden = d_ref[...].astype(F32) + (
            scale * weighted - hidden * (scale * scale * scale) * inner_mean
        )
        dattn_ref[...] = d_hidden.astype(BF)
        gains_ref[...] = jnp.zeros_like(gains_ref)
        gains_ref[0:1, :] = jnp.sum(d_act * hidden * scale, axis=0, keepdims=True)
        allowed = visible_pairs(ident_row_ref, ident_col_ref)
        mask_ref[...] = jnp.where(allowed, 0.0, NEG)
        acc_ref[...] = jnp.zeros_like(acc_ref)
        ddecay_ref[...] = jnp.zeros_like(ddecay_ref)

    d_gated = dot_nt(dattn_ref[...], wo_ref[...])
    gate = sigmoid(gpre_ref[...].astype(F32))
    attended = att_ref[...].astype(F32)
    d_gate_pre = (d_gated * attended * gate * (1.0 - gate)).astype(BF)
    dgp_ref[...] = d_gate_pre
    d_attended = (d_gated * gate).astype(BF)
    grads_q, grads_k, grads_v = [], [], []
    for pair in range(BLOCK_HEADS // 2):
        cols = slice(pair * LANES, (pair + 1) * LANES)
        q_low = q_ref[:, cols]
        k_low = k_ref[:, cols]
        v_low = v_ref[:, cols]
        q_pair = q_low.astype(F32)
        k_pair = k_low.astype(F32)
        v_pair = v_low.astype(F32)
        do_low = d_attended[:, cols]
        do_pair = do_low.astype(F32)
        row_products = do_pair * attended[:, cols]
        dqs, dks, dvs = [], [], []
        for half in range(2):
            own = (lanes < HEAD) if half == 0 else (lanes >= HEAD)
            base = HEAD if half == 0 else 0
            head = step * BLOCK_HEADS + pair * 2 + half
            decay = column_of(lanes, decay_ref[...], head)
            lse = column_of(lanes, lse_ref[...], head)
            row_inner = jnp.sum(jnp.where(own, row_products, 0.0), axis=1, keepdims=True)
            q_ext = place_extras(
                lanes, own, q_pair * (HEAD**-0.5), base, split_three(decay - lse), 3
            )
            k_ext = place_extras(
                lanes, own, k_pair, base, [-value for value in split_three(decay)], 0
            )
            do_ext = place_extras(lanes, own, do_pair, base, split_three(-row_inner), 3)
            v_ext = place_extras(lanes, own, v_pair, base, [], 0)
            k_one = jnp.where(own, k_pair, 1.0).astype(BF)
            q_one = jnp.where(own, q_pair, 1.0).astype(BF)
            probs_p = jnp.exp(
                dot_nt(q_ext[:PROMPT], k_ext[:PROMPT]) + mask_ref[:PROMPT, :PROMPT]
            )
            probs_a = jnp.exp(dot_nt(q_ext[PROMPT:], k_ext[:PROMPT]))
            probs_b = jnp.exp(
                dot_nt(q_ext[PROMPT:], k_ext[PROMPT:]) + mask_ref[PROMPT:, PROMPT:]
            )
            ds_p = (probs_p * dot_nt(do_ext[:PROMPT], v_ext[:PROMPT])).astype(BF)
            ds_a = (probs_a * dot_nt(do_ext[PROMPT:], v_ext[:PROMPT])).astype(BF)
            ds_b = (probs_b * dot_nt(do_ext[PROMPT:], v_ext[PROMPT:])).astype(BF)
            dv_top = dot_tn(probs_p.astype(BF), do_low[:PROMPT]) + dot_tn(
                probs_a.astype(BF), do_low[PROMPT:]
            )
            dv_low = dot_tn(probs_b.astype(BF), do_low[PROMPT:])
            dk_top = dot_tn(ds_p, q_one[:PROMPT]) + dot_tn(ds_a, q_one[PROMPT:])
            dk_low = dot_tn(ds_b, q_one[PROMPT:])
            dq_top = dot_nn(ds_p, k_one[:PROMPT])
            dq_low = dot_nn(ds_a, k_one[:PROMPT]) + dot_nn(ds_b, k_one[PROMPT:])
            dvs.append(jnp.concatenate([dv_top, dv_low], axis=0))
            dks.append(jnp.concatenate([dk_top, dk_low], axis=0))
            dqs.append(jnp.concatenate([dq_top, dq_low], axis=0))
            sums = (dqs[-1] - dks[-1])[:, base : base + 1]
            ddecay_ref[...] = jnp.where(lanes == head, sums, ddecay_ref[...])
        grads_q.append(jnp.where(lanes < HEAD, dqs[0], dqs[1]) * (HEAD**-0.5))
        grads_k.append(jnp.where(lanes < HEAD, dks[0], dks[1]) * (HEAD**-0.5))
        grads_v.append(jnp.where(lanes < HEAD, dvs[0], dvs[1]))
    d_queries = jnp.concatenate(grads_q, axis=1).astype(BF)
    d_keys = jnp.concatenate(grads_k, axis=1).astype(BF)
    d_values = jnp.concatenate(grads_v, axis=1).astype(BF)
    dq_ref[...] = d_queries
    dk_ref[...] = d_keys
    dv_ref[...] = d_values
    acc_ref[...] += (
        dot_nt(d_queries, wq_ref[...])
        + dot_nt(d_keys, wk_ref[...])
        + dot_nt(d_values, wv_ref[...])
        + dot_nt(d_gate_pre, wg_ref[...])
    )

    @pl.when(step == pl.num_programs(0) - 1)
    def _():
        ancestry = jnp.where(visible_pairs(ident_row_ref, ident_col_ref), 1.0, 0.0).astype(BF)
        high, middle, low = split_three(ddecay_ref[...])
        d_log_forget = (
            dot_tn(ancestry, high.astype(BF))
            + dot_tn(ancestry, middle.astype(BF))
            + dot_tn(ancestry, low.astype(BF))
        )
        d_forget = (d_log_forget * sigmoid(-forget_ref[...])).astype(BF)
        dfp_ref[...] = d_forget
        gbias_ref[0:1, :] = jnp.sum(d_forget.astype(F32), axis=0, keepdims=True)
        d_act = (acc_ref[...] + dot_nt(d_forget, wf_ref[...])).astype(BF)
        dact_ref[...] = d_act
        x = x_ref[...].astype(F32)
        scale = lax.rsqrt(jnp.mean(x * x, axis=1, keepdims=True) + EPS)
        gains_ref[1:2, :] = jnp.sum(d_act.astype(F32) * x * scale, axis=0, keepdims=True)


def whole(shape):
    return pl.BlockSpec(shape, lambda step: (0,) * len(shape), pipeline_mode=pl.Buffered(1))


def rows_of(group, width):
    return pl.BlockSpec(
        (GROUP, width), lambda step: (group, 0), pipeline_mode=pl.Buffered(1)
    )


def cols_block(rows, width):
    return pl.BlockSpec((rows, width), lambda step: (0, step))


def rows_block(width, cols):
    return pl.BlockSpec((width, cols), lambda step: (step, 0))


def shape_of(rows, cols, dtype):
    return jax.ShapeDtypeStruct((rows, cols), dtype)


def brief_cost():
    return pl.CostEstimate(flops=100_000_000, bytes_accessed=100_000, transcendentals=0)


def params_for(mebibytes):
    return pltpu.CompilerParams(
        vmem_limit_bytes=mebibytes * 1024 * 1024, dimension_semantics=("arbitrary",)
    )


def attn_forward(group, tokens, ident, gain, weights, forget_weight, forget_bias, w_out):
    width = tokens.shape[1]
    head_cols = w_out.shape[0]
    return pl.pallas_call(
        attn_fwd_kernel,
        grid=(head_cols // BLOCK_COLS,),
        in_specs=[
            rows_of(group, width),
            whole((1, GROUP)),
            whole((GROUP, 1)),
            whole((1, width)),
            cols_block(width, BLOCK_COLS),
            cols_block(width, BLOCK_COLS),
            cols_block(width, BLOCK_COLS),
            cols_block(width, BLOCK_COLS),
            whole((width, LANES)),
            whole((1, LANES)),
            rows_block(BLOCK_COLS, width),
        ],
        out_specs=[
            whole((GROUP, width)),
            whole((GROUP, width)),
            cols_block(GROUP, BLOCK_COLS),
            cols_block(GROUP, BLOCK_COLS),
            cols_block(GROUP, BLOCK_COLS),
            cols_block(GROUP, BLOCK_COLS),
            cols_block(GROUP, BLOCK_COLS),
            cols_block(GROUP, BLOCK_COLS),
            whole((GROUP, LANES)),
            whole((GROUP, LANES)),
            whole((GROUP, LANES)),
        ],
        out_shape=[
            shape_of(GROUP, width, BF),
            shape_of(GROUP, width, BF),
            shape_of(GROUP, head_cols, BF),
            shape_of(GROUP, head_cols, BF),
            shape_of(GROUP, head_cols, BF),
            shape_of(GROUP, head_cols, BF),
            shape_of(GROUP, head_cols, BF),
            shape_of(GROUP, head_cols, BF),
            shape_of(GROUP, LANES, F32),
            shape_of(GROUP, LANES, F32),
            shape_of(GROUP, LANES, F32),
        ],
        scratch_shapes=[pltpu.VMEM((GROUP, width), F32), pltpu.VMEM((GROUP, GROUP), F32)],
        compiler_params=params_for(VM[0]),
        cost_estimate=brief_cost(),
        name="attn_fwd",
    )(tokens, ident[0], ident[1], gain, *weights, forget_weight, forget_bias, w_out)


def mlp_both(group, tokens, own, other, cotangent, gain, w_gate, w_up, w_down):
    width = tokens.shape[1]
    hidden_units = w_down.shape[0]
    block = 512
    return pl.pallas_call(
        mlp_kernel,
        grid=(hidden_units // block,),
        in_specs=[
            rows_of(group, width),
            whole((GROUP, width)),
            whole((GROUP, width)),
            rows_of(group, width),
            whole((1, width)),
            cols_block(width, block),
            cols_block(width, block),
            rows_block(block, width),
        ],
        out_specs=[
            whole((GROUP, width)),
            whole((GROUP, width)),
            cols_block(GROUP, block),
            cols_block(GROUP, block),
            cols_block(GROUP, block),
            rows_of(0, width),
            whole((GROUP, width)),
        ],
        out_shape=[
            shape_of(GROUP, width, F32),
            shape_of(GROUP, width, BF),
            shape_of(GROUP, hidden_units, BF),
            shape_of(GROUP, hidden_units, BF),
            shape_of(GROUP, hidden_units, BF),
            shape_of(2 * GROUP, width, BF),
            shape_of(GROUP, width, BF),
        ],
        scratch_shapes=[pltpu.VMEM((GROUP, width), F32), pltpu.VMEM((GROUP, width), F32)],
        compiler_params=params_for(VM[1]),
        cost_estimate=brief_cost(),
        name="mlp_both",
    )(tokens, own, other, cotangent, gain, w_gate, w_up, w_down)


def attn_backward(
    group, tokens, cotangent, hidden, own, other, gain, ident, saved, w_out, weights, forget_weight,
    pair,
):
    width = tokens.shape[1]
    head_cols = w_out.shape[0]
    queries, keys_low, values_low, gate, attended, lse, decay, forget_pre = saved
    return pl.pallas_call(
        attn_bwd_kernel,
        grid=(head_cols // BLOCK_COLS,),
        in_specs=[
            rows_of(group, width),
            rows_of(group, width),
            whole((GROUP, width)),
            whole((GROUP, width)),
            whole((GROUP, width)),
            whole((1, width)),
            whole((1, GROUP)),
            whole((GROUP, 1)),
            cols_block(GROUP, BLOCK_COLS),
            cols_block(GROUP, BLOCK_COLS),
            cols_block(GROUP, BLOCK_COLS),
            cols_block(GROUP, BLOCK_COLS),
            cols_block(GROUP, BLOCK_COLS),
            whole((GROUP, LANES)),
            whole((GROUP, LANES)),
            whole((GROUP, LANES)),
            rows_block(BLOCK_COLS, width),
            cols_block(width, BLOCK_COLS),
            cols_block(width, BLOCK_COLS),
            cols_block(width, BLOCK_COLS),
            cols_block(width, BLOCK_COLS),
            whole((width, LANES)),
            pl.BlockSpec(memory_space=pl.ANY),
        ],
        out_specs=[
            whole((GROUP, width)),
            whole((8, width)),
            cols_block(GROUP, BLOCK_COLS),
            cols_block(GROUP, BLOCK_COLS),
            cols_block(GROUP, BLOCK_COLS),
            cols_block(GROUP, BLOCK_COLS),
            whole((GROUP, LANES)),
            whole((8, LANES)),
            rows_of(1, width),
        ],
        out_shape=[
            shape_of(GROUP, width, BF),
            shape_of(8, width, F32),
            shape_of(GROUP, head_cols, BF),
            shape_of(GROUP, head_cols, BF),
            shape_of(GROUP, head_cols, BF),
            shape_of(GROUP, head_cols, BF),
            shape_of(GROUP, LANES, BF),
            shape_of(8, LANES, F32),
            shape_of(2 * GROUP, width, BF),
        ],
        input_output_aliases={22: 8},
        scratch_shapes=[
            pltpu.VMEM((GROUP, width), F32),
            pltpu.VMEM((GROUP, GROUP), F32),
            pltpu.VMEM((GROUP, LANES), F32),
        ],
        compiler_params=params_for(VM[2]),
        cost_estimate=brief_cost(),
        name="attn_bwd",
    )(
        tokens,
        cotangent,
        hidden,
        own,
        other,
        gain,
        ident[0],
        ident[1],
        queries,
        keys_low,
        values_low,
        gate,
        attended,
        lse,
        decay,
        forget_pre,
        w_out,
        *weights,
        forget_weight,
        pair,
    )


def grad_kernel(place_ref, columns_ref, row_ref, *refs, groups, sets):
    total_ref = refs[-1]
    outputs = refs[-1 - 3 * len(sets) : -1]
    step = pl.program_id(0)
    blocks, block_rows = total_ref.shape[0], total_ref.shape[1]
    place = place_ref[0]

    def emit(left_refs, right_refs, extra_from, order, flip, keep_ref, low_ref, high_ref):
        total = dot_tn(left_refs[0][...], right_refs[0][...])
        for left_ref, right_ref in zip(left_refs[1:], right_refs[1:]):
            total = total + dot_tn(left_ref[...], right_ref[...])
        block = total.shape[1]
        if extra_from:
            lanes = lax.broadcasted_iota(jnp.int32, (8, block), 1)
            lines = lax.broadcasted_iota(jnp.int32, (8, block), 0)
            chosen = jnp.where(
                jnp.logical_and(lanes == lines + extra_from, lines < 2), 1.0, 0.0
            ).astype(BF)
            for part in split_three(columns_ref[...]):
                total = total + dot_tn(part.astype(BF), chosen)
            total = total + row_ref[0:1, :]
        for index in range(blocks):
            total_ref[index, :, :block] = total[index * block_rows : (index + 1) * block_rows]
        half = len(order) // 2
        for index, slot in enumerate(order):
            kept = total_ref[jnp.bitwise_xor(place, slot), :, :block]
            sent = total_ref[jnp.bitwise_xor(place, slot ^ flip), :, :block]
            keep_ref[index, :, :block] = kept.astype(BF)
            target = low_ref if index < half else high_ref
            target[index % half, :, :block] = sent.astype(BF)

    for number, (order, flip, plan) in enumerate(sets):
        for left_at, right_at, first, count, extra_from in plan:
            pl.when(jnp.logical_and(step >= first, step < first + count))(
                functools.partial(
                    emit,
                    refs[left_at : left_at + groups],
                    refs[right_at : right_at + groups],
                    extra_from,
                    order,
                    flip,
                    *outputs[3 * number : 3 * number + 3],
                )
            )


def half_order(bits):
    slots = [0]
    for bit in reversed(bits[1:]):
        slots = slots + [slot ^ bit for slot in slots]
    return slots


def weight_grad(sets, place, devices, block, extra=None):
    lefts = sets[0][0][0][0]
    width = lefts[0].shape[1]
    groups = len(lefts)
    rows = width // devices
    half = devices // 2
    arrays, specs, seen, layout, out_specs, out_shape = [], [], {}, [], [], []
    first = 0

    def span(start, count):
        return lambda step: (0, jnp.minimum(jnp.maximum(step - start, 0), count - 1))

    def add(items, spec):
        arrays.extend(items)
        specs.extend([spec] * groups)
        return len(arrays) - groups

    for number, (products, bits) in enumerate(sets):
        plan, start = [], first
        for index, (lefts, rights) in enumerate(products):
            if id(lefts[0]) not in seen:
                seen[id(lefts[0])] = add(lefts, rows_of(0, width))
            cols = rights[0].shape[1]
            narrow = cols < block
            count = max(cols // block, 1)
            at = add(rights, pl.BlockSpec((GROUP, min(cols, block)), span(first, count)))
            plan.append((seen[id(lefts[0])], at, first, count, extra[2] if narrow else 0))
            first += count
        layout.append((half_order(bits), bits[0], plan))
        place_of = span(start, first - start)
        for count in (half, half // 2, half // 2):
            out_specs.append(
                pl.BlockSpec(
                    (count, rows, block), lambda step, place_of=place_of: (0,) + place_of(step)
                )
            )
            out_shape.append(jax.ShapeDtypeStruct((count, rows, (first - start) * block), BF))
    columns, row = (jnp.zeros((8, LANES), F32),) * 2 if extra is None else extra[:2]
    outputs = pl.pallas_call(
        functools.partial(grad_kernel, groups=groups, sets=layout),
        grid=(first,),
        in_specs=[pl.BlockSpec(memory_space=pltpu.SMEM), whole(columns.shape), whole(row.shape)]
        + specs,
        out_specs=out_specs,
        out_shape=out_shape,
        scratch_shapes=[pltpu.VMEM((devices, rows, block), F32)],
        compiler_params=params_for(VM[3]),
        cost_estimate=brief_cost(),
        name="weight_grad",
    )(place, columns, row, *arrays)
    return [
        SharedSum(*outputs[3 * number : 3 * number + 3], bits, devices)
        for number, (_, bits) in enumerate(sets)
    ]


class SharedSum:
    def __init__(self, keep, low, high, bits, devices):
        self.parts, self.send = [keep], (low, high)
        self.bits, self.devices, self.stage = bits, devices, 0

    def exchange(self, *earlier):
        bit = self.bits[self.stage]
        pairs = [(index, index ^ bit) for index in range(self.devices)]
        got = jax.tree.map(lambda piece: lax.ppermute(piece, "dp", pairs), self.send)
        if earlier:
            got = after(got, *earlier)
        self.stage += 1
        if self.stage == len(self.bits):
            self.parts.append(got)
            return
        low, high = got if isinstance(got, tuple) else jnp.split(got, 2)
        half = low.shape[0]
        leaving = [part[half:] for part in self.parts] + [high]
        self.parts = [part[:half] for part in self.parts] + [low]
        self.send = functools.reduce(jnp.add, [part.astype(F32) for part in leaving]).astype(BF)

    def result(self):
        return functools.reduce(jnp.add, [part[0].astype(F32) for part in self.parts])


def finish_kernel(
    x_ref,
    hidden_ref,
    dattn_ref,
    mlp_ref,
    mlp_other_ref,
    dact_ref,
    dact_other_ref,
    gain_ref,
    *refs,
):
    result_ref, dtokens_ref = refs[-2:]
    mlp_sum = mlp_ref[...].astype(F32) + mlp_other_ref[...].astype(F32)
    result_ref[...] = (hidden_ref[...] + mlp_sum).astype(BF)
    x = x_ref[...].astype(F32)
    scale = lax.rsqrt(jnp.mean(x * x, axis=1, keepdims=True) + EPS)
    weighted = (dact_ref[...].astype(F32) + dact_other_ref[...].astype(F32)) * gain_ref[...]
    inner_mean = jnp.mean(weighted * x, axis=1, keepdims=True)
    d_norm = scale * weighted - x * (scale * scale * scale) * inner_mean
    dtokens_ref[...] = (dattn_ref[...].astype(F32) + d_norm).astype(BF)


def finish(group, tokens, hidden, d_hidden, own, other, gain, outputs):
    width = tokens.shape[1]
    block = 128
    count = GROUP // block

    def at(first):
        return pl.BlockSpec((block, width), lambda step: (first * count + step, 0))

    return pl.pallas_call(
        finish_kernel,
        grid=(count,),
        in_specs=[at(group), at(0), at(0), at(0), at(0), at(1), at(1), whole((1, width))]
        + [pl.BlockSpec(memory_space=pl.ANY)] * len(outputs),
        out_specs=[at(group)] * 2,
        out_shape=[shape_of(tokens.shape[0], width, BF)] * 2,
        input_output_aliases={8 + index: index for index in range(len(outputs))},
        compiler_params=params_for(16),
        cost_estimate=brief_cost(),
        name="finish",
    )(tokens, hidden, d_hidden, own, other, own, other, gain, *outputs)


def after(values, *earlier):
    return lax.optimization_barrier((values, earlier))[0]


def local(
    tokens,
    cotangent,
    segments,
    gain_attn,
    w_query,
    w_key,
    w_value,
    w_outgate,
    w_forget,
    b_forget,
    w_out,
    gain_mlp,
    w_gate,
    w_up,
    w_down,
):
    devices = lax.axis_size("dp")
    place_index = lax.axis_index("dp")
    width = tokens.shape[1]
    groups = tokens.shape[0] // GROUP
    heads = w_forget.shape[1]
    rows = width // devices
    butterfly = devices & (devices - 1) == 0 and rows % 16 == 0
    place = jnp.reshape(place_index, (1,)).astype(jnp.int32)
    bits = [1 << level for level in range(devices.bit_length() - 1)]

    def swap(values):
        return lax.ppermute(values, "tensor", [(0, 1), (1, 0)])

    gain_attn_row = gain_attn[None, :]
    gain_mlp_row = gain_mlp[None, :]
    forget_weight = jnp.pad(w_forget, ((0, 0), (0, LANES - heads)))
    forget_bias = jnp.pad(b_forget, (0, LANES - heads))[None, :]
    weights = (w_query, w_key, w_value, w_outgate)
    idents = []
    for group in range(groups):
        row = jnp.concatenate([jnp.full((PROMPT,), -1, jnp.int32), segments[group]])
        idents.append((row[None, :], row[:, None]))

    def pick(source, index):
        return [source[group][index] for group in range(groups)]

    def scattered(lefts, rights):
        total = functools.reduce(
            jnp.add, [dot_tn(left, right) for left, right in zip(lefts, rights)]
        )
        return lax.psum_scatter(total, "dp", scatter_dimension=0, tiled=True)

    def forward_of(group, rows_in):
        return attn_forward(
            group,
            rows_in,
            idents[group],
            gain_attn_row,
            weights,
            forget_weight,
            forget_bias,
            w_out,
        )

    def middle_of(group, own):
        return mlp_both(
            group,
            tokens,
            own,
            attn_other[group],
            cotangent,
            gain_mlp_row,
            w_gate,
            w_up,
            w_down,
        )

    def backward_of(group, own):
        (_, _, queries, keys_low, values_low, gate, attended, _, lse, decay, forget_pre) = forward[
            group
        ]
        return attn_backward(
            group,
            tokens,
            cotangent,
            middle[group][0],
            own,
            dact_other[group],
            gain_mlp_row,
            idents[group],
            (queries, keys_low, values_low, gate, attended, lse, decay, forget_pre),
            w_out,
            weights,
            forget_weight,
            middle[group][5],
        )

    done = []

    def ordered(values):
        return after(values, *done) if done else values

    def mark(*values):
        done[:] = values

    def step(*sums_at_work):
        for one in sums_at_work:
            one.exchange(*done)
            mark(one.send if one.stage < len(one.bits) else one.parts)

    def gradient(sets, block, extra=None):
        lefts = sets[0][0][0][0]
        held = ordered(lefts)
        sets = [
            ([(held if left is lefts else left, right) for left, right in products], bits)
            for products, bits in sets
        ]
        sums_made = weight_grad(sets, place, devices, block, extra)
        mark(*[one.send for one in sums_made])
        return sums_made

    forward = []
    for group in range(groups):
        forward.append(forward_of(group, ordered(tokens)))
        mark(forward[-1][0])
    attn_other = [swap(forward[group][0]) for group in range(groups)]
    middle = []
    for group in range(groups):
        middle.append(middle_of(group, ordered(forward[group][0])))
        mark(middle[-1][6])
    dact_other = [swap(middle[group][6]) for group in range(groups)]
    d_rows = [cotangent[group * GROUP : (group + 1) * GROUP] for group in range(groups)]
    acts_mlp = pick(middle, 1)
    acts_attn = pick(forward, 1)
    z_first = [bits[0]] + bits[2:] + bits[1:2]
    sums = {}
    backward, last_other, outputs = [], [], []

    def go_back(group):
        backward.append(backward_of(group, ordered(middle[group][6])))
        mark(backward[-1][8])

    def finish_group(group):
        outputs[:] = finish(
            group,
            tokens,
            middle[group][0],
            backward[group][0],
            backward[group][8],
            ordered(last_other[group]),
            gain_attn_row,
            outputs,
        )
        mark(*outputs)

    def send_last(group):
        last_other.append(swap(ordered(backward[group][8])))

    if butterfly:
        (sum_gate,) = gradient([([(acts_mlp, pick(middle, 3))], bits)], 512)
        dact_other[0] = ordered(dact_other[0])
        sum_gate.send = after(sum_gate.send, dact_other[0])
        (sum_up,) = gradient([([(acts_mlp, pick(middle, 4))], z_first)], 512)
        step(sum_gate)
        (sum_down,) = gradient([([(d_rows, pick(middle, 2))], bits)], 512)
        step(sum_up)
        go_back(0)
        for group in range(1, groups):
            dact_other[group] = ordered(dact_other[group])
        mark(dact_other[1:])
        step(sum_gate, sum_up, sum_down)
        send_last(0)
        for group in range(1, groups):
            go_back(group)
        step(sum_gate, sum_up, sum_down)
    else:
        sums["gate"] = scattered(acts_mlp, pick(middle, 3))
        sums["up"] = scattered(acts_mlp, pick(middle, 4))
        sums["down"] = scattered(d_rows, pick(middle, 2))
        for group in range(groups):
            go_back(group)
            send_last(group)
            finish_group(group)

    gains = functools.reduce(jnp.add, pick(backward, 1))
    g_bias = functools.reduce(jnp.add, pick(backward, 7))
    g_bias = jnp.pad(g_bias[:, :heads], ((0, 0), (heads + 2, LANES - 2 * heads - 2)))
    dattns = pick(backward, 0)
    gateds = pick(forward, 7)
    forget_grads = pick(backward, 6)
    if butterfly:
        head_cols = w_out.shape[0]
        (sum_first,) = gradient(
            [
                (
                    [
                        (acts_attn, pick(backward, 2)),
                        (acts_attn, pick(backward, 3)),
                        (dattns, gateds),
                    ],
                    bits,
                )
            ],
            384,
        )
        step(sum_gate, sum_up, sum_down)
        (sum_second,) = gradient(
            [
                (
                    [
                        (acts_attn, pick(backward, 4)),
                        (acts_attn, pick(backward, 5)),
                        (acts_attn, forget_grads),
                    ],
                    z_first,
                )
            ],
            256,
            (gains, g_bias, heads),
        )
        last_other[0] = ordered(last_other[0])
        mark(last_other[0])
        step(sum_first, sum_second)
        for group in range(1, groups):
            send_last(group)
        finish_group(0)
        sum_down.send = ordered(sum_down.send)
        step(sum_second, sum_down, sum_first)
        step(sum_first, sum_second)
        for group in range(1, groups):
            finish_group(group)
        step(sum_second)
        second_total = sum_second.result()
        small_sum = second_total[:, 2 * head_cols : 2 * head_cols + LANES]
        gain_attn_sum = small_sum[:, heads + 1] + swap(small_sum[:, heads + 1])
        mark(gain_attn_sum)
        step(sum_first)
        sums["gate"], sums["up"], sums["down"] = [
            one.result() for one in (sum_gate, sum_up, sum_down)
        ]
        total = sum_first.result()
        sums["query"], sums["key"], sums["out"] = [
            total[:, index * head_cols : (index + 1) * head_cols] for index in range(3)
        ]
        sums["value"], sums["outgate"] = [
            second_total[:, index * head_cols : (index + 1) * head_cols] for index in range(2)
        ]
    else:
        sums["out"] = scattered(dattns, gateds)
        for index, name in enumerate(("query", "key", "value", "outgate")):
            sums[name] = scattered(acts_attn, pick(backward, 2 + index))
        g_forget = functools.reduce(
            jnp.add, [dot_tn(left, right) for left, right in zip(acts_attn, forget_grads)]
        )
        columns = jnp.pad(gains[:2].T, ((0, 0), (heads, LANES - heads - 2)))
        small = g_forget + columns + g_bias[:1]
        small_sum = lax.psum_scatter(small, "dp", scatter_dimension=0, tiled=True)
        gain_attn_sum = small_sum[:, heads + 1] + swap(small_sum[:, heads + 1])
    return (
        outputs[0],
        outputs[1],
        gain_attn_sum,
        sums["query"],
        sums["key"],
        sums["value"],
        sums["outgate"],
        small_sum[:, :heads],
        small_sum[0, heads + 2 : 2 * heads + 2],
        sums["out"].T,
        small_sum[:, heads],
        sums["gate"],
        sums["up"],
        sums["down"].T,
    )


def solution(mesh):
    in_specs = (
        P("dp", None),
        P("dp", None),
        P("dp", None),
        P(),
        P(None, "tensor"),
        P(None, "tensor"),
        P(None, "tensor"),
        P(None, "tensor"),
        P(None, "tensor"),
        P("tensor"),
        P("tensor", None),
        P(),
        P(None, "tensor"),
        P(None, "tensor"),
        P("tensor", None),
    )
    out_specs = (
        P("dp", None),
        P("dp", None),
        P("dp"),
        P("dp", "tensor"),
        P("dp", "tensor"),
        P("dp", "tensor"),
        P("dp", "tensor"),
        P("dp", "tensor"),
        P("tensor"),
        P("tensor", "dp"),
        P("dp"),
        P("dp", "tensor"),
        P("dp", "tensor"),
        P("tensor", "dp"),
    )
    return jax.shard_map(local, mesh=mesh, in_specs=in_specs, out_specs=out_specs, check_vma=False)
```

```python
import functools

import jax
import jax.numpy as jnp
from jax import lax
from jax.experimental import pallas as pl
from jax.experimental.pallas import tpu as pltpu
from jax.sharding import PartitionSpec as P

PROMPT = 256
CONT_TOK = 256
GROUP = PROMPT + CONT_TOK
LANES = 128
HEAD = 64
BLOCK_HEADS = 4
BLOCK_COLS = HEAD * BLOCK_HEADS
EPS = 1e-06
NEG = -1e30
VM = (60, 40, 38, 26)
BF = jnp.bfloat16
F32 = jnp.float32


def dot_dims(first_arg, second_arg, first_dim, second_dim):
    return lax.dot_general(
        first_arg,
        second_arg,
        (((first_dim,), (second_dim,)), ((), ())),
        preferred_element_type=F32,
    )


def dot_nn(first_arg, second_arg):
    return dot_dims(first_arg, second_arg, 1, 0)


def dot_nt(first_arg, second_arg):
    return dot_dims(first_arg, second_arg, 1, 1)


def dot_tn(first_arg, second_arg):
    return dot_dims(first_arg, second_arg, 0, 0)


def sigmoid(values):
    return 1.0 / (1.0 + jnp.exp(-values))


def split_three(values):
    high = values.astype(BF).astype(F32)
    rest = values - high
    middle = rest.astype(BF).astype(F32)
    return high, middle, rest - middle


def visible_pairs(ident_row_ref, ident_col_ref):
    row_ids = lax.broadcasted_iota(jnp.int32, (GROUP, GROUP), 0)
    col_ids = lax.broadcasted_iota(jnp.int32, (GROUP, GROUP), 1)
    ident_row = ident_row_ref[...]
    same = jnp.logical_or(ident_row == -1, ident_row == ident_col_ref[...])
    return jnp.logical_and(col_ids <= row_ids, same)


def lane_ids():
    return lax.broadcasted_iota(jnp.int32, (GROUP, LANES), 1)


def place_extras(lanes, own, main, base, extras, constant_at):
    value = jnp.where(
        jnp.logical_and(lanes >= base + constant_at, lanes < base + constant_at + 3), 1.0, 0.0
    )
    offset = 0 if constant_at else 3
    for position, column in enumerate(extras):
        value = jnp.where(lanes == base + offset + position, column, value)
    return jnp.where(own, main, value).astype(BF)


def column_of(lanes, values, index):
    return jnp.sum(jnp.where(lanes == index, values, 0.0), axis=1, keepdims=True)


def attn_fwd_kernel(
    x_ref,
    ident_row_ref,
    ident_col_ref,
    gain_ref,
    wq_ref,
    wk_ref,
    wv_ref,
    wg_ref,
    wf_ref,
    bias_ref,
    wo_ref,
    part_ref,
    act_ref,
    q_ref,
    k_ref,
    v_ref,
    gpre_ref,
    att_ref,
    gated_ref,
    lse_ref,
    decay_ref,
    forget_ref,
    acc_ref,
    mask_ref,
):
    step = pl.program_id(0)
    lanes = lane_ids()

    @pl.when(step == 0)
    def _():
        x = x_ref[...].astype(F32)
        scale = lax.rsqrt(jnp.mean(x * x, axis=1, keepdims=True) + EPS)
        act = (x * scale * gain_ref[...]).astype(BF)
        act_ref[...] = act
        forget_pre = dot_nn(act, wf_ref[...]) + bias_ref[...]
        forget_ref[...] = forget_pre
        log_forget = jnp.minimum(forget_pre, 0.0) - jnp.log1p(jnp.exp(-jnp.abs(forget_pre)))
        allowed = visible_pairs(ident_row_ref, ident_col_ref)
        mask_ref[...] = jnp.where(allowed, 0.0, NEG)
        ancestry = jnp.where(allowed, 1.0, 0.0).astype(BF)
        high, middle, low = split_three(log_forget)
        decay_ref[...] = (
            dot_nn(ancestry, high.astype(BF))
            + dot_nn(ancestry, middle.astype(BF))
            + dot_nn(ancestry, low.astype(BF))
        )
        acc_ref[...] = jnp.zeros_like(acc_ref)
        lse_ref[...] = jnp.zeros_like(lse_ref)

    act = act_ref[...]
    queries = dot_nn(act, wq_ref[...]).astype(BF)
    keys_low = dot_nn(act, wk_ref[...]).astype(BF)
    values_low = dot_nn(act, wv_ref[...]).astype(BF)
    gate_pre = dot_nn(act, wg_ref[...])
    gate = sigmoid(gate_pre)
    q_ref[...] = queries
    k_ref[...] = keys_low
    v_ref[...] = values_low
    gpre_ref[...] = gate_pre.astype(BF)
    attended_pairs = []
    for pair in range(BLOCK_HEADS // 2):
        cols = slice(pair * LANES, (pair + 1) * LANES)
        q_pair = queries[:, cols].astype(F32) * (HEAD**-0.5)
        k_pair = keys_low[:, cols].astype(F32)
        v_pair = values_low[:, cols]
        outs = []
        for half in range(2):
            own = (lanes < HEAD) if half == 0 else (lanes >= HEAD)
            base = HEAD if half == 0 else 0
            head = step * BLOCK_HEADS + pair * 2 + half
            decay = column_of(lanes, decay_ref[...], head)
            parts = split_three(decay)
            q_ext = place_extras(lanes, own, q_pair, base, parts, 3)
            k_ext = place_extras(lanes, own, k_pair, base, [-value for value in parts], 0)
            scores_p = dot_nt(q_ext[:PROMPT], k_ext[:PROMPT]) + mask_ref[:PROMPT, :PROMPT]
            scores_a = dot_nt(q_ext[PROMPT:], k_ext[:PROMPT])
            scores_b = dot_nt(q_ext[PROMPT:], k_ext[PROMPT:]) + mask_ref[PROMPT:, PROMPT:]
            max_p = jnp.max(scores_p, axis=1, keepdims=True)
            exp_p = jnp.exp(scores_p - max_p)
            sum_p = jnp.sum(exp_p, axis=1, keepdims=True)
            out_p = dot_nn(exp_p.astype(BF), v_pair[:PROMPT]) * (1.0 / sum_p)
            max_c = jnp.maximum(
                jnp.max(scores_a, axis=1, keepdims=True), jnp.max(scores_b, axis=1, keepdims=True)
            )
            exp_a = jnp.exp(scores_a - max_c)
            exp_b = jnp.exp(scores_b - max_c)
            sum_c = jnp.sum(exp_a, axis=1, keepdims=True) + jnp.sum(exp_b, axis=1, keepdims=True)
            out_c = dot_nn(exp_a.astype(BF), v_pair[:PROMPT]) + dot_nn(
                exp_b.astype(BF), v_pair[PROMPT:]
            )
            out_c = out_c * (1.0 / sum_c)
            outs.append(jnp.concatenate([out_p, out_c], axis=0))
            lse = jnp.concatenate([max_p + jnp.log(sum_p), max_c + jnp.log(sum_c)], axis=0)
            lse_ref[...] = jnp.where(lanes == head, lse, lse_ref[...])
        attended_pairs.append(jnp.where(lanes < HEAD, outs[0], outs[1]))
    attended = jnp.concatenate(attended_pairs, axis=1)
    att_ref[...] = attended.astype(BF)
    gated = (attended * gate).astype(BF)
    gated_ref[...] = gated
    acc_ref[...] += dot_nn(gated, wo_ref[...])

    @pl.when(step == pl.num_programs(0) - 1)
    def _():
        part_ref[...] = acc_ref[...].astype(BF)


def mlp_kernel(
    x_ref,
    own_ref,
    other_ref,
    d_ref,
    gain_ref,
    wg_ref,
    wu_ref,
    wd_ref,
    hidden_ref,
    act_ref,
    inner_ref,
    dgate_ref,
    dup_ref,
    mlp_ref,
    dact_ref,
    acc_mlp_ref,
    acc_dact_ref,
):
    step = pl.program_id(0)

    @pl.when(step == 0)
    def _():
        hidden = x_ref[...].astype(F32) + (own_ref[...].astype(F32) + other_ref[...].astype(F32))
        hidden_ref[...] = hidden
        scale = lax.rsqrt(jnp.mean(hidden * hidden, axis=1, keepdims=True) + EPS)
        act_ref[...] = (hidden * scale * gain_ref[...]).astype(BF)
        acc_mlp_ref[...] = jnp.zeros_like(acc_mlp_ref)
        acc_dact_ref[...] = jnp.zeros_like(acc_dact_ref)

    act = act_ref[...]
    gate = dot_nn(act, wg_ref[...])
    up = dot_nn(act, wu_ref[...])
    d_inner = dot_nt(d_ref[...], wd_ref[...])
    gate_sigmoid = sigmoid(gate)
    silu_value = gate * gate_sigmoid
    inner = (silu_value * up).astype(BF)
    d_gate = (d_inner * up * gate_sigmoid * (1.0 + gate * (1.0 - gate_sigmoid))).astype(BF)
    d_up = (d_inner * silu_value).astype(BF)
    inner_ref[...] = inner
    dgate_ref[...] = d_gate
    dup_ref[...] = d_up
    acc_dact_ref[...] += dot_nt(d_gate, wg_ref[...]) + dot_nt(d_up, wu_ref[...])
    acc_mlp_ref[...] += dot_nn(inner, wd_ref[...])

    @pl.when(step == pl.num_programs(0) - 1)
    def _():
        dact_ref[...] = acc_dact_ref[...].astype(BF)
        mlp_ref[...] = acc_mlp_ref[...].astype(BF)


def attn_bwd_kernel(
    x_ref,
    d_ref,
    hidden_ref,
    own_ref,
    other_ref,
    gain_ref,
    ident_row_ref,
    ident_col_ref,
    q_ref,
    k_ref,
    v_ref,
    gpre_ref,
    att_ref,
    lse_ref,
    decay_ref,
    forget_ref,
    wo_ref,
    wq_ref,
    wk_ref,
    wv_ref,
    wg_ref,
    wf_ref,
    pair_ref,
    dattn_ref,
    gains_ref,
    dq_ref,
    dk_ref,
    dv_ref,
    dgp_ref,
    dfp_ref,
    gbias_ref,
    dact_ref,
    acc_ref,
    mask_ref,
    ddecay_ref,
):
    step = pl.program_id(0)
    lanes = lane_ids()

    @pl.when(step == 0)
    def _():
        hidden = hidden_ref[...].astype(F32)
        d_act = own_ref[...].astype(F32) + other_ref[...].astype(F32)
        scale = lax.rsqrt(jnp.mean(hidden * hidden, axis=1, keepdims=True) + EPS)
        weighted = d_act * gain_ref[...]
        inner_mean = jnp.mean(weighted * hidden, axis=1, keepdims=True)
        d_hidden = d_ref[...].astype(F32) + (
            scale * weighted - hidden * (scale * scale * scale) * inner_mean
        )
        dattn_ref[...] = d_hidden.astype(BF)
        gains_ref[...] = jnp.zeros_like(gains_ref)
        gains_ref[0:1, :] = jnp.sum(d_act * hidden * scale, axis=0, keepdims=True)
        allowed = visible_pairs(ident_row_ref, ident_col_ref)
        mask_ref[...] = jnp.where(allowed, 0.0, NEG)
        acc_ref[...] = jnp.zeros_like(acc_ref)
        ddecay_ref[...] = jnp.zeros_like(ddecay_ref)

    d_gated = dot_nt(dattn_ref[...], wo_ref[...])
    gate = sigmoid(gpre_ref[...].astype(F32))
    attended = att_ref[...].astype(F32)
    d_gate_pre = (d_gated * attended * gate * (1.0 - gate)).astype(BF)
    dgp_ref[...] = d_gate_pre
    d_attended = (d_gated * gate).astype(BF)
    grads_q, grads_k, grads_v = [], [], []
    for pair in range(BLOCK_HEADS // 2):
        cols = slice(pair * LANES, (pair + 1) * LANES)
        q_low = q_ref[:, cols]
        k_low = k_ref[:, cols]
        v_low = v_ref[:, cols]
        q_pair = q_low.astype(F32)
        k_pair = k_low.astype(F32)
        v_pair = v_low.astype(F32)
        do_low = d_attended[:, cols]
        do_pair = do_low.astype(F32)
        row_products = do_pair * attended[:, cols]
        dqs, dks, dvs = [], [], []
        for half in range(2):
            own = (lanes < HEAD) if half == 0 else (lanes >= HEAD)
            base = HEAD if half == 0 else 0
            head = step * BLOCK_HEADS + pair * 2 + half
            decay = column_of(lanes, decay_ref[...], head)
            lse = column_of(lanes, lse_ref[...], head)
            row_inner = jnp.sum(jnp.where(own, row_products, 0.0), axis=1, keepdims=True)
            q_ext = place_extras(
                lanes, own, q_pair * (HEAD**-0.5), base, split_three(decay - lse), 3
            )
            k_ext = place_extras(
                lanes, own, k_pair, base, [-value for value in split_three(decay)], 0
            )
            do_ext = place_extras(lanes, own, do_pair, base, split_three(-row_inner), 3)
            v_ext = place_extras(lanes, own, v_pair, base, [], 0)
            k_one = jnp.where(own, k_pair, 1.0).astype(BF)
            q_one = jnp.where(own, q_pair, 1.0).astype(BF)
            probs_p = jnp.exp(
                dot_nt(q_ext[:PROMPT], k_ext[:PROMPT]) + mask_ref[:PROMPT, :PROMPT]
            )
            probs_a = jnp.exp(dot_nt(q_ext[PROMPT:], k_ext[:PROMPT]))
            probs_b = jnp.exp(
                dot_nt(q_ext[PROMPT:], k_ext[PROMPT:]) + mask_ref[PROMPT:, PROMPT:]
            )
            ds_p = (probs_p * dot_nt(do_ext[:PROMPT], v_ext[:PROMPT])).astype(BF)
            ds_a = (probs_a * dot_nt(do_ext[PROMPT:], v_ext[:PROMPT])).astype(BF)
            ds_b = (probs_b * dot_nt(do_ext[PROMPT:], v_ext[PROMPT:])).astype(BF)
            dv_top = dot_tn(probs_p.astype(BF), do_low[:PROMPT]) + dot_tn(
                probs_a.astype(BF), do_low[PROMPT:]
            )
            dv_low = dot_tn(probs_b.astype(BF), do_low[PROMPT:])
            dk_top = dot_tn(ds_p, q_one[:PROMPT]) + dot_tn(ds_a, q_one[PROMPT:])
            dk_low = dot_tn(ds_b, q_one[PROMPT:])
            dq_top = dot_nn(ds_p, k_one[:PROMPT])
            dq_low = dot_nn(ds_a, k_one[:PROMPT]) + dot_nn(ds_b, k_one[PROMPT:])
            dvs.append(jnp.concatenate([dv_top, dv_low], axis=0))
            dks.append(jnp.concatenate([dk_top, dk_low], axis=0))
            dqs.append(jnp.concatenate([dq_top, dq_low], axis=0))
            sums = (dqs[-1] - dks[-1])[:, base : base + 1]
            ddecay_ref[...] = jnp.where(lanes == head, sums, ddecay_ref[...])
        grads_q.append(jnp.where(lanes < HEAD, dqs[0], dqs[1]) * (HEAD**-0.5))
        grads_k.append(jnp.where(lanes < HEAD, dks[0], dks[1]) * (HEAD**-0.5))
        grads_v.append(jnp.where(lanes < HEAD, dvs[0], dvs[1]))
    d_queries = jnp.concatenate(grads_q, axis=1).astype(BF)
    d_keys = jnp.concatenate(grads_k, axis=1).astype(BF)
    d_values = jnp.concatenate(grads_v, axis=1).astype(BF)
    dq_ref[...] = d_queries
    dk_ref[...] = d_keys
    dv_ref[...] = d_values
    acc_ref[...] += (
        dot_nt(d_queries, wq_ref[...])
        + dot_nt(d_keys, wk_ref[...])
        + dot_nt(d_values, wv_ref[...])
        + dot_nt(d_gate_pre, wg_ref[...])
    )

    @pl.when(step == pl.num_programs(0) - 1)
    def _():
        ancestry = jnp.where(visible_pairs(ident_row_ref, ident_col_ref), 1.0, 0.0).astype(BF)
        high, middle, low = split_three(ddecay_ref[...])
        d_log_forget = (
            dot_tn(ancestry, high.astype(BF))
            + dot_tn(ancestry, middle.astype(BF))
            + dot_tn(ancestry, low.astype(BF))
        )
        d_forget = (d_log_forget * sigmoid(-forget_ref[...])).astype(BF)
        dfp_ref[...] = d_forget
        gbias_ref[0:1, :] = jnp.sum(d_forget.astype(F32), axis=0, keepdims=True)
        d_act = (acc_ref[...] + dot_nt(d_forget, wf_ref[...])).astype(BF)
        dact_ref[...] = d_act
        x = x_ref[...].astype(F32)
        scale = lax.rsqrt(jnp.mean(x * x, axis=1, keepdims=True) + EPS)
        gains_ref[1:2, :] = jnp.sum(d_act.astype(F32) * x * scale, axis=0, keepdims=True)


def whole(shape):
    return pl.BlockSpec(shape, lambda step: (0,) * len(shape), pipeline_mode=pl.Buffered(1))


def rows_of(group, width):
    return pl.BlockSpec(
        (GROUP, width), lambda step: (group, 0), pipeline_mode=pl.Buffered(1)
    )


def cols_block(rows, width):
    return pl.BlockSpec((rows, width), lambda step: (0, step))


def rows_block(width, cols):
    return pl.BlockSpec((width, cols), lambda step: (step, 0))


def shape_of(rows, cols, dtype):
    return jax.ShapeDtypeStruct((rows, cols), dtype)


def brief_cost(flops=100_000_000):
    return pl.CostEstimate(flops=flops, bytes_accessed=100_000, transcendentals=0)


def params_for(mebibytes):
    return pltpu.CompilerParams(
        vmem_limit_bytes=mebibytes * 1024 * 1024, dimension_semantics=("arbitrary",)
    )


def attn_forward(group, tokens, ident, gain, weights, forget_weight, forget_bias, w_out):
    width = tokens.shape[1]
    head_cols = w_out.shape[0]
    return pl.pallas_call(
        attn_fwd_kernel,
        grid=(head_cols // BLOCK_COLS,),
        in_specs=[
            rows_of(group, width),
            whole((1, GROUP)),
            whole((GROUP, 1)),
            whole((1, width)),
            cols_block(width, BLOCK_COLS),
            cols_block(width, BLOCK_COLS),
            cols_block(width, BLOCK_COLS),
            cols_block(width, BLOCK_COLS),
            whole((width, LANES)),
            whole((1, LANES)),
            rows_block(BLOCK_COLS, width),
        ],
        out_specs=[
            whole((GROUP, width)),
            whole((GROUP, width)),
            cols_block(GROUP, BLOCK_COLS),
            cols_block(GROUP, BLOCK_COLS),
            cols_block(GROUP, BLOCK_COLS),
            cols_block(GROUP, BLOCK_COLS),
            cols_block(GROUP, BLOCK_COLS),
            cols_block(GROUP, BLOCK_COLS),
            whole((GROUP, LANES)),
            whole((GROUP, LANES)),
            whole((GROUP, LANES)),
        ],
        out_shape=[
            shape_of(GROUP, width, BF),
            shape_of(GROUP, width, BF),
            shape_of(GROUP, head_cols, BF),
            shape_of(GROUP, head_cols, BF),
            shape_of(GROUP, head_cols, BF),
            shape_of(GROUP, head_cols, BF),
            shape_of(GROUP, head_cols, BF),
            shape_of(GROUP, head_cols, BF),
            shape_of(GROUP, LANES, F32),
            shape_of(GROUP, LANES, F32),
            shape_of(GROUP, LANES, F32),
        ],
        scratch_shapes=[pltpu.VMEM((GROUP, width), F32), pltpu.VMEM((GROUP, GROUP), F32)],
        compiler_params=params_for(VM[0]),
        cost_estimate=brief_cost(),
        name="attn_fwd",
    )(tokens, ident[0], ident[1], gain, *weights, forget_weight, forget_bias, w_out)


def mlp_both(group, tokens, own, other, cotangent, gain, w_gate, w_up, w_down):
    width = tokens.shape[1]
    hidden_units = w_down.shape[0]
    block = 512
    return pl.pallas_call(
        mlp_kernel,
        grid=(hidden_units // block,),
        in_specs=[
            rows_of(group, width),
            whole((GROUP, width)),
            whole((GROUP, width)),
            rows_of(group, width),
            whole((1, width)),
            cols_block(width, block),
            cols_block(width, block),
            rows_block(block, width),
        ],
        out_specs=[
            whole((GROUP, width)),
            whole((GROUP, width)),
            cols_block(GROUP, block),
            cols_block(GROUP, block),
            cols_block(GROUP, block),
            rows_of(0, width),
            whole((GROUP, width)),
        ],
        out_shape=[
            shape_of(GROUP, width, F32),
            shape_of(GROUP, width, BF),
            shape_of(GROUP, hidden_units, BF),
            shape_of(GROUP, hidden_units, BF),
            shape_of(GROUP, hidden_units, BF),
            shape_of(2 * GROUP, width, BF),
            shape_of(GROUP, width, BF),
        ],
        scratch_shapes=[pltpu.VMEM((GROUP, width), F32), pltpu.VMEM((GROUP, width), F32)],
        compiler_params=params_for(VM[1]),
        cost_estimate=brief_cost(),
        name="mlp_both",
    )(tokens, own, other, cotangent, gain, w_gate, w_up, w_down)


def attn_backward(
    group, tokens, cotangent, hidden, own, other, gain, ident, saved, w_out, weights, forget_weight,
    pair,
):
    width = tokens.shape[1]
    head_cols = w_out.shape[0]
    queries, keys_low, values_low, gate, attended, lse, decay, forget_pre = saved
    return pl.pallas_call(
        attn_bwd_kernel,
        grid=(head_cols // BLOCK_COLS,),
        in_specs=[
            rows_of(group, width),
            rows_of(group, width),
            whole((GROUP, width)),
            whole((GROUP, width)),
            whole((GROUP, width)),
            whole((1, width)),
            whole((1, GROUP)),
            whole((GROUP, 1)),
            cols_block(GROUP, BLOCK_COLS),
            cols_block(GROUP, BLOCK_COLS),
            cols_block(GROUP, BLOCK_COLS),
            cols_block(GROUP, BLOCK_COLS),
            cols_block(GROUP, BLOCK_COLS),
            whole((GROUP, LANES)),
            whole((GROUP, LANES)),
            whole((GROUP, LANES)),
            rows_block(BLOCK_COLS, width),
            cols_block(width, BLOCK_COLS),
            cols_block(width, BLOCK_COLS),
            cols_block(width, BLOCK_COLS),
            cols_block(width, BLOCK_COLS),
            whole((width, LANES)),
            pl.BlockSpec(memory_space=pl.ANY),
        ],
        out_specs=[
            whole((GROUP, width)),
            whole((8, width)),
            cols_block(GROUP, BLOCK_COLS),
            cols_block(GROUP, BLOCK_COLS),
            cols_block(GROUP, BLOCK_COLS),
            cols_block(GROUP, BLOCK_COLS),
            whole((GROUP, LANES)),
            whole((8, LANES)),
            rows_of(1, width),
        ],
        out_shape=[
            shape_of(GROUP, width, BF),
            shape_of(8, width, F32),
            shape_of(GROUP, head_cols, BF),
            shape_of(GROUP, head_cols, BF),
            shape_of(GROUP, head_cols, BF),
            shape_of(GROUP, head_cols, BF),
            shape_of(GROUP, LANES, BF),
            shape_of(8, LANES, F32),
            shape_of(2 * GROUP, width, BF),
        ],
        input_output_aliases={22: 8},
        scratch_shapes=[
            pltpu.VMEM((GROUP, width), F32),
            pltpu.VMEM((GROUP, GROUP), F32),
            pltpu.VMEM((GROUP, LANES), F32),
        ],
        compiler_params=params_for(VM[2]),
        cost_estimate=brief_cost(),
        name="attn_bwd",
    )(
        tokens,
        cotangent,
        hidden,
        own,
        other,
        gain,
        ident[0],
        ident[1],
        queries,
        keys_low,
        values_low,
        gate,
        attended,
        lse,
        decay,
        forget_pre,
        w_out,
        *weights,
        forget_weight,
        pair,
    )


def grad_kernel(place_ref, columns_ref, row_ref, *refs, groups, sets):
    total_ref = refs[-1]
    outputs = refs[-1 - 3 * len(sets) : -1]
    step = pl.program_id(0)
    blocks, block_rows = total_ref.shape[0], total_ref.shape[1]
    place = place_ref[0]

    def emit(left_refs, right_refs, extra_from, order, flip, keep_ref, low_ref, high_ref):
        total = dot_tn(left_refs[0][...], right_refs[0][...])
        for left_ref, right_ref in zip(left_refs[1:], right_refs[1:]):
            total = total + dot_tn(left_ref[...], right_ref[...])
        block = total.shape[1]
        if extra_from:
            lanes = lax.broadcasted_iota(jnp.int32, (8, block), 1)
            lines = lax.broadcasted_iota(jnp.int32, (8, block), 0)
            chosen = jnp.where(
                jnp.logical_and(lanes == lines + extra_from, lines < 2), 1.0, 0.0
            ).astype(BF)
            for part in split_three(columns_ref[...]):
                total = total + dot_tn(part.astype(BF), chosen)
            total = total + row_ref[0:1, :]
        for index in range(blocks):
            total_ref[index, :, :block] = total[index * block_rows : (index + 1) * block_rows]
        half = len(order) // 2
        for index, slot in enumerate(order):
            kept = total_ref[jnp.bitwise_xor(place, slot), :, :block]
            sent = total_ref[jnp.bitwise_xor(place, slot ^ flip), :, :block]
            keep_ref[index, :, :block] = kept.astype(BF)
            target = low_ref if index < half else high_ref
            target[index % half, :, :block] = sent.astype(BF)

    for number, (order, flip, plan) in enumerate(sets):
        for left_at, right_at, first, count, extra_from in plan:
            pl.when(jnp.logical_and(step >= first, step < first + count))(
                functools.partial(
                    emit,
                    refs[left_at : left_at + groups],
                    refs[right_at : right_at + groups],
                    extra_from,
                    order,
                    flip,
                    *outputs[3 * number : 3 * number + 3],
                )
            )


def half_order(bits):
    slots = [0]
    for bit in reversed(bits[1:]):
        slots = slots + [slot ^ bit for slot in slots]
    return slots


def weight_grad(sets, place, devices, block, extra=None):
    lefts = sets[0][0][0][0]
    width = lefts[0].shape[1]
    groups = len(lefts)
    rows = width // devices
    half = devices // 2
    arrays, specs, seen, layout, out_specs, out_shape = [], [], {}, [], [], []
    first = 0

    def span(start, count):
        return lambda step: (0, jnp.minimum(jnp.maximum(step - start, 0), count - 1))

    def add(items, spec):
        arrays.extend(items)
        specs.extend([spec] * groups)
        return len(arrays) - groups

    for number, (products, bits) in enumerate(sets):
        plan, start = [], first
        for index, (lefts, rights) in enumerate(products):
            if id(lefts[0]) not in seen:
                seen[id(lefts[0])] = add(lefts, rows_of(0, width))
            cols = rights[0].shape[1]
            narrow = cols < block
            count = max(cols // block, 1)
            at = add(rights, pl.BlockSpec((GROUP, min(cols, block)), span(first, count)))
            plan.append((seen[id(lefts[0])], at, first, count, extra[2] if narrow else 0))
            first += count
        layout.append((half_order(bits), bits[0], plan))
        place_of = span(start, first - start)
        for count in (half, half // 2, half // 2):
            out_specs.append(
                pl.BlockSpec(
                    (count, rows, block), lambda step, place_of=place_of: (0,) + place_of(step)
                )
            )
            out_shape.append(jax.ShapeDtypeStruct((count, rows, (first - start) * block), BF))
    columns, row = (jnp.zeros((8, LANES), F32),) * 2 if extra is None else extra[:2]
    outputs = pl.pallas_call(
        functools.partial(grad_kernel, groups=groups, sets=layout),
        grid=(first,),
        in_specs=[pl.BlockSpec(memory_space=pltpu.SMEM), whole(columns.shape), whole(row.shape)]
        + specs,
        out_specs=out_specs,
        out_shape=out_shape,
        scratch_shapes=[pltpu.VMEM((devices, rows, block), F32)],
        compiler_params=params_for(VM[3]),
        cost_estimate=brief_cost(100_000_000 if extra is None else 10_000_000_000),
        name="weight_grad",
    )(place, columns, row, *arrays)
    return [
        SharedSum(*outputs[3 * number : 3 * number + 3], bits, devices)
        for number, (_, bits) in enumerate(sets)
    ]


class SharedSum:
    def __init__(self, keep, low, high, bits, devices):
        self.parts, self.send = [keep], (low, high)
        self.bits, self.devices, self.stage = bits, devices, 0

    def exchange(self, *earlier):
        bit = self.bits[self.stage]
        pairs = [(index, index ^ bit) for index in range(self.devices)]
        got = jax.tree.map(lambda piece: lax.ppermute(piece, "dp", pairs), self.send)
        if earlier:
            got = after(got, *earlier)
        self.stage += 1
        if self.stage == len(self.bits):
            self.parts.append(got)
            return
        low, high = got if isinstance(got, tuple) else jnp.split(got, 2)
        half = low.shape[0]
        leaving = [part[half:] for part in self.parts] + [high]
        self.parts = [part[:half] for part in self.parts] + [low]
        self.send = functools.reduce(jnp.add, [part.astype(F32) for part in leaving]).astype(BF)

    def result(self):
        return functools.reduce(jnp.add, [part[0].astype(F32) for part in self.parts])


def finish_kernel(
    x_ref,
    hidden_ref,
    dattn_ref,
    mlp_ref,
    mlp_other_ref,
    dact_ref,
    dact_other_ref,
    gain_ref,
    *refs,
):
    result_ref, dtokens_ref = refs[-2:]
    mlp_sum = mlp_ref[...].astype(F32) + mlp_other_ref[...].astype(F32)
    result_ref[...] = (hidden_ref[...] + mlp_sum).astype(BF)
    x = x_ref[...].astype(F32)
    scale = lax.rsqrt(jnp.mean(x * x, axis=1, keepdims=True) + EPS)
    weighted = (dact_ref[...].astype(F32) + dact_other_ref[...].astype(F32)) * gain_ref[...]
    inner_mean = jnp.mean(weighted * x, axis=1, keepdims=True)
    d_norm = scale * weighted - x * (scale * scale * scale) * inner_mean
    dtokens_ref[...] = (dattn_ref[...].astype(F32) + d_norm).astype(BF)


def finish(group, tokens, hidden, d_hidden, own, other, gain, outputs):
    width = tokens.shape[1]
    block = 128
    count = GROUP // block

    def at(first):
        return pl.BlockSpec((block, width), lambda step: (first * count + step, 0))

    return pl.pallas_call(
        finish_kernel,
        grid=(count,),
        in_specs=[at(group), at(0), at(0), at(0), at(0), at(1), at(1), whole((1, width))]
        + [pl.BlockSpec(memory_space=pl.ANY)] * len(outputs),
        out_specs=[at(group)] * 2,
        out_shape=[shape_of(tokens.shape[0], width, BF)] * 2,
        input_output_aliases={8 + index: index for index in range(len(outputs))},
        compiler_params=params_for(16),
        cost_estimate=brief_cost(),
        name="finish",
    )(tokens, hidden, d_hidden, own, other, own, other, gain, *outputs)


def after(values, *earlier):
    return lax.optimization_barrier((values, earlier))[0]


def local(
    tokens,
    cotangent,
    segments,
    gain_attn,
    w_query,
    w_key,
    w_value,
    w_outgate,
    w_forget,
    b_forget,
    w_out,
    gain_mlp,
    w_gate,
    w_up,
    w_down,
):
    devices = lax.axis_size("dp")
    place_index = lax.axis_index("dp")
    width = tokens.shape[1]
    groups = tokens.shape[0] // GROUP
    heads = w_forget.shape[1]
    rows = width // devices
    butterfly = devices & (devices - 1) == 0 and rows % 16 == 0
    place = jnp.reshape(place_index, (1,)).astype(jnp.int32)
    bits = [1 << level for level in range(devices.bit_length() - 1)]

    def swap(values):
        return lax.ppermute(values, "tensor", [(0, 1), (1, 0)])

    gain_attn_row = gain_attn[None, :]
    gain_mlp_row = gain_mlp[None, :]
    forget_weight = jnp.pad(w_forget, ((0, 0), (0, LANES - heads)))
    forget_bias = jnp.pad(b_forget, (0, LANES - heads))[None, :]
    weights = (w_query, w_key, w_value, w_outgate)
    idents = []
    for group in range(groups):
        row = jnp.concatenate([jnp.full((PROMPT,), -1, jnp.int32), segments[group]])
        idents.append((row[None, :], row[:, None]))

    def pick(source, index):
        return [source[group][index] for group in range(groups)]

    def scattered(lefts, rights):
        total = functools.reduce(
            jnp.add, [dot_tn(left, right) for left, right in zip(lefts, rights)]
        )
        return lax.psum_scatter(total, "dp", scatter_dimension=0, tiled=True)

    def forward_of(group, rows_in):
        return attn_forward(
            group,
            rows_in,
            idents[group],
            gain_attn_row,
            weights,
            forget_weight,
            forget_bias,
            w_out,
        )

    def middle_of(group, own):
        return mlp_both(
            group,
            tokens,
            own,
            attn_other[group],
            cotangent,
            gain_mlp_row,
            w_gate,
            w_up,
            w_down,
        )

    def backward_of(group, own):
        (_, _, queries, keys_low, values_low, gate, attended, _, lse, decay, forget_pre) = forward[
            group
        ]
        return attn_backward(
            group,
            tokens,
            cotangent,
            middle[group][0],
            own,
            dact_other[group],
            gain_mlp_row,
            idents[group],
            (queries, keys_low, values_low, gate, attended, lse, decay, forget_pre),
            w_out,
            weights,
            forget_weight,
            middle[group][5],
        )

    done = []

    def ordered(values):
        return after(values, *done) if done else values

    def mark(*values):
        done[:] = values

    def step(*sums_at_work):
        for one in sums_at_work:
            one.exchange(*done)
            mark(one.send if one.stage < len(one.bits) else one.parts)

    def gradient(sets, block, extra=None):
        lefts = sets[0][0][0][0]
        held = ordered(lefts)
        sets = [
            ([(held if left is lefts else left, right) for left, right in products], bits)
            for products, bits in sets
        ]
        sums_made = weight_grad(sets, place, devices, block, extra)
        mark(*[one.send for one in sums_made])
        return sums_made

    forward = []
    for group in range(groups):
        forward.append(forward_of(group, ordered(tokens)))
        mark(forward[-1][0])
    attn_other = [swap(forward[group][0]) for group in range(groups)]
    middle = []
    for group in range(groups):
        middle.append(middle_of(group, ordered(forward[group][0])))
        mark(middle[-1][6])
    dact_other = [swap(middle[group][6]) for group in range(groups)]
    d_rows = [cotangent[group * GROUP : (group + 1) * GROUP] for group in range(groups)]
    acts_mlp = pick(middle, 1)
    acts_attn = pick(forward, 1)
    z_first = [bits[0]] + bits[2:] + bits[1:2]
    sums = {}
    backward, last_other, outputs = [], [], []

    def go_back(group):
        backward.append(backward_of(group, ordered(middle[group][6])))
        mark(backward[-1][8])

    def finish_group(group):
        outputs[:] = finish(
            group,
            tokens,
            middle[group][0],
            backward[group][0],
            backward[group][8],
            ordered(last_other[group]),
            gain_attn_row,
            outputs,
        )
        mark(*outputs)

    def send_last(group):
        last_other.append(swap(ordered(backward[group][8])))

    if butterfly:
        (sum_gate,) = gradient([([(acts_mlp, pick(middle, 3))], bits)], 512)
        dact_other[0] = ordered(dact_other[0])
        sum_gate.send = after(sum_gate.send, dact_other[0])
        (sum_up,) = gradient([([(acts_mlp, pick(middle, 4))], z_first)], 512)
        step(sum_gate)
        (sum_down,) = gradient([([(d_rows, pick(middle, 2))], bits)], 512)
        step(sum_up)
        go_back(0)
        for group in range(1, groups):
            dact_other[group] = ordered(dact_other[group])
        mark(dact_other[1:])
        step(sum_gate, sum_up, sum_down)
        send_last(0)
        for group in range(1, groups):
            go_back(group)
        step(sum_gate, sum_up, sum_down)
    else:
        sums["gate"] = scattered(acts_mlp, pick(middle, 3))
        sums["up"] = scattered(acts_mlp, pick(middle, 4))
        sums["down"] = scattered(d_rows, pick(middle, 2))
        for group in range(groups):
            go_back(group)
            send_last(group)
            finish_group(group)

    gains = functools.reduce(jnp.add, pick(backward, 1))
    g_bias = functools.reduce(jnp.add, pick(backward, 7))
    g_bias = jnp.pad(g_bias[:, :heads], ((0, 0), (heads + 2, LANES - 2 * heads - 2)))
    dattns = pick(backward, 0)
    gateds = pick(forward, 7)
    forget_grads = pick(backward, 6)
    if butterfly:
        head_cols = w_out.shape[0]
        (sum_first,) = gradient(
            [
                (
                    [
                        (acts_attn, pick(backward, 2)),
                        (acts_attn, pick(backward, 3)),
                        (dattns, gateds),
                    ],
                    bits,
                )
            ],
            384,
        )
        step(sum_gate, sum_down)
        (sum_second,) = gradient(
            [
                (
                    [
                        (acts_attn, pick(backward, 4)),
                        (acts_attn, pick(backward, 5)),
                        (acts_attn, forget_grads),
                    ],
                    z_first,
                )
            ],
            256,
            (gains, g_bias, heads),
        )
        last_other[0] = ordered(last_other[0])
        mark(last_other[0])
        step(sum_first, sum_second)
        for group in range(1, groups):
            send_last(group)
        finish_group(0)
        sum_down.send = ordered(sum_down.send)
        step(sum_second, sum_down, sum_first, sum_up)
        step(sum_first, sum_second)
        for group in range(1, groups):
            finish_group(group)
        step(sum_second)
        second_total = sum_second.result()
        small_sum = second_total[:, 2 * head_cols : 2 * head_cols + LANES]
        gain_attn_sum = small_sum[:, heads + 1] + swap(small_sum[:, heads + 1])
        mark(gain_attn_sum)
        step(sum_first)
        sums["gate"], sums["up"], sums["down"] = [
            one.result() for one in (sum_gate, sum_up, sum_down)
        ]
        total = sum_first.result()
        sums["query"], sums["key"], sums["out"] = [
            total[:, index * head_cols : (index + 1) * head_cols] for index in range(3)
        ]
        sums["value"], sums["outgate"] = [
            second_total[:, index * head_cols : (index + 1) * head_cols] for index in range(2)
        ]
    else:
        sums["out"] = scattered(dattns, gateds)
        for index, name in enumerate(("query", "key", "value", "outgate")):
            sums[name] = scattered(acts_attn, pick(backward, 2 + index))
        g_forget = functools.reduce(
            jnp.add, [dot_tn(left, right) for left, right in zip(acts_attn, forget_grads)]
        )
        columns = jnp.pad(gains[:2].T, ((0, 0), (heads, LANES - heads - 2)))
        small = g_forget + columns + g_bias[:1]
        small_sum = lax.psum_scatter(small, "dp", scatter_dimension=0, tiled=True)
        gain_attn_sum = small_sum[:, heads + 1] + swap(small_sum[:, heads + 1])
    return (
        outputs[0],
        outputs[1],
        gain_attn_sum,
        sums["query"],
        sums["key"],
        sums["value"],
        sums["outgate"],
        small_sum[:, :heads],
        small_sum[0, heads + 2 : 2 * heads + 2],
        sums["out"].T,
        small_sum[:, heads],
        sums["gate"],
        sums["up"],
        sums["down"].T,
    )


def solution(mesh):
    in_specs = (
        P("dp", None),
        P("dp", None),
        P("dp", None),
        P(),
        P(None, "tensor"),
        P(None, "tensor"),
        P(None, "tensor"),
        P(None, "tensor"),
        P(None, "tensor"),
        P("tensor"),
        P("tensor", None),
        P(),
        P(None, "tensor"),
        P(None, "tensor"),
        P("tensor", None),
    )
    out_specs = (
        P("dp", None),
        P("dp", None),
        P("dp"),
        P("dp", "tensor"),
        P("dp", "tensor"),
        P("dp", "tensor"),
        P("dp", "tensor"),
        P("dp", "tensor"),
        P("tensor"),
        P("tensor", "dp"),
        P("dp"),
        P("dp", "tensor"),
        P("dp", "tensor"),
        P("tensor", "dp"),
    )
    return jax.shard_map(local, mesh=mesh, in_specs=in_specs, out_specs=out_specs, check_vma=False)
```

```python
import functools

import jax
import jax.numpy as jnp
from jax import lax
from jax.experimental import pallas as pl
from jax.experimental.pallas import tpu as pltpu
from jax.sharding import PartitionSpec as P

PROMPT = 256
CONT_TOK = 256
GROUP = PROMPT + CONT_TOK
LANES = 128
HEAD = 64
BLOCK_HEADS = 4
BLOCK_COLS = HEAD * BLOCK_HEADS
EPS = 1e-06
NEG = -1e30
VM = (60, 50, 38, 26)
BF = jnp.bfloat16
F32 = jnp.float32


def dot_dims(first_arg, second_arg, first_dim, second_dim):
    return lax.dot_general(
        first_arg,
        second_arg,
        (((first_dim,), (second_dim,)), ((), ())),
        preferred_element_type=F32,
    )


def dot_nn(first_arg, second_arg):
    return dot_dims(first_arg, second_arg, 1, 0)


def dot_nt(first_arg, second_arg):
    return dot_dims(first_arg, second_arg, 1, 1)


def dot_tn(first_arg, second_arg):
    return dot_dims(first_arg, second_arg, 0, 0)


def sigmoid(values):
    return 1.0 / (1.0 + jnp.exp(-values))


def split_three(values):
    high = values.astype(BF).astype(F32)
    rest = values - high
    middle = rest.astype(BF).astype(F32)
    return high, middle, rest - middle


def visible_pairs(ident_row_ref, ident_col_ref):
    row_ids = lax.broadcasted_iota(jnp.int32, (GROUP, GROUP), 0)
    col_ids = lax.broadcasted_iota(jnp.int32, (GROUP, GROUP), 1)
    ident_row = ident_row_ref[...]
    same = jnp.logical_or(ident_row == -1, ident_row == ident_col_ref[...])
    return jnp.logical_and(col_ids <= row_ids, same)


def lane_ids():
    return lax.broadcasted_iota(jnp.int32, (GROUP, LANES), 1)


def place_extras(lanes, own, main, base, extras, constant_at):
    value = jnp.where(
        jnp.logical_and(lanes >= base + constant_at, lanes < base + constant_at + 3), 1.0, 0.0
    )
    offset = 0 if constant_at else 3
    for position, column in enumerate(extras):
        value = jnp.where(lanes == base + offset + position, column, value)
    return jnp.where(own, main, value).astype(BF)


def column_of(lanes, values, index):
    return jnp.sum(jnp.where(lanes == index, values, 0.0), axis=1, keepdims=True)


def attn_fwd_kernel(
    x_ref,
    ident_row_ref,
    ident_col_ref,
    gain_ref,
    wq_ref,
    wk_ref,
    wv_ref,
    wg_ref,
    wf_ref,
    bias_ref,
    wo_ref,
    part_ref,
    act_ref,
    q_ref,
    k_ref,
    v_ref,
    gpre_ref,
    att_ref,
    gated_ref,
    lse_ref,
    decay_ref,
    forget_ref,
    acc_ref,
    mask_ref,
):
    step = pl.program_id(0)
    lanes = lane_ids()

    @pl.when(step == 0)
    def _():
        x = x_ref[...].astype(F32)
        scale = lax.rsqrt(jnp.mean(x * x, axis=1, keepdims=True) + EPS)
        act = (x * scale * gain_ref[...][None, :]).astype(BF)
        act_ref[...] = act
        forget_pre = dot_nn(act, wf_ref[...]) + bias_ref[...]
        forget_ref[...] = forget_pre
        log_forget = jnp.minimum(forget_pre, 0.0) - jnp.log1p(jnp.exp(-jnp.abs(forget_pre)))
        allowed = visible_pairs(ident_row_ref, ident_col_ref)
        mask_ref[...] = jnp.where(allowed, 0.0, NEG)
        ancestry = jnp.where(allowed, 1.0, 0.0).astype(BF)
        high, middle, low = split_three(log_forget)
        decay_ref[...] = (
            dot_nn(ancestry, high.astype(BF))
            + dot_nn(ancestry, middle.astype(BF))
            + dot_nn(ancestry, low.astype(BF))
        )
        acc_ref[...] = jnp.zeros_like(acc_ref)
        lse_ref[...] = jnp.zeros_like(lse_ref)

    act = act_ref[...]
    queries = dot_nn(act, wq_ref[...]).astype(BF)
    keys_low = dot_nn(act, wk_ref[...]).astype(BF)
    values_low = dot_nn(act, wv_ref[...]).astype(BF)
    gate_pre = dot_nn(act, wg_ref[...])
    gate = sigmoid(gate_pre)
    q_ref[...] = queries
    k_ref[...] = keys_low
    v_ref[...] = values_low
    gpre_ref[...] = gate_pre.astype(BF)
    attended_pairs = []
    for pair in range(BLOCK_HEADS // 2):
        cols = slice(pair * LANES, (pair + 1) * LANES)
        q_pair = queries[:, cols].astype(F32) * (HEAD**-0.5)
        k_pair = keys_low[:, cols].astype(F32)
        v_pair = values_low[:, cols]
        outs = []
        for half in range(2):
            own = (lanes < HEAD) if half == 0 else (lanes >= HEAD)
            base = HEAD if half == 0 else 0
            head = step * BLOCK_HEADS + pair * 2 + half
            decay = column_of(lanes, decay_ref[...], head)
            parts = split_three(decay)
            q_ext = place_extras(lanes, own, q_pair, base, parts, 3)
            k_ext = place_extras(lanes, own, k_pair, base, [-value for value in parts], 0)
            scores_p = dot_nt(q_ext[:PROMPT], k_ext[:PROMPT]) + mask_ref[:PROMPT, :PROMPT]
            scores_a = dot_nt(q_ext[PROMPT:], k_ext[:PROMPT])
            scores_b = dot_nt(q_ext[PROMPT:], k_ext[PROMPT:]) + mask_ref[PROMPT:, PROMPT:]
            max_p = jnp.max(scores_p, axis=1, keepdims=True)
            exp_p = jnp.exp(scores_p - max_p)
            sum_p = jnp.sum(exp_p, axis=1, keepdims=True)
            out_p = dot_nn(exp_p.astype(BF), v_pair[:PROMPT]) * (1.0 / sum_p)
            max_c = jnp.maximum(
                jnp.max(scores_a, axis=1, keepdims=True), jnp.max(scores_b, axis=1, keepdims=True)
            )
            exp_a = jnp.exp(scores_a - max_c)
            exp_b = jnp.exp(scores_b - max_c)
            sum_c = jnp.sum(exp_a, axis=1, keepdims=True) + jnp.sum(exp_b, axis=1, keepdims=True)
            out_c = dot_nn(exp_a.astype(BF), v_pair[:PROMPT]) + dot_nn(
                exp_b.astype(BF), v_pair[PROMPT:]
            )
            out_c = out_c * (1.0 / sum_c)
            outs.append(jnp.concatenate([out_p, out_c], axis=0))
            lse = jnp.concatenate([max_p + jnp.log(sum_p), max_c + jnp.log(sum_c)], axis=0)
            lse_ref[...] = jnp.where(lanes == head, lse, lse_ref[...])
        attended_pairs.append(jnp.where(lanes < HEAD, outs[0], outs[1]))
    attended = jnp.concatenate(attended_pairs, axis=1)
    att_ref[...] = attended.astype(BF)
    gated = (attended * gate).astype(BF)
    gated_ref[...] = gated
    acc_ref[...] += dot_nn(gated, wo_ref[...])

    @pl.when(step == pl.num_programs(0) - 1)
    def _():
        part_ref[...] = acc_ref[...].astype(BF)


def mlp_kernel(
    x_ref,
    own_ref,
    other_ref,
    d_ref,
    gain_ref,
    wg_ref,
    wu_ref,
    wd_ref,
    hidden_ref,
    act_ref,
    inner_ref,
    dgate_ref,
    dup_ref,
    mlp_ref,
    dact_ref,
    acc_mlp_ref,
    acc_dact_ref,
):
    step = pl.program_id(0)

    @pl.when(step == 0)
    def _():
        hidden = x_ref[...].astype(F32) + (own_ref[...].astype(F32) + other_ref[...].astype(F32))
        hidden_ref[...] = hidden
        scale = lax.rsqrt(jnp.mean(hidden * hidden, axis=1, keepdims=True) + EPS)
        act_ref[...] = (hidden * scale * gain_ref[...][None, :]).astype(BF)
        acc_mlp_ref[...] = jnp.zeros_like(acc_mlp_ref)
        acc_dact_ref[...] = jnp.zeros_like(acc_dact_ref)

    act = act_ref[...]
    gate = dot_nn(act, wg_ref[...])
    up = dot_nn(act, wu_ref[...])
    d_inner = dot_nt(d_ref[...], wd_ref[...])
    gate_sigmoid = sigmoid(gate)
    silu_value = gate * gate_sigmoid
    inner = (silu_value * up).astype(BF)
    d_gate = (d_inner * up * gate_sigmoid * (1.0 + gate * (1.0 - gate_sigmoid))).astype(BF)
    d_up = (d_inner * silu_value).astype(BF)
    inner_ref[...] = inner
    dgate_ref[...] = d_gate
    dup_ref[...] = d_up
    acc_dact_ref[...] += dot_nt(d_gate, wg_ref[...]) + dot_nt(d_up, wu_ref[...])
    acc_mlp_ref[...] += dot_nn(inner, wd_ref[...])

    @pl.when(step == pl.num_programs(0) - 1)
    def _():
        dact_ref[...] = acc_dact_ref[...].astype(BF)
        mlp_ref[...] = acc_mlp_ref[...].astype(BF)


def attn_bwd_kernel(
    x_ref,
    d_ref,
    hidden_ref,
    own_ref,
    other_ref,
    gain_ref,
    ident_row_ref,
    ident_col_ref,
    q_ref,
    k_ref,
    v_ref,
    gpre_ref,
    att_ref,
    lse_ref,
    decay_ref,
    forget_ref,
    wo_ref,
    wq_ref,
    wk_ref,
    wv_ref,
    wg_ref,
    wf_ref,
    pair_ref,
    dattn_ref,
    gains_ref,
    dq_ref,
    dk_ref,
    dv_ref,
    dgp_ref,
    dfp_ref,
    gbias_ref,
    dact_ref,
    acc_ref,
    mask_ref,
    ddecay_ref,
):
    step = pl.program_id(0)
    lanes = lane_ids()

    @pl.when(step == 0)
    def _():
        hidden = hidden_ref[...].astype(F32)
        d_act = own_ref[...].astype(F32) + other_ref[...].astype(F32)
        scale = lax.rsqrt(jnp.mean(hidden * hidden, axis=1, keepdims=True) + EPS)
        weighted = d_act * gain_ref[...][None, :]
        inner_mean = jnp.mean(weighted * hidden, axis=1, keepdims=True)
        d_hidden = d_ref[...].astype(F32) + (
            scale * weighted - hidden * (scale * scale * scale) * inner_mean
        )
        dattn_ref[...] = d_hidden.astype(BF)
        gains_ref[...] = jnp.zeros_like(gains_ref)
        gains_ref[0:1, :] = jnp.sum(d_act * hidden * scale, axis=0, keepdims=True)
        allowed = visible_pairs(ident_row_ref, ident_col_ref)
        mask_ref[...] = jnp.where(allowed, 0.0, NEG)
        acc_ref[...] = jnp.zeros_like(acc_ref)
        ddecay_ref[...] = jnp.zeros_like(ddecay_ref)

    d_gated = dot_nt(dattn_ref[...], wo_ref[...])
    gate = sigmoid(gpre_ref[...].astype(F32))
    attended = att_ref[...].astype(F32)
    d_gate_pre = (d_gated * attended * gate * (1.0 - gate)).astype(BF)
    dgp_ref[...] = d_gate_pre
    d_attended = (d_gated * gate).astype(BF)
    grads_q, grads_k, grads_v = [], [], []
    for pair in range(BLOCK_HEADS // 2):
        cols = slice(pair * LANES, (pair + 1) * LANES)
        q_low = q_ref[:, cols]
        k_low = k_ref[:, cols]
        v_low = v_ref[:, cols]
        q_pair = q_low.astype(F32)
        k_pair = k_low.astype(F32)
        v_pair = v_low.astype(F32)
        do_low = d_attended[:, cols]
        do_pair = do_low.astype(F32)
        row_products = do_pair * attended[:, cols]
        dqs, dks, dvs = [], [], []
        for half in range(2):
            own = (lanes < HEAD) if half == 0 else (lanes >= HEAD)
            base = HEAD if half == 0 else 0
            head = step * BLOCK_HEADS + pair * 2 + half
            decay = column_of(lanes, decay_ref[...], head)
            lse = column_of(lanes, lse_ref[...], head)
            row_inner = jnp.sum(jnp.where(own, row_products, 0.0), axis=1, keepdims=True)
            q_ext = place_extras(
                lanes, own, q_pair * (HEAD**-0.5), base, split_three(decay - lse), 3
            )
            k_ext = place_extras(
                lanes, own, k_pair, base, [-value for value in split_three(decay)], 0
            )
            do_ext = place_extras(lanes, own, do_pair, base, split_three(-row_inner), 3)
            v_ext = place_extras(lanes, own, v_pair, base, [], 0)
            k_one = jnp.where(own, k_pair, 1.0).astype(BF)
            q_one = jnp.where(own, q_pair, 1.0).astype(BF)
            probs_p = jnp.exp(
                dot_nt(q_ext[:PROMPT], k_ext[:PROMPT]) + mask_ref[:PROMPT, :PROMPT]
            )
            probs_a = jnp.exp(dot_nt(q_ext[PROMPT:], k_ext[:PROMPT]))
            probs_b = jnp.exp(
                dot_nt(q_ext[PROMPT:], k_ext[PROMPT:]) + mask_ref[PROMPT:, PROMPT:]
            )
            ds_p = (probs_p * dot_nt(do_ext[:PROMPT], v_ext[:PROMPT])).astype(BF)
            ds_a = (probs_a * dot_nt(do_ext[PROMPT:], v_ext[:PROMPT])).astype(BF)
            ds_b = (probs_b * dot_nt(do_ext[PROMPT:], v_ext[PROMPT:])).astype(BF)
            dv_top = dot_tn(probs_p.astype(BF), do_low[:PROMPT]) + dot_tn(
                probs_a.astype(BF), do_low[PROMPT:]
            )
            dv_low = dot_tn(probs_b.astype(BF), do_low[PROMPT:])
            dk_top = dot_tn(ds_p, q_one[:PROMPT]) + dot_tn(ds_a, q_one[PROMPT:])
            dk_low = dot_tn(ds_b, q_one[PROMPT:])
            dq_top = dot_nn(ds_p, k_one[:PROMPT])
            dq_low = dot_nn(ds_a, k_one[:PROMPT]) + dot_nn(ds_b, k_one[PROMPT:])
            dvs.append(jnp.concatenate([dv_top, dv_low], axis=0))
            dks.append(jnp.concatenate([dk_top, dk_low], axis=0))
            dqs.append(jnp.concatenate([dq_top, dq_low], axis=0))
            sums = (dqs[-1] - dks[-1])[:, base : base + 1]
            ddecay_ref[...] = jnp.where(lanes == head, sums, ddecay_ref[...])
        grads_q.append(jnp.where(lanes < HEAD, dqs[0], dqs[1]) * (HEAD**-0.5))
        grads_k.append(jnp.where(lanes < HEAD, dks[0], dks[1]) * (HEAD**-0.5))
        grads_v.append(jnp.where(lanes < HEAD, dvs[0], dvs[1]))
    d_queries = jnp.concatenate(grads_q, axis=1).astype(BF)
    d_keys = jnp.concatenate(grads_k, axis=1).astype(BF)
    d_values = jnp.concatenate(grads_v, axis=1).astype(BF)
    dq_ref[...] = d_queries
    dk_ref[...] = d_keys
    dv_ref[...] = d_values
    acc_ref[...] += (
        dot_nt(d_queries, wq_ref[...])
        + dot_nt(d_keys, wk_ref[...])
        + dot_nt(d_values, wv_ref[...])
        + dot_nt(d_gate_pre, wg_ref[...])
    )

    @pl.when(step == pl.num_programs(0) - 1)
    def _():
        ancestry = jnp.where(visible_pairs(ident_row_ref, ident_col_ref), 1.0, 0.0).astype(BF)
        high, middle, low = split_three(ddecay_ref[...])
        d_log_forget = (
            dot_tn(ancestry, high.astype(BF))
            + dot_tn(ancestry, middle.astype(BF))
            + dot_tn(ancestry, low.astype(BF))
        )
        d_forget = (d_log_forget * sigmoid(-forget_ref[...])).astype(BF)
        dfp_ref[...] = d_forget
        gbias_ref[0:1, :] = jnp.sum(d_forget.astype(F32), axis=0, keepdims=True)
        d_act = (acc_ref[...] + dot_nt(d_forget, wf_ref[...])).astype(BF)
        dact_ref[...] = d_act
        x = x_ref[...].astype(F32)
        scale = lax.rsqrt(jnp.mean(x * x, axis=1, keepdims=True) + EPS)
        gains_ref[1:2, :] = jnp.sum(d_act.astype(F32) * x * scale, axis=0, keepdims=True)


def whole(shape):
    return pl.BlockSpec(shape, lambda step: (0,) * len(shape), pipeline_mode=pl.Buffered(1))


def rows_of(group, width):
    return pl.BlockSpec(
        (GROUP, width), lambda step: (group, 0), pipeline_mode=pl.Buffered(1)
    )


def cols_block(rows, width):
    return pl.BlockSpec((rows, width), lambda step: (0, step))


def rows_block(width, cols):
    return pl.BlockSpec((width, cols), lambda step: (step, 0))


def shape_of(rows, cols, dtype):
    return jax.ShapeDtypeStruct((rows, cols), dtype)


def brief_cost(flops=100_000_000):
    return pl.CostEstimate(flops=flops, bytes_accessed=100_000, transcendentals=0)


def params_for(mebibytes):
    return pltpu.CompilerParams(
        vmem_limit_bytes=mebibytes * 1024 * 1024, dimension_semantics=("arbitrary",)
    )


def attn_forward(group, tokens, ident, gain, weights, forget_weight, forget_bias, w_out):
    width = tokens.shape[1]
    head_cols = w_out.shape[0]
    return pl.pallas_call(
        attn_fwd_kernel,
        grid=(head_cols // BLOCK_COLS,),
        in_specs=[
            rows_of(group, width),
            whole((1, GROUP)),
            whole((GROUP, 1)),
            whole((width,)),
            cols_block(width, BLOCK_COLS),
            cols_block(width, BLOCK_COLS),
            cols_block(width, BLOCK_COLS),
            cols_block(width, BLOCK_COLS),
            whole((width, LANES)),
            whole((1, LANES)),
            rows_block(BLOCK_COLS, width),
        ],
        out_specs=[
            whole((GROUP, width)),
            whole((GROUP, width)),
            cols_block(GROUP, BLOCK_COLS),
            cols_block(GROUP, BLOCK_COLS),
            cols_block(GROUP, BLOCK_COLS),
            cols_block(GROUP, BLOCK_COLS),
            cols_block(GROUP, BLOCK_COLS),
            cols_block(GROUP, BLOCK_COLS),
            whole((GROUP, LANES)),
            whole((GROUP, LANES)),
            whole((GROUP, LANES)),
        ],
        out_shape=[
            shape_of(GROUP, width, BF),
            shape_of(GROUP, width, BF),
            shape_of(GROUP, head_cols, BF),
            shape_of(GROUP, head_cols, BF),
            shape_of(GROUP, head_cols, BF),
            shape_of(GROUP, head_cols, BF),
            shape_of(GROUP, head_cols, BF),
            shape_of(GROUP, head_cols, BF),
            shape_of(GROUP, LANES, F32),
            shape_of(GROUP, LANES, F32),
            shape_of(GROUP, LANES, F32),
        ],
        scratch_shapes=[pltpu.VMEM((GROUP, width), F32), pltpu.VMEM((GROUP, GROUP), F32)],
        compiler_params=params_for(VM[0]),
        cost_estimate=brief_cost(),
        name="attn_fwd",
    )(tokens, ident[0], ident[1], gain, *weights, forget_weight, forget_bias, w_out)


def mlp_both(group, tokens, own, other, cotangent, gain, w_gate, w_up, w_down):
    width = tokens.shape[1]
    hidden_units = w_down.shape[0]
    block = 512
    return pl.pallas_call(
        mlp_kernel,
        grid=(hidden_units // block,),
        in_specs=[
            rows_of(group, width),
            whole((GROUP, width)),
            whole((GROUP, width)),
            rows_of(group, width),
            whole((width,)),
            cols_block(width, block),
            cols_block(width, block),
            rows_block(block, width),
        ],
        out_specs=[
            whole((GROUP, width)),
            whole((GROUP, width)),
            cols_block(GROUP, block),
            cols_block(GROUP, block),
            cols_block(GROUP, block),
            rows_of(0, width),
            whole((GROUP, width)),
        ],
        out_shape=[
            shape_of(GROUP, width, F32),
            shape_of(GROUP, width, BF),
            shape_of(GROUP, hidden_units, BF),
            shape_of(GROUP, hidden_units, BF),
            shape_of(GROUP, hidden_units, BF),
            shape_of(2 * GROUP, width, BF),
            shape_of(GROUP, width, BF),
        ],
        scratch_shapes=[pltpu.VMEM((GROUP, width), F32), pltpu.VMEM((GROUP, width), F32)],
        compiler_params=params_for(VM[1]),
        cost_estimate=brief_cost(),
        name="mlp_both",
    )(tokens, own, other, cotangent, gain, w_gate, w_up, w_down)


def attn_backward(
    group, tokens, cotangent, hidden, own, other, gain, ident, saved, w_out, weights, forget_weight,
    pair,
):
    width = tokens.shape[1]
    head_cols = w_out.shape[0]
    queries, keys_low, values_low, gate, attended, lse, decay, forget_pre = saved
    return pl.pallas_call(
        attn_bwd_kernel,
        grid=(head_cols // BLOCK_COLS,),
        in_specs=[
            rows_of(group, width),
            rows_of(group, width),
            whole((GROUP, width)),
            whole((GROUP, width)),
            whole((GROUP, width)),
            whole((width,)),
            whole((1, GROUP)),
            whole((GROUP, 1)),
            cols_block(GROUP, BLOCK_COLS),
            cols_block(GROUP, BLOCK_COLS),
            cols_block(GROUP, BLOCK_COLS),
            cols_block(GROUP, BLOCK_COLS),
            cols_block(GROUP, BLOCK_COLS),
            whole((GROUP, LANES)),
            whole((GROUP, LANES)),
            whole((GROUP, LANES)),
            rows_block(BLOCK_COLS, width),
            cols_block(width, BLOCK_COLS),
            cols_block(width, BLOCK_COLS),
            cols_block(width, BLOCK_COLS),
            cols_block(width, BLOCK_COLS),
            whole((width, LANES)),
            pl.BlockSpec(memory_space=pl.ANY),
        ],
        out_specs=[
            whole((GROUP, width)),
            whole((8, width)),
            cols_block(GROUP, BLOCK_COLS),
            cols_block(GROUP, BLOCK_COLS),
            cols_block(GROUP, BLOCK_COLS),
            cols_block(GROUP, BLOCK_COLS),
            whole((GROUP, LANES)),
            whole((8, LANES)),
            rows_of(1, width),
        ],
        out_shape=[
            shape_of(GROUP, width, BF),
            shape_of(8, width, F32),
            shape_of(GROUP, head_cols, BF),
            shape_of(GROUP, head_cols, BF),
            shape_of(GROUP, head_cols, BF),
            shape_of(GROUP, head_cols, BF),
            shape_of(GROUP, LANES, BF),
            shape_of(8, LANES, F32),
            shape_of(2 * GROUP, width, BF),
        ],
        input_output_aliases={22: 8},
        scratch_shapes=[
            pltpu.VMEM((GROUP, width), F32),
            pltpu.VMEM((GROUP, GROUP), F32),
            pltpu.VMEM((GROUP, LANES), F32),
        ],
        compiler_params=params_for(VM[2]),
        cost_estimate=brief_cost(),
        name="attn_bwd",
    )(
        tokens,
        cotangent,
        hidden,
        own,
        other,
        gain,
        ident[0],
        ident[1],
        queries,
        keys_low,
        values_low,
        gate,
        attended,
        lse,
        decay,
        forget_pre,
        w_out,
        *weights,
        forget_weight,
        pair,
    )


def grad_kernel(place_ref, columns_ref, row_ref, *refs, groups, sets):
    total_ref = refs[-1]
    outputs = refs[-1 - 3 * len(sets) : -1]
    step = pl.program_id(0)
    blocks, block_rows = total_ref.shape[0], total_ref.shape[1]
    place = place_ref[0]

    def emit(left_refs, right_refs, extra_from, order, flip, keep_ref, low_ref, high_ref):
        total = dot_tn(left_refs[0][...], right_refs[0][...])
        for left_ref, right_ref in zip(left_refs[1:], right_refs[1:]):
            total = total + dot_tn(left_ref[...], right_ref[...])
        block = total.shape[1]
        if extra_from:
            lanes = lax.broadcasted_iota(jnp.int32, (8, block), 1)
            lines = lax.broadcasted_iota(jnp.int32, (8, block), 0)
            chosen = jnp.where(
                jnp.logical_and(lanes == lines + extra_from, lines < 2), 1.0, 0.0
            ).astype(BF)
            for part in split_three(columns_ref[...]):
                total = total + dot_tn(part.astype(BF), chosen)
            total = total + row_ref[0:1, :]
        for index in range(blocks):
            total_ref[index, :, :block] = total[index * block_rows : (index + 1) * block_rows]
        half = len(order) // 2
        for index, slot in enumerate(order):
            kept = total_ref[jnp.bitwise_xor(place, slot), :, :block]
            sent = total_ref[jnp.bitwise_xor(place, slot ^ flip), :, :block]
            keep_ref[index, :, :block] = kept.astype(BF)
            target = low_ref if index < half else high_ref
            target[index % half, :, :block] = sent.astype(BF)

    for number, (order, flip, plan) in enumerate(sets):
        for left_at, right_at, first, count, extra_from in plan:
            pl.when(jnp.logical_and(step >= first, step < first + count))(
                functools.partial(
                    emit,
                    refs[left_at : left_at + groups],
                    refs[right_at : right_at + groups],
                    extra_from,
                    order,
                    flip,
                    *outputs[3 * number : 3 * number + 3],
                )
            )


def half_order(bits):
    slots = [0]
    for bit in reversed(bits[1:]):
        slots = slots + [slot ^ bit for slot in slots]
    return slots


def weight_grad(sets, place, devices, block, extra=None):
    lefts = sets[0][0][0][0]
    width = lefts[0].shape[1]
    groups = len(lefts)
    rows = width // devices
    half = devices // 2
    arrays, specs, seen, layout, out_specs, out_shape = [], [], {}, [], [], []
    first = 0

    def span(start, count):
        return lambda step: (0, jnp.minimum(jnp.maximum(step - start, 0), count - 1))

    def add(items, spec):
        arrays.extend(items)
        specs.extend([spec] * groups)
        return len(arrays) - groups

    for number, (products, bits) in enumerate(sets):
        plan, start = [], first
        for index, (lefts, rights) in enumerate(products):
            if id(lefts[0]) not in seen:
                seen[id(lefts[0])] = add(lefts, rows_of(0, width))
            cols = rights[0].shape[1]
            narrow = cols < block
            count = max(cols // block, 1)
            at = add(rights, pl.BlockSpec((GROUP, min(cols, block)), span(first, count)))
            plan.append((seen[id(lefts[0])], at, first, count, extra[2] if narrow else 0))
            first += count
        layout.append((half_order(bits), bits[0], plan))
        place_of = span(start, first - start)
        for count in (half, half // 2, half // 2):
            out_specs.append(
                pl.BlockSpec(
                    (count, rows, block), lambda step, place_of=place_of: (0,) + place_of(step)
                )
            )
            out_shape.append(jax.ShapeDtypeStruct((count, rows, (first - start) * block), BF))
    columns, row = (jnp.zeros((8, LANES), F32),) * 2 if extra is None else extra[:2]
    outputs = pl.pallas_call(
        functools.partial(grad_kernel, groups=groups, sets=layout),
        grid=(first,),
        in_specs=[pl.BlockSpec(memory_space=pltpu.SMEM), whole(columns.shape), whole(row.shape)]
        + specs,
        out_specs=out_specs,
        out_shape=out_shape,
        scratch_shapes=[pltpu.VMEM((devices, rows, block), F32)],
        compiler_params=params_for(VM[3]),
        cost_estimate=brief_cost(100_000_000 if extra is None else 10_000_000_000),
        name="weight_grad",
    )(place, columns, row, *arrays)
    return [
        SharedSum(*outputs[3 * number : 3 * number + 3], bits, devices)
        for number, (_, bits) in enumerate(sets)
    ]


class SharedSum:
    def __init__(self, keep, low, high, bits, devices):
        self.parts, self.send = [keep], (low, high)
        self.bits, self.devices, self.stage = bits, devices, 0

    def exchange(self, *earlier):
        bit = self.bits[self.stage]
        pairs = [(index, index ^ bit) for index in range(self.devices)]
        got = jax.tree.map(lambda piece: lax.ppermute(piece, "dp", pairs), self.send)
        if earlier:
            got = after(got, *earlier)
        self.stage += 1
        if self.stage == len(self.bits):
            self.parts.append(got)
            return
        low, high = got if isinstance(got, tuple) else jnp.split(got, 2)
        half = low.shape[0]
        leaving = [part[half:] for part in self.parts] + [high]
        self.parts = [part[:half] for part in self.parts] + [low]
        self.send = functools.reduce(jnp.add, [part.astype(F32) for part in leaving]).astype(BF)

    def result(self):
        return functools.reduce(jnp.add, [part[0].astype(F32) for part in self.parts])


def finish_kernel(
    x_ref,
    hidden_ref,
    dattn_ref,
    mlp_ref,
    mlp_other_ref,
    dact_ref,
    dact_other_ref,
    gain_ref,
    *refs,
):
    result_ref, dtokens_ref = refs[-2:]
    mlp_sum = mlp_ref[...].astype(F32) + mlp_other_ref[...].astype(F32)
    result_ref[...] = (hidden_ref[...] + mlp_sum).astype(BF)
    x = x_ref[...].astype(F32)
    scale = lax.rsqrt(jnp.mean(x * x, axis=1, keepdims=True) + EPS)
    weighted = (dact_ref[...].astype(F32) + dact_other_ref[...].astype(F32)) * gain_ref[...][None, :]
    inner_mean = jnp.mean(weighted * x, axis=1, keepdims=True)
    d_norm = scale * weighted - x * (scale * scale * scale) * inner_mean
    dtokens_ref[...] = (dattn_ref[...].astype(F32) + d_norm).astype(BF)


def finish(group, tokens, hidden, d_hidden, own, other, gain, outputs):
    width = tokens.shape[1]
    block = 128
    count = GROUP // block

    def at(first):
        return pl.BlockSpec((block, width), lambda step: (first * count + step, 0))

    return pl.pallas_call(
        finish_kernel,
        grid=(count,),
        in_specs=[at(group), at(0), at(0), at(0), at(0), at(1), at(1), whole((width,))]
        + [pl.BlockSpec(memory_space=pl.ANY)] * len(outputs),
        out_specs=[at(group)] * 2,
        out_shape=[shape_of(tokens.shape[0], width, BF)] * 2,
        input_output_aliases={8 + index: index for index in range(len(outputs))},
        compiler_params=params_for(16),
        cost_estimate=brief_cost(),
        name="finish",
    )(tokens, hidden, d_hidden, own, other, own, other, gain, *outputs)


def after(values, *earlier):
    return lax.optimization_barrier((values, earlier))[0]


def local(
    tokens,
    cotangent,
    segments,
    gain_attn,
    w_query,
    w_key,
    w_value,
    w_outgate,
    w_forget,
    b_forget,
    w_out,
    gain_mlp,
    w_gate,
    w_up,
    w_down,
):
    devices = lax.axis_size("dp")
    place_index = lax.axis_index("dp")
    width = tokens.shape[1]
    groups = tokens.shape[0] // GROUP
    heads = w_forget.shape[1]
    rows = width // devices
    butterfly = devices & (devices - 1) == 0 and rows % 16 == 0
    place = jnp.reshape(place_index, (1,)).astype(jnp.int32)
    bits = [1 << level for level in range(devices.bit_length() - 1)]

    def swap(values):
        return lax.ppermute(values, "tensor", [(0, 1), (1, 0)])

    gain_attn_row, gain_mlp_row = gain_attn, gain_mlp
    forget_weight = jnp.pad(w_forget, ((0, 0), (0, LANES - heads)))
    forget_bias = jnp.pad(b_forget, (0, LANES - heads))[None, :]
    weights = (w_query, w_key, w_value, w_outgate)
    idents = []
    for group in range(groups):
        row = jnp.concatenate([jnp.full((PROMPT,), -1, jnp.int32), segments[group]])
        idents.append((row[None, :], row[:, None]))

    def pick(source, index):
        return [source[group][index] for group in range(groups)]

    def scattered(lefts, rights):
        total = functools.reduce(
            jnp.add, [dot_tn(left, right) for left, right in zip(lefts, rights)]
        )
        return lax.psum_scatter(total, "dp", scatter_dimension=0, tiled=True)

    def forward_of(group, rows_in):
        return attn_forward(
            group,
            rows_in,
            idents[group],
            gain_attn_row,
            weights,
            forget_weight,
            forget_bias,
            w_out,
        )

    def middle_of(group, own):
        return mlp_both(
            group,
            tokens,
            own,
            attn_other[group],
            cotangent,
            gain_mlp_row,
            w_gate,
            w_up,
            w_down,
        )

    def backward_of(group, own):
        (_, _, queries, keys_low, values_low, gate, attended, _, lse, decay, forget_pre) = forward[
            group
        ]
        return attn_backward(
            group,
            tokens,
            cotangent,
            middle[group][0],
            own,
            dact_other[group],
            gain_mlp_row,
            idents[group],
            (queries, keys_low, values_low, gate, attended, lse, decay, forget_pre),
            w_out,
            weights,
            forget_weight,
            middle[group][5],
        )

    done = []

    def ordered(values):
        return after(values, *done) if done else values

    def mark(*values):
        done[:] = values

    def step(*sums_at_work):
        for one in sums_at_work:
            one.exchange(*done)
            mark(one.send if one.stage < len(one.bits) else one.parts)

    def gradient(sets, block, extra=None):
        lefts = sets[0][0][0][0]
        held = ordered(lefts)
        sets = [
            ([(held if left is lefts else left, right) for left, right in products], bits)
            for products, bits in sets
        ]
        sums_made = weight_grad(sets, place, devices, block, extra)
        mark(*[one.send for one in sums_made])
        return sums_made

    forward = []
    for group in range(groups):
        forward.append(forward_of(group, ordered(tokens)))
        mark(forward[-1][0])
    attn_other = [swap(forward[group][0]) for group in range(groups)]
    middle = []
    for group in range(groups):
        middle.append(middle_of(group, ordered(forward[group][0])))
        mark(middle[-1][6])
    dact_other = [swap(middle[group][6]) for group in range(groups)]
    d_rows = [cotangent[group * GROUP : (group + 1) * GROUP] for group in range(groups)]
    acts_mlp = pick(middle, 1)
    acts_attn = pick(forward, 1)
    z_first = [bits[0]] + bits[2:] + bits[1:2]
    sums = {}
    backward, last_other, outputs = [], [], []

    def go_back(group):
        backward.append(backward_of(group, ordered(middle[group][6])))
        mark(backward[-1][8])

    def finish_group(group):
        outputs[:] = finish(
            group,
            tokens,
            middle[group][0],
            backward[group][0],
            backward[group][8],
            ordered(last_other[group]),
            gain_attn_row,
            outputs,
        )
        mark(*outputs)

    def send_last(group):
        last_other.append(swap(ordered(backward[group][8])))

    if butterfly:
        (sum_gate,) = gradient([([(acts_mlp, pick(middle, 3))], bits)], 512)
        dact_other[0] = ordered(dact_other[0])
        sum_gate.send = after(sum_gate.send, dact_other[0])
        (sum_up,) = gradient([([(acts_mlp, pick(middle, 4))], z_first)], 512)
        step(sum_gate)
        (sum_down,) = gradient([([(d_rows, pick(middle, 2))], bits)], 512)
        step(sum_up)
        go_back(0)
        for group in range(1, groups):
            dact_other[group] = ordered(dact_other[group])
        mark(dact_other[1:])
        step(sum_gate, sum_up, sum_down)
        send_last(0)
        for group in range(1, groups):
            go_back(group)
        step(sum_gate, sum_up, sum_down)
    else:
        sums["gate"] = scattered(acts_mlp, pick(middle, 3))
        sums["up"] = scattered(acts_mlp, pick(middle, 4))
        sums["down"] = scattered(d_rows, pick(middle, 2))
        for group in range(groups):
            go_back(group)
            send_last(group)
            finish_group(group)

    gains = functools.reduce(jnp.add, pick(backward, 1))
    g_bias = functools.reduce(jnp.add, pick(backward, 7))
    g_bias = jnp.pad(g_bias[:, :heads], ((0, 0), (heads + 2, LANES - 2 * heads - 2)))
    dattns = pick(backward, 0)
    gateds = pick(forward, 7)
    forget_grads = pick(backward, 6)
    if butterfly:
        head_cols = w_out.shape[0]
        (sum_first,) = gradient(
            [
                (
                    [
                        (acts_attn, pick(backward, 2)),
                        (acts_attn, pick(backward, 3)),
                        (dattns, gateds),
                    ],
                    bits,
                )
            ],
            384,
        )
        step(sum_gate, sum_down)
        (sum_second,) = gradient(
            [
                (
                    [
                        (acts_attn, pick(backward, 4)),
                        (acts_attn, pick(backward, 5)),
                        (acts_attn, forget_grads),
                    ],
                    z_first,
                )
            ],
            256,
            (gains, g_bias, heads),
        )
        last_other[0] = ordered(last_other[0])
        mark(last_other[0])
        step(sum_first, sum_second)
        for group in range(1, groups):
            send_last(group)
        finish_group(0)
        sum_down.send = ordered(sum_down.send)
        step(sum_second, sum_down, sum_first, sum_up)
        step(sum_first, sum_second)
        for group in range(1, groups):
            finish_group(group)
        step(sum_second)
        second_total = sum_second.result()
        small_sum = second_total[:, 2 * head_cols : 2 * head_cols + LANES]
        gain_attn_sum = small_sum[:, heads + 1] + swap(small_sum[:, heads + 1])
        mark(gain_attn_sum)
        step(sum_first)
        sums["gate"], sums["up"], sums["down"] = [
            one.result() for one in (sum_gate, sum_up, sum_down)
        ]
        total = sum_first.result()
        sums["query"], sums["key"], sums["out"] = [
            total[:, index * head_cols : (index + 1) * head_cols] for index in range(3)
        ]
        sums["value"], sums["outgate"] = [
            second_total[:, index * head_cols : (index + 1) * head_cols] for index in range(2)
        ]
    else:
        sums["out"] = scattered(dattns, gateds)
        for index, name in enumerate(("query", "key", "value", "outgate")):
            sums[name] = scattered(acts_attn, pick(backward, 2 + index))
        g_forget = functools.reduce(
            jnp.add, [dot_tn(left, right) for left, right in zip(acts_attn, forget_grads)]
        )
        columns = jnp.pad(gains[:2].T, ((0, 0), (heads, LANES - heads - 2)))
        small = g_forget + columns + g_bias[:1]
        small_sum = lax.psum_scatter(small, "dp", scatter_dimension=0, tiled=True)
        gain_attn_sum = small_sum[:, heads + 1] + swap(small_sum[:, heads + 1])
    return (
        outputs[0],
        outputs[1],
        gain_attn_sum,
        sums["query"],
        sums["key"],
        sums["value"],
        sums["outgate"],
        small_sum[:, :heads],
        small_sum[0, heads + 2 : 2 * heads + 2],
        sums["out"].T,
        small_sum[:, heads],
        sums["gate"],
        sums["up"],
        sums["down"].T,
    )


def solution(mesh):
    in_specs = (
        P("dp", None),
        P("dp", None),
        P("dp", None),
        P(),
        P(None, "tensor"),
        P(None, "tensor"),
        P(None, "tensor"),
        P(None, "tensor"),
        P(None, "tensor"),
        P("tensor"),
        P("tensor", None),
        P(),
        P(None, "tensor"),
        P(None, "tensor"),
        P("tensor", None),
    )
    out_specs = (
        P("dp", None),
        P("dp", None),
        P("dp"),
        P("dp", "tensor"),
        P("dp", "tensor"),
        P("dp", "tensor"),
        P("dp", "tensor"),
        P("dp", "tensor"),
        P("tensor"),
        P("tensor", "dp"),
        P("dp"),
        P("dp", "tensor"),
        P("dp", "tensor"),
        P("tensor", "dp"),
    )
    return jax.shard_map(local, mesh=mesh, in_specs=in_specs, out_specs=out_specs, check_vma=False)
```
